32 devices in a mesh: dp: 16 (over z, y, core), mp: 2 (over x).
Axes of the slice: x: 2, y: 2, z: 4, core: 2. Of those that a mesh axis runs over, the one named last changes fastest.
Arguments:
- tokens: bfloat16 [2, 9856, 1024], P(None, ('dp', 'mp')), may hold values from -6 to 6
- segments: int32 [2, 9856], P(None, 'dp'), may hold values from 0 to 7, as said below
- qkv_weight: bfloat16 [2, 3, 1024, 1024], P(None, None, 'dp', 'mp'), may hold values from -0.1875 to 0.1875
- out_weight: bfloat16 [2, 1024, 1024], P(None, 'mp', 'dp'), may hold values from -0.75 to 0.75
- up_weight: bfloat16 [2, 1024, 4096], P(None, 'dp', 'mp'), may hold values from -0.1875 to 0.1875
- down_weight: bfloat16 [2, 4096, 1024], P(None, 'mp', 'dp'), may hold values from -0.125 to 0.125
- vectors: bfloat16 [2, 8, 1024], P(None, None, 'dp'), may hold values from -1.2 to 1.6, as said below
- qv_bias: bfloat16 [2, 2, 16, 64], P(None, None, 'mp', 'dp'), may hold values from -3 to 3
- up_bias: bfloat16 [2, 64, 64], P(None, 'mp', 'dp'), may hold values from -3 to 3
- cotangent: bfloat16 [2, 9856, 1024], P(None, ('dp', 'mp')), may hold values from -6 to 6
Outputs:
- output: bfloat16 [2, 9856, 1024], P(None, ('dp', 'mp'))
- tokens_grad: float32 [2, 9856, 1024], P(None, ('dp', 'mp'))
- qkv_grad: float32 [2, 3, 1024, 1024], P(None, None, 'dp', 'mp')
- out_grad: float32 [2, 1024, 1024], P(None, 'mp', 'dp')
- up_grad: float32 [2, 1024, 4096], P(None, 'dp', 'mp')
- down_grad: float32 [2, 4096, 1024], P(None, 'mp', 'dp')
- vectors_grad: float32 [2, 8, 1024], P(None, None, 'dp')
- qv_bias_grad: float32 [2, 2, 16, 64], P(None, None, 'mp', 'dp')
- up_bias_grad: float32 [2, 64, 64], P(None, 'mp', 'dp')
The draws below stay inside these ranges and needn't reach their ends.
Inputs may be any that keep to these rules, and one draw needn't show every extreme that they name: `segments`: each block of 616 consecutive rows of a micro-batch holds 2 crops of 197 tokens and 6 crops of 37 tokens in a drawn order, numbered 0 upward in order of position. `vectors`: rows 0 and 4 lie in 0.4 to 1.6, rows 3 and 7 in 0.4 to 1.2.
All inputs are finite; a program needn't handle non-finite values.
Results may differ from the reference program's by a relative error of at most 0.019.
Values may be sent and summed in bfloat16 or wider, within the bound.
A program may use at most 320 MiB of HBM per device.

```python
import math
import jax
import jax.numpy as jnp
from jax import lax

D = 1024
HEADS = 16
HD = 64
FF = 4096
LAYERS = 2
GLEN = 197
LLEN = 37
GLOBALS = 2
MICRO = 2
CROPS = 8
ROWS = 616
BLOCKS = 32
N_DP = 16


def draw_segments(key, part):
    block_keys = jax.random.split(key, BLOCKS)
    orders = jax.vmap(lambda single: jax.random.permutation(single, CROPS))(block_keys)
    lengths = jnp.where(orders < GLOBALS, GLEN, LLEN).astype(jnp.int32)
    ends = jnp.cumsum(lengths, axis=1)
    places = jnp.arange(ROWS, dtype=jnp.int32)
    numbers = jnp.sum((ends[:, None, :] <= places[None, :, None]).astype(jnp.int32), axis=2)
    return numbers.reshape(MICRO, ROWS * N_DP)


def draw_vectors(key, part):
    shape = (LAYERS, 8, D)
    first_key = jax.random.fold_in(key, 11)
    second_key = jax.random.fold_in(key, 12)
    third_key = jax.random.fold_in(key, 13)
    gains = jnp.clip(1.0 + 0.2 * jax.random.normal(first_key, shape, jnp.float32), 0.41, 1.59)
    shifts = jnp.clip(0.3 * jax.random.normal(second_key, shape, jnp.float32), -1.19, 1.19)
    scales = jax.random.uniform(third_key, shape, jnp.float32, 0.41, 1.19)
    place = jnp.arange(8)[None, :, None]
    is_gain = (place == 0) | (place == 4)
    is_scale = (place == 3) | (place == 7)
    return jnp.where(is_gain, gains, jnp.where(is_scale, scales, shifts)).astype(jnp.bfloat16)


def block_levels(own_key, extent, cuts, low, high):
    def one(dim, blocks):
        heights = jax.random.uniform(jax.random.fold_in(jax.random.fold_in(own_key, 6), dim), (blocks,), jnp.float32, low / len(cuts), high / len(cuts))
        return jnp.repeat(jnp.exp(heights), extent[dim] // blocks).reshape((-1,) + (1,) * (len(extent) - dim - 1))

    loudness = one(*cuts[0])
    for cut in cuts[1:]:
        loudness = loudness * one(*cut)
    return loudness


def gaussian(rng, shape, scale, bound, shards=(), kind=jnp.bfloat16):
    values = jax.random.normal(rng, shape, jnp.float32) * scale
    if len(shards) > 0:
        values = block_levels(rng, shape, shards, -0.22, 0.18) * values
    return jnp.clip(values, min=-bound, max=bound).astype(kind)


def setup_inputs(seed: int = 0) -> dict:
    arg_keys = jax.random.split(jax.random.key(seed), 11)
    tokens = gaussian(arg_keys[0], (MICRO, ROWS * N_DP, D), 1.0, 6.0, ((1, 32),))
    segments = draw_segments(jax.random.fold_in(arg_keys[10], 71), 0)
    qkv_weight = gaussian(arg_keys[2], (LAYERS, 3, D, D), D ** -0.5, 0.1875, ((2, 16), (3, 2)))
    out_weight = gaussian(arg_keys[3], (LAYERS, D, D), (D // 16) ** -0.5, 0.75, ((1, 2), (2, 16)))
    up_weight = gaussian(arg_keys[4], (LAYERS, D, FF), D ** -0.5, 0.1875, ((1, 16), (2, 2)))
    down_weight = gaussian(arg_keys[5], (LAYERS, FF, D), (FF // 2) ** -0.5, 0.125, ((1, 2), (2, 16)))
    vectors = draw_vectors(jax.random.fold_in(arg_keys[10], 71), 0)
    qv_bias = gaussian(arg_keys[7], (LAYERS, 2, HEADS, HD), 0.5, 3.0, ((2, 2), (3, 16)))
    up_bias = gaussian(arg_keys[8], (LAYERS, FF // HD, HD), 0.5, 3.0, ((1, 2), (2, 16)))
    cotangent = gaussian(arg_keys[9], (MICRO, ROWS * N_DP, D), 1.0, 6.0, ((1, 32),))
    return {"tokens": tokens, "segments": segments, "qkv_weight": qkv_weight, "out_weight": out_weight, "up_weight": up_weight, "down_weight": down_weight, "vectors": vectors, "qv_bias": qv_bias, "up_bias": up_bias, "cotangent": cotangent}


@jax.custom_vjp
def low(v):
    return lax.optimization_barrier(v.astype(jnp.bfloat16)).astype(jnp.float32)

@jax.custom_vjp
def low_back(v):
    return v

def low_keep(v):
    return (low(v), None)

def low_pass(kept, grad):
    return (grad,)

def back_keep(v):
    return (v, None)

def back_low(kept, grad):
    return (low(grad),)
low.defvjp(low_keep, low_pass)
low_back.defvjp(back_keep, back_low)

def layer_norm(values, gain, shift):
    centred = values - lax.optimization_barrier(jnp.mean(values, axis=-1, keepdims=True))
    inverse = lax.rsqrt(lax.optimization_barrier(jnp.mean(centred * centred, axis=-1, keepdims=True)) + 1e-06)
    return centred * inverse * gain + shift

def one_layer(resid, same_crop, qkv_w, out_w, up_w, down_w, vector_rows, qv_shift, up_shift):
    count = resid.shape[0]
    heads = qv_shift.shape[1]
    scale = 1.0 / math.sqrt(qv_shift.shape[2])
    highest = lax.Precision.HIGHEST
    first = low(layer_norm(resid, vector_rows[0], vector_rows[1]))
    qv_flat = qv_shift.reshape(2, -1)
    query = low(low_back(jnp.dot(first, qkv_w[0], precision=highest) + qv_flat[0]))
    keys = low(low_back(jnp.dot(first, qkv_w[1], precision=highest)))
    values = low(low_back(jnp.dot(first, qkv_w[2], precision=highest) + qv_flat[1]))
    query_heads = query.reshape(count, heads, -1)
    key_heads = keys.reshape(count, heads, -1)
    value_heads = values.reshape(count, heads, -1)
    scores = low_back(jnp.einsum('qhd,khd->hqk', query_heads, key_heads, precision=highest) * scale)
    scores = jnp.where(same_crop, scores, -1000000000.0)
    peak = lax.optimization_barrier(jnp.max(scores, axis=-1, keepdims=True))
    powers = jnp.exp(scores - peak)
    probs = low(powers / lax.optimization_barrier(jnp.sum(powers, axis=-1, keepdims=True)))
    attended = jnp.einsum('hqk,khd->qhd', probs, value_heads, precision=highest).reshape(count, -1)
    attended = low(low_back(attended))
    projected = low_back(jnp.dot(attended, out_w, precision=highest))
    middle = resid + vector_rows[3] * (projected + vector_rows[2])
    second = low(layer_norm(middle, vector_rows[4], vector_rows[5]))
    hidden_pre = low_back(jnp.dot(second, up_w, precision=highest) + up_shift.reshape(-1))
    hidden = low(0.5 * hidden_pre * (1.0 + lax.erf(hidden_pre * 0.7071067811865476)))
    returned = low_back(jnp.dot(hidden, down_w, precision=highest))
    return middle + vector_rows[7] * (returned + vector_rows[6])

def forward(resid_all, ids_all, params):
    qkv_w, out_w, up_w, down_w, vector_all, qv_all, up_all = params

    def block(resid, ids):
        same_crop = (ids[:, None] == ids[None, :])[None]
        for layer in range(LAYERS):
            resid = one_layer(resid, same_crop, qkv_w[layer], out_w[layer], up_w[layer], down_w[layer], vector_all[layer], qv_all[layer], up_all[layer])
        return resid
    checked = jax.checkpoint(block)

    def step(carry, inputs):
        return (carry, checked(inputs[0], inputs[1]))
    _, outs = lax.scan(step, None, (resid_all, ids_all))
    return outs

def reference(tokens, segments, qkv_weight, out_weight, up_weight, down_weight, vectors, qv_bias, up_bias, cotangent):
    blocks = MICRO * N_DP
    resid_all = tokens.astype(jnp.float32).reshape(blocks, ROWS, D)
    ids_all = segments.reshape(blocks, ROWS)
    upstream = cotangent.astype(jnp.float32).reshape(blocks, ROWS, D)
    params = (qkv_weight.astype(jnp.float32), out_weight.astype(jnp.float32), up_weight.astype(jnp.float32), down_weight.astype(jnp.float32), vectors.astype(jnp.float32), qv_bias.astype(jnp.float32), up_bias.astype(jnp.float32))
    outs, pullback = jax.vjp(lambda resid, weights: forward(resid, ids_all, weights), resid_all, params)
    tokens_grad, grads = pullback(upstream)
    shape = (MICRO, ROWS * N_DP, D)
    return (outs.reshape(shape).astype(jnp.bfloat16), tokens_grad.reshape(shape), grads[0], grads[1], grads[2], grads[3], grads[4], grads[5], grads[6])
```

```python
import functools
import math

import jax
import jax.numpy as jnp
from jax import lax
from jax.experimental import pallas as pl
from jax.experimental.pallas import tpu as pltpu
from jax.sharding import PartitionSpec as P

INV_ROOT_TWO = 0.7071067811865476
INV_ROOT_TAU = 0.3989422804014327


def layer_norm(values, gain, shift):
    centred = values - jnp.mean(values, axis=-1, keepdims=True)
    inverse = lax.rsqrt(jnp.mean(centred * centred, axis=-1, keepdims=True) + 1e-06)
    normed = centred * inverse
    return (normed * gain + shift, normed, inverse)


def norm_backward(upstream, normed, inverse, gain):
    scaled = upstream * gain
    inner = (
        scaled
        - jnp.mean(scaled, axis=-1, keepdims=True)
        - normed * jnp.mean(scaled * normed, axis=-1, keepdims=True)
    )
    return (inverse * inner, jnp.sum(upstream * normed, axis=0), jnp.sum(upstream, axis=0))


def contract_rows(left, right):
    return lax.dot_general(
        left, right, (((0,), (0,)), ((), ())), preferred_element_type=jnp.float32
    )


def against_rows(left, right):
    return lax.dot_general(
        left, right, (((1,), (1,)), ((), ())), preferred_element_type=jnp.float32
    )


def gather_normed(values):
    return lax.all_gather(values, "mp", axis=0, tiled=True)


def gather_upstream(values):
    return lax.all_gather(values, "mp", axis=0, tiled=True)


def branch_sum(term, count):
    return lax.psum_scatter(
        term(jnp.int32(0), count * lax.axis_size("mp")).astype(jnp.bfloat16),
        "mp",
        scatter_dimension=0,
        tiled=True,
    ).astype(jnp.float32)


def input_sum(term, count):
    return lax.psum_scatter(
        term(jnp.int32(0), count * lax.axis_size("mp")).astype(jnp.bfloat16),
        "mp",
        scatter_dimension=0,
        tiled=True,
    ).astype(jnp.float32)


def on_device(
    tokens,
    segments,
    qkv_weight,
    out_weight,
    up_weight,
    down_weight,
    vectors,
    qv_bias,
    up_bias,
    cotangent,
):
    layers = qkv_weight.shape[0]
    micro = tokens.shape[0]
    width = tokens.shape[2]
    head_dim = qv_bias.shape[3] * lax.axis_size("dp")
    scale = 1.0 / math.sqrt(head_dim)

    def attention_scores(query, keys, same_crop, heads):
        total_rows = query.shape[0]
        raw = (
            jnp.einsum(
                "qhd,khd->hqk",
                query.reshape(total_rows, heads, -1),
                keys.reshape(total_rows, heads, -1),
                preferred_element_type=jnp.float32,
            )
            * scale
        )
        return jnp.where(same_crop, raw, -1000000000.0)

    def forward_layer(resid, same_crop, whole):
        qkv_full, out_full, up_full, down_full, vector_half, qv_full, up_shift = whole
        vector_rows = vector_half.astype(jnp.float32)
        normed_in, first_normed, first_inverse = layer_norm(resid, vector_rows[0], vector_rows[1])
        first_all = gather_normed(normed_in.astype(jnp.bfloat16))
        total_rows = first_all.shape[0]
        heads = qv_full.shape[1]
        qv_flat = qv_full.astype(jnp.float32).reshape(2, -1)
        query = (
            jnp.dot(first_all, qkv_full[0], preferred_element_type=jnp.float32) + qv_flat[0]
        ).astype(jnp.bfloat16)
        keys = jnp.dot(first_all, qkv_full[1], preferred_element_type=jnp.float32).astype(
            jnp.bfloat16
        )
        values = (
            jnp.dot(first_all, qkv_full[2], preferred_element_type=jnp.float32) + qv_flat[1]
        ).astype(jnp.bfloat16)
        scores = attention_scores(query, keys, same_crop, heads)
        peak = jnp.max(scores, axis=-1, keepdims=True)
        powers = jnp.exp(scores - peak)
        totals = jnp.sum(powers, axis=-1, keepdims=True)
        probs = (powers / totals).astype(jnp.bfloat16)
        log_totals = peak + jnp.log(totals)
        attended = (
            jnp.einsum(
                "hqk,khd->qhd",
                probs,
                values.reshape(total_rows, heads, -1),
                preferred_element_type=jnp.float32,
            )
            .reshape(total_rows, -1)
            .astype(jnp.bfloat16)
        )

        def project_rows(start, size):
            return jnp.dot(attended, out_full, preferred_element_type=jnp.float32)

        projected = branch_sum(project_rows, resid.shape[0])
        middle = resid + vector_rows[3] * (projected + vector_rows[2])
        normed_mid, second_normed, second_inverse = layer_norm(
            middle, vector_rows[4], vector_rows[5]
        )
        second_all = gather_normed(normed_mid.astype(jnp.bfloat16))
        hidden_pre = jnp.dot(
            second_all, up_full, preferred_element_type=jnp.float32
        ) + up_shift.astype(jnp.float32).reshape(-1)
        hidden = (0.5 * hidden_pre * (1.0 + lax.erf(hidden_pre * INV_ROOT_TWO))).astype(
            jnp.bfloat16
        )

        def down_rows(start, size):
            return jnp.dot(hidden, down_full, preferred_element_type=jnp.float32)

        returned = branch_sum(down_rows, resid.shape[0])
        result = middle + vector_rows[7] * (returned + vector_rows[6])
        saved = (
            first_normed,
            first_inverse,
            first_all,
            query,
            keys,
            values,
            log_totals,
            attended,
            projected,
            second_normed,
            second_inverse,
            second_all,
            hidden_pre,
            hidden,
            returned,
        )
        return (result, saved)

    def backward_layer(upstream, same_crop, whole, saved):
        qkv_full, out_full, up_full, down_full, vector_half, qv_full, up_shift = whole
        (
            first_normed,
            first_inverse,
            first_all,
            query,
            keys,
            values,
            log_totals,
            attended,
            projected,
            second_normed,
            second_inverse,
            second_all,
            hidden_pre,
            hidden,
            returned,
        ) = saved
        vector_rows = vector_half.astype(jnp.float32)
        count = upstream.shape[0]
        total_rows = first_all.shape[0]
        heads = qv_full.shape[1]
        scaled_up = vector_rows[7] * upstream
        grad_shift_mlp = jnp.sum(scaled_up, axis=0)
        grad_scale_mlp = jnp.sum(upstream * (returned + vector_rows[6]), axis=0)
        returned_all = gather_upstream(scaled_up.astype(jnp.bfloat16))
        grad_down = contract_rows(hidden, returned_all)
        grad_hidden = against_rows(returned_all, down_full)
        normal_cdf = 0.5 * (1.0 + lax.erf(hidden_pre * INV_ROOT_TWO))
        normal_pdf = jnp.exp(-0.5 * hidden_pre * hidden_pre) * INV_ROOT_TAU
        grad_pre = (grad_hidden * (normal_cdf + hidden_pre * normal_pdf)).astype(jnp.bfloat16)
        grad_up_shift = jnp.sum(grad_pre.astype(jnp.float32), axis=0).reshape(-1, head_dim)
        grad_up = contract_rows(second_all, grad_pre)

        def up_rows(start, size):
            return against_rows(lax.dynamic_slice_in_dim(grad_pre, start, size, 0), up_full)

        grad_second = input_sum(up_rows, count)
        grad_mid_norm, grad_gain_two, grad_shift_two = norm_backward(
            grad_second, second_normed, second_inverse, vector_rows[4]
        )
        grad_middle = upstream + grad_mid_norm
        scaled_mid = vector_rows[3] * grad_middle
        grad_shift_attn = jnp.sum(scaled_mid, axis=0)
        grad_scale_attn = jnp.sum(grad_middle * (projected + vector_rows[2]), axis=0)
        projected_all = gather_upstream(scaled_mid.astype(jnp.bfloat16))
        grad_out = contract_rows(attended, projected_all)
        grad_attended = (
            against_rows(projected_all, out_full)
            .astype(jnp.bfloat16)
            .reshape(total_rows, heads, -1)
        )
        query_heads = query.reshape(total_rows, heads, -1)
        key_heads = keys.reshape(total_rows, heads, -1)
        value_heads = values.reshape(total_rows, heads, -1)
        scores = attention_scores(query, keys, same_crop, heads)
        probs = jnp.exp(scores - log_totals)
        grad_values = jnp.einsum(
            "hqk,qhd->khd",
            probs.astype(jnp.bfloat16),
            grad_attended,
            preferred_element_type=jnp.float32,
        )
        grad_probs = jnp.einsum(
            "qhd,khd->hqk", grad_attended, value_heads, preferred_element_type=jnp.float32
        )
        grad_scores = (
            probs * (grad_probs - jnp.sum(probs * grad_probs, axis=-1, keepdims=True))
        ).astype(jnp.bfloat16)
        grad_query = (
            jnp.einsum("hqk,khd->qhd", grad_scores, key_heads, preferred_element_type=jnp.float32)
            * scale
        )
        grad_keys = (
            jnp.einsum("hqk,qhd->khd", grad_scores, query_heads, preferred_element_type=jnp.float32)
            * scale
        )
        grad_project = (
            jnp.stack([grad_query, grad_keys, grad_values])
            .reshape(3, total_rows, -1)
            .astype(jnp.bfloat16)
        )
        grad_qv = jnp.stack(
            [
                jnp.sum(grad_project[0].astype(jnp.float32), axis=0),
                jnp.sum(grad_project[2].astype(jnp.float32), axis=0),
            ]
        ).reshape(2, heads, head_dim)
        grad_qkv = jnp.einsum(
            "rd,trc->tdc", first_all, grad_project, preferred_element_type=jnp.float32
        )

        def qkv_rows(start, size):
            return jnp.einsum(
                "trc,tdc->rd",
                lax.dynamic_slice_in_dim(grad_project, start, size, 1),
                qkv_full,
                preferred_element_type=jnp.float32,
            )

        grad_first = input_sum(qkv_rows, count)
        grad_in_norm, grad_gain_one, grad_shift_one = norm_backward(
            grad_first, first_normed, first_inverse, vector_rows[0]
        )
        grad_vectors = jnp.stack(
            [
                grad_gain_one,
                grad_shift_one,
                grad_shift_attn,
                grad_scale_attn,
                grad_gain_two,
                grad_shift_two,
                grad_shift_mlp,
                grad_scale_mlp,
            ]
        )
        parts = (grad_qkv, grad_out, grad_up, grad_down, grad_vectors, grad_qv, grad_up_shift)
        return (grad_middle + grad_in_norm, parts)

    shapes = [
        (3, width, qkv_weight.shape[3]),
        (out_weight.shape[1], width),
        (width, up_weight.shape[2]),
        (down_weight.shape[1], width),
        (8, width),
        (2, qv_bias.shape[2], head_dim),
        (up_bias.shape[1], head_dim),
    ]
    zeroed = tuple((jnp.zeros(shape, jnp.float32) for shape in shapes))
    start_sums = tuple((zeroed for layer in range(layers)))

    def one_micro(index, carry):
        sums, out_buffer, grad_buffer = carry
        resid = lax.dynamic_index_in_dim(tokens, index, 0, keepdims=False).astype(jnp.float32)
        crop_ids = lax.dynamic_index_in_dim(segments, index, 0, keepdims=False)
        same_crop = (crop_ids[:, None] == crop_ids[None, :])[None]
        wholes = []
        saves = []
        for layer in range(layers):
            whole = (
                lax.all_gather(qkv_weight[layer], "dp", axis=1, tiled=True),
                lax.all_gather(out_weight[layer], "dp", axis=1, tiled=True),
                lax.all_gather(up_weight[layer], "dp", axis=0, tiled=True),
                lax.all_gather(down_weight[layer], "dp", axis=1, tiled=True),
                lax.all_gather(vectors[layer], "dp", axis=1, tiled=True),
                lax.all_gather(qv_bias[layer], "dp", axis=2, tiled=True),
                lax.all_gather(up_bias[layer], "dp", axis=1, tiled=True),
            )
            resid, saved = forward_layer(resid, same_crop, whole)
            wholes.append(whole)
            saves.append(saved)
        out_buffer = lax.dynamic_update_index_in_dim(
            out_buffer, resid.astype(jnp.bfloat16), index, 0
        )
        upstream = lax.dynamic_index_in_dim(cotangent, index, 0, keepdims=False).astype(jnp.float32)
        new_sums = list(sums)
        for layer in reversed(range(layers)):
            whole = (
                lax.all_gather(qkv_weight[layer], "dp", axis=1, tiled=True),
                lax.all_gather(out_weight[layer], "dp", axis=1, tiled=True),
                lax.all_gather(up_weight[layer], "dp", axis=0, tiled=True),
                lax.all_gather(down_weight[layer], "dp", axis=1, tiled=True),
                lax.all_gather(vectors[layer], "dp", axis=1, tiled=True),
                lax.all_gather(qv_bias[layer], "dp", axis=2, tiled=True),
                lax.all_gather(up_bias[layer], "dp", axis=1, tiled=True),
            )
            upstream, parts = backward_layer(upstream, same_crop, whole, saves[layer])
            new_sums[layer] = tuple((total + piece for total, piece in zip(sums[layer], parts)))
        grad_buffer = lax.dynamic_update_index_in_dim(grad_buffer, upstream, index, 0)
        return (tuple(new_sums), out_buffer, grad_buffer)

    start = (
        start_sums,
        jnp.zeros(tokens.shape, jnp.bfloat16),
        jnp.zeros(tokens.shape, jnp.float32),
    )
    sums, output, tokens_grad = lax.fori_loop(0, micro, one_micro, start)
    reduced = []
    for layer in range(layers):
        totals = sums[layer]
        totals = (
            lax.psum_scatter(
                totals[0].astype(jnp.bfloat16), "dp", scatter_dimension=1, tiled=True
            ).astype(jnp.float32),
            lax.psum_scatter(
                totals[1].astype(jnp.bfloat16), "dp", scatter_dimension=1, tiled=True
            ).astype(jnp.float32),
            lax.psum_scatter(
                totals[2].astype(jnp.bfloat16), "dp", scatter_dimension=0, tiled=True
            ).astype(jnp.float32),
            lax.psum_scatter(
                totals[3].astype(jnp.bfloat16), "dp", scatter_dimension=1, tiled=True
            ).astype(jnp.float32),
            lax.psum_scatter(
                totals[4].astype(jnp.bfloat16), "dp", scatter_dimension=1, tiled=True
            ).astype(jnp.float32),
            lax.psum_scatter(
                totals[5].astype(jnp.bfloat16), "dp", scatter_dimension=2, tiled=True
            ).astype(jnp.float32),
            lax.psum_scatter(
                totals[6].astype(jnp.bfloat16), "dp", scatter_dimension=1, tiled=True
            ).astype(jnp.float32),
        )
        reduced.append(totals)
    stacked = [
        jnp.stack([reduced[layer][member] for layer in range(layers)]) for member in range(7)
    ]
    vector_total = lax.psum(stacked[4], "mp")
    return (
        output,
        tokens_grad,
        stacked[0],
        stacked[1],
        stacked[2],
        stacked[3],
        vector_total,
        stacked[5],
        stacked[6],
    )


MESH = pl.DeviceIdType.MESH
NZ, NY, NC, NX = 4, 2, 2, 2
SHARD = 64
COLS = 6144
CHUNK = 1024
PER_LAYER = COLS // CHUNK
ROUTES = (("zxy", 0, 16, 0, 1024), ("yzx", 16, 48, 0, 512), ("xzy", 16, 48, 512, 512))
LAG = 2


class Place:
    def __init__(self):
        dp = lax.axis_index("dp")
        self.x = lax.axis_index("mp")
        self.z = dp // 4
        self.y = lax.rem(dp // 2, 2)
        self.c = lax.rem(dp, 2)

    def device(self, x=None, z=None, y=None, c=None):
        x = self.x if x is None else x
        z = self.z if z is None else z
        y = self.y if y is None else y
        c = self.c if c is None else c
        return (z * 4 + y * 2 + c, x)

    def other(self, axis):
        if axis == "x":
            return self.device(x=1 - self.x)
        if axis == "y":
            return self.device(y=1 - self.y)
        return self.device(c=1 - self.c)

    def along(self, k):
        return lax.rem(self.z + k, NZ)


def greet(place):
    barrier = pltpu.get_barrier_semaphore()
    for axis in "cxy":
        pl.semaphore_signal(barrier, inc=1, device_id=place.other(axis), device_id_type=MESH)
    for k in (1, 2, 3):
        pl.semaphore_signal(
            barrier, inc=1, device_id=place.device(z=place.along(k)), device_id_type=MESH
        )
    pl.semaphore_wait(barrier, 6)


def block(place, filled, z=None):
    return (
        slice(None) if "x" in filled else place.x,
        slice(None) if "z" in filled else (place.z if z is None else z),
        slice(None) if "y" in filled else place.y,
        place.c,
    )


class Spread:
    def __init__(self, place, axis, source, target, send, recv, base):
        self.place, self.axis = place, axis
        self.source, self.target = source, target
        self.send, self.recv, self.base = send, recv, base

    def single(self):
        return pltpu.make_async_remote_copy(
            src_ref=self.source, dst_ref=self.target(None),
            send_sem=self.send(self.base), recv_sem=self.recv(self.base),
            device_id=self.place.other(self.axis), device_id_type=MESH)

    def direct(self, k):
        place = self.place
        return pltpu.make_async_remote_copy(
            src_ref=self.source, dst_ref=self.target(None),
            send_sem=self.send(self.base + k), recv_sem=self.recv(self.base + place.z),
            device_id=place.device(z=place.along(k)), device_id_type=MESH)

    def arrival(self, z):
        place = self.place
        return pltpu.make_async_remote_copy(
            src_ref=self.source, dst_ref=self.target(z),
            send_sem=self.send(self.base), recv_sem=self.recv(self.base + z),
            device_id=place.device(z=z), device_id_type=MESH)

    def passed(self):
        place = self.place
        origin = jnp.where(place.z == 2, 0, 3)
        return origin, pltpu.make_async_remote_copy(
            src_ref=self.target(origin), dst_ref=self.target(origin),
            send_sem=self.send(self.base), recv_sem=self.recv(self.base + origin),
            device_id=place.device(z=3 - origin), device_id_type=MESH)

    def start(self):
        if self.axis != "z":
            self.single().start()
            return
        for k in (1, 2, 3):
            if k == 2:
                self.direct(k).start()
            else:
                @pl.when(self.place.z != (3 if k == 1 else 0))
                def _():
                    self.direct(k).start()

    def relay(self):
        if self.axis != "z":
            return

        @pl.when((self.place.z == 1) | (self.place.z == 2))
        def _():
            origin, copy = self.passed()
            self.arrival(origin).wait_recv()
            copy.start()

    def arrive(self):
        if self.axis != "z":
            self.single().wait_recv()
            return
        z = self.place.z
        inner = (z == 1) | (z == 2)
        far = jnp.where(z == 2, 0, 3)
        for k in (1, 2, 3):
            origin = lax.rem(z + k, NZ)

            @pl.when(jnp.logical_not(inner & (origin == far)))
            def _():
                self.arrival(origin).wait_recv()

    def finish(self):
        if self.axis != "z":
            self.single().wait_send()
            return
        for k in (1, 2, 3):
            if k == 2:
                self.direct(k).wait_send()
            else:
                @pl.when(self.place.z != (3 if k == 1 else 0))
                def _():
                    self.direct(k).wait_send()

        @pl.when((self.place.z == 1) | (self.place.z == 2))
        def _():
            self.passed()[1].wait_send()


class Gather:
    def __init__(self, place, chunks, shard, whole, send, recv, sib, local):
        self.place, self.chunks = place, chunks
        self.shard, self.whole = shard, whole
        self.send, self.recv, self.sib, self.local = send, recv, sib, local

    def spot(self, step):
        return step // PER_LAYER, lax.rem(step, PER_LAYER) * CHUNK

    def spread(self, step, route, phase):
        order, row, rows, col, cols = ROUTES[route]
        layer, first = self.spot(step)
        area = (pl.ds(row, rows), pl.ds(pl.multiple_of(first + col, 128), cols))
        filled = order[:phase]
        target = lambda z: self.whole.at[(layer,) + block(self.place, filled, z) + area]
        source = self.shard.at[(layer,) + area] if phase == 0 else target(None)
        axis = order[phase]
        base = {"z": 0, "y": 4, "x": 5}[axis]
        return Spread(
            self.place, axis, source, target,
            lambda slot: self.send.at[step, route, slot], lambda slot: self.recv.at[step, route, slot], base)

    def own(self, step):
        layer, first = self.spot(step)
        cols = pl.ds(pl.multiple_of(first, CHUNK), CHUNK)
        return pltpu.make_async_copy(
            self.shard.at[layer, :, cols],
            self.whole.at[(layer,) + block(self.place, "") + (slice(None), cols)], self.local.at[step])

    def sibling(self, step):
        layer, first = self.spot(step)
        cols = pl.ds(pl.multiple_of(first, CHUNK), CHUNK)
        part = self.whole.at[(layer,) + block(self.place, "xyz") + (slice(None), cols)]
        return pltpu.make_async_remote_copy(
            src_ref=part, dst_ref=part, send_sem=self.sib.at[0, step], recv_sem=self.sib.at[1, step],
            device_id=self.place.other("c"), device_id_type=MESH)

    def phase(self, step, number):
        every = range(len(ROUTES))
        if number == 0:
            self.own(step).start()
        if number == 1:
            self.own(step).wait()
        for route in every:
            if 1 <= number <= 3:
                self.spread(step, route, number - 1).arrive()
            if number <= 2:
                self.spread(step, route, number).start()
        if number == 3:
            self.sibling(step).start()
        if number == 4:
            self.sibling(step).wait()
            for route in every:
                for phase in range(3):
                    self.spread(step, route, phase).finish()

    def tick(self, step):
        for number in range(5):
            at = step - LAG * number

            @pl.when((at >= 0) & (at < self.chunks))
            def _():
                self.phase(at, number)
            if number < 3:
                early = step - LAG * number - 1

                @pl.when((early >= 0) & (early < self.chunks))
                def _():
                    for route in range(len(ROUTES)):
                        self.spread(early, route, number).relay()

    @property
    def ticks(self):
        return self.chunks + 4 * LAG


def ag_kernel(chunks, shard, small, tokens, cotangent, whole, small_all, mine, mine_grad, send, recv, sib, local, odd):
    place = Place()
    greet(place)
    gather = Gather(place, chunks, shard, whole, send, recv, sib, local)

    def halves(n, source, target):
        return (
            pltpu.make_async_remote_copy(
                src_ref=source.at[1 - place.x], dst_ref=target.at[place.x],
                send_sem=odd.at[4 * n], recv_sem=odd.at[4 * n + 1],
                device_id=place.other("x"), device_id_type=MESH),
            pltpu.make_async_copy(source.at[place.x], target.at[place.x], odd.at[4 * n + 2]),
        )

    order = "zyx"

    def small_spread(phase):
        target = lambda z: small_all.at[block(place, order[:phase], z)]
        base = {"z": 0, "y": 4, "x": 5}[order[phase]]
        return Spread(
            place, order[phase], small if phase == 0 else target(None), target,
            lambda slot: odd.at[8 + slot], lambda slot: odd.at[16 + slot], base)

    part = small_all.at[block(place, "xyz")]
    small_sibling = pltpu.make_async_remote_copy(
        src_ref=part, dst_ref=part, send_sem=odd.at[24], recv_sem=odd.at[25],
        device_id=place.other("c"), device_id_type=MESH)
    small_own = pltpu.make_async_copy(small, small_all.at[block(place, "")], odd.at[26])
    token_copies = halves(0, tokens, mine)
    grad_copies = halves(1, cotangent, mine_grad)
    for copy in token_copies:
        copy.start()
    small_own.start()
    small_spread(0).start()

    def tick(step, carry):
        @pl.when(step == 1)
        def _():
            small_spread(0).relay()
            small_own.wait()

        for phase in (1, 2):
            @pl.when(step == 1 + phase)
            def _():
                small_spread(phase - 1).arrive()
                small_spread(phase).start()

        @pl.when(step == 4)
        def _():
            small_spread(2).arrive()
            small_sibling.start()
        gather.tick(step)

        @pl.when(step == chunks // 2)
        def _():
            for copy in grad_copies:
                copy.start()
        return carry

    lax.fori_loop(0, gather.ticks, tick, 0)
    small_sibling.wait()
    for phase in range(3):
        small_spread(phase).finish()
    for copy in token_copies + grad_copies:
        copy.wait()


def gather_all(shard, small, tokens, cotangent):
    layers = shard.shape[0]
    chunks = layers * PER_LAYER
    half = tokens.shape
    any_spec = pl.BlockSpec(memory_space=pl.ANY)
    return pl.pallas_call(
        functools.partial(ag_kernel, chunks),
        out_shape=(
            jax.ShapeDtypeStruct((layers, NX, NZ, NY, NC, SHARD, COLS), jnp.bfloat16),
            jax.ShapeDtypeStruct((NX, NZ, NY, NC) + small.shape, small.dtype),
            jax.ShapeDtypeStruct(half, jnp.bfloat16),
            jax.ShapeDtypeStruct(half, jnp.bfloat16),
        ),
        in_specs=[pl.BlockSpec(memory_space=pltpu.VMEM)] * 4,
        out_specs=(any_spec,) * 4,
        scratch_shapes=[
            pltpu.SemaphoreType.DMA((chunks, len(ROUTES), 6)),
            pltpu.SemaphoreType.DMA((chunks, len(ROUTES), 6)),
            pltpu.SemaphoreType.DMA((2, chunks)),
            pltpu.SemaphoreType.DMA((chunks,)),
            pltpu.SemaphoreType.DMA((32,)),
        ],
        compiler_params=pltpu.CompilerParams(collective_id=1, has_side_effects=True, vmem_limit_bytes=32 * 1024 * 1024),
        name="gather_all",
    )(shard, small, tokens, cotangent)
SLOTS = 5


class Scatter:
    def __init__(self, place, chunks, grads, summed, acc, near, first, second, third, send, recv, local, free):
        self.place, self.chunks = place, chunks
        self.grads, self.summed = grads, summed
        self.acc, self.near = acc, near
        self.landing = (first, second, third)
        self.send, self.recv, self.local, self.free = send, recv, local, free

    def spot(self, step):
        chunk = self.chunks - 1 - step
        return chunk // PER_LAYER, pl.multiple_of(lax.rem(chunk, PER_LAYER) * CHUNK, CHUNK)

    def slot(self, step):
        return lax.rem(step, SLOTS)

    def core_copies(self, step):
        layer, first = self.spot(step)
        cols = pl.ds(first, CHUNK)
        slot = self.slot(step)
        return (
            pltpu.make_async_remote_copy(
                src_ref=self.grads.at[layer, :, :, :, 1 - self.place.c, :, cols], dst_ref=self.near.at[slot],
                send_sem=self.send.at[step, len(ROUTES), 0], recv_sem=self.recv.at[step, len(ROUTES), 0],
                device_id=self.place.other("c"), device_id_type=MESH),
            pltpu.make_async_copy(
                self.grads.at[layer, :, :, :, self.place.c, :, cols], self.acc.at[slot], self.local.at[step]),
        )

    def core_add(self, step):
        slot = self.slot(step)

        def one(n, carry):
            x, z, y = n // 8, lax.rem(n // 2, 4), lax.rem(n, 2)
            self.acc[slot, x, z, y] = self.acc[slot, x, z, y] + self.near[slot, x, z, y]
            return carry

        lax.fori_loop(0, NX * NZ * NY, one, 0)

    def area(self, route):
        _, row, rows, col, cols = ROUTES[route]
        return (pl.ds(row, rows), pl.ds(col, cols))

    def index(self, route, phase, over):
        order = ROUTES[route][0]
        left = order[:2 - phase]
        place = self.place
        picked = []
        for axis, own in (("x", place.x), ("z", place.z), ("y", place.y)):
            picked.append(over[axis] if axis in over else (slice(None) if axis in left else own))
        return tuple(picked)

    def copy(self, step, route, phase, over, device, source_slot, sem):
        slot = self.slot(step)
        axis = ROUTES[route][0][2 - phase]
        land = self.landing[phase][route].at[slot]
        if axis == "z":
            land = land.at[source_slot]
        base = {"z": 0, "y": 4, "x": 5}[axis]
        return pltpu.make_async_remote_copy(
            src_ref=self.acc.at[(slot,) + self.index(route, phase, over) + self.area(route)], dst_ref=land,
            send_sem=self.send.at[step, route, base + sem], recv_sem=self.recv.at[step, route, base + source_slot],
            device_id=device, device_id_type=MESH)

    def single(self, step, route, phase):
        axis = ROUTES[route][0][2 - phase]
        own = self.place.x if axis == "x" else self.place.y
        return self.copy(step, route, phase, {axis: 1 - own}, self.place.other(axis), 0, 0)

    def along(self, step, route, phase, k):
        place = self.place
        z = place.along(k)
        far = (place.z + z == 3) & ((place.z == 0) | (place.z == 3))
        via = jnp.where(far, jnp.where(place.z == 0, 1, 2), z)
        return self.copy(
            step, route, phase, {"z": z}, place.device(z=via), jnp.where(far, via, place.z), k)

    def arrival(self, step, route, phase, z):
        return self.copy(step, route, phase, {"z": self.place.z}, self.place.device(z=lax.rem(z + 1, NZ)), z, 1)

    def start(self, step, route, phase):
        if ROUTES[route][0][2 - phase] != "z":
            self.single(step, route, phase).start()
            return
        z = self.place.z
        for k in (1, 2, 3):
            if k == 2:
                @pl.when((z == 0) | (z == 3))
                def _():
                    self.along(step, route, phase, k).start()
            else:
                self.along(step, route, phase, k).start()

    def relay(self, step, route, phase):
        if ROUTES[route][0][2 - phase] != "z":
            return
        z = self.place.z
        slot = self.slot(step)

        @pl.when((z == 1) | (z == 2))
        def _():
            self.arrival(step, route, phase, z).wait_recv()
            far = lax.rem(z + 2, NZ)
            at = (slot,) + self.index(route, phase, {"z": far}) + self.area(route)
            self.acc[at] = self.acc[at] + self.landing[phase][route][slot, z]
            self.along(step, route, phase, 2).start()

    def arrive(self, step, route, phase):
        slot = self.slot(step)
        area = self.area(route)
        axis = ROUTES[route][0][2 - phase]
        land = self.landing[phase][route]
        if axis != "z":
            self.single(step, route, phase).wait_recv()
            at = self.index(route, phase, {axis: self.place.x if axis == "x" else self.place.y})
            lead = [n for n, entry in enumerate(at) if isinstance(entry, slice)]
            extents = [(NX, NZ, NY)[n] for n in lead]
            total = 1
            for extent in extents:
                total *= extent

            def one(n, carry):
                part = []
                for extent in reversed(extents):
                    part.append(lax.rem(n, extent))
                    n = n // extent
                part.reverse()
                full = list(at)
                for position, value in zip(lead, part):
                    full[position] = value
                self.acc[(slot,) + tuple(full) + area] = (
                    self.acc[(slot,) + tuple(full) + area] + land[(slot,) + tuple(part)])
                return carry

            if total == 1:
                one(0, 0)
            else:
                lax.fori_loop(0, total, one, 0)
            return
        z = self.place.z
        ends = (z == 0) | (z == 3)
        at = (slot,) + self.index(route, phase, {"z": z}) + area
        for k in (1, 2, 3):
            origin = lax.rem(z + k, NZ)

            @pl.when(jnp.logical_not(ends & (z + origin == 3)))
            def _():
                self.arrival(step, route, phase, origin).wait_recv()
                self.acc[at] = self.acc[at] + land[slot, origin]

    def finish(self, step, route, phase):
        if ROUTES[route][0][2 - phase] != "z":
            self.single(step, route, phase).wait_send()
            return
        for k in (1, 2, 3):
            self.along(step, route, phase, k).wait_send()

    def others(self):
        place = self.place
        pairs = [(place.other(axis), n, n) for n, axis in enumerate("cxy")]
        for k in (1, 2, 3):
            z = place.along(k)
            pairs.append((place.device(z=z), 3 + place.z, 3 + z))
        return pairs

    def phase(self, step, number):
        every = range(len(ROUTES))
        if number == 0:
            @pl.when(step >= SLOTS)
            def _():
                for _, _, mine in self.others():
                    pl.semaphore_wait(self.free.at[mine], 1)
            for copy in self.core_copies(step):
                copy.start()
            return
        if number == 1:
            remote, own = self.core_copies(step)
            own.wait()
            remote.wait_recv()
            self.core_add(step)
        for route in every:
            if number >= 2:
                self.arrive(step, route, number - 2)
            if number <= 3:
                self.start(step, route, number - 1)
        if number == 4:
            slot = self.slot(step)
            layer, first = self.spot(step)
            place = self.place
            self.summed[layer, :, pl.ds(first, CHUNK)] = self.acc[slot, place.x, place.z, place.y].astype(jnp.float32)
            self.core_copies(step)[0].wait_send()
            for route in every:
                for phase in range(3):
                    self.finish(step, route, phase)

            @pl.when(step + SLOTS < self.chunks)
            def _():
                for device, there, _ in self.others():
                    pl.semaphore_signal(self.free.at[there], inc=1, device_id=device, device_id_type=MESH)

    def tick(self, step):
        for number in (4, 3, 2, 1, 0):
            at = step - number

            @pl.when((at >= 0) & (at < self.chunks))
            def _():
                self.phase(at, number)
            if number >= 2:
                pass
        for number in (1, 2, 3):
            at = step - number

            @pl.when((at >= 0) & (at < self.chunks))
            def _():
                for route in range(len(ROUTES)):
                    self.relay(at, route, number - 1)

    @property
    def ticks(self):
        return self.chunks + 4


def landing_shapes():
    shapes = []
    for phase in range(3):
        for order, row, rows, col, cols in ROUTES:
            left = order[:2 - phase]
            axis = order[2 - phase]
            lead = tuple(extent for name, extent in (("x", NX), ("z", NZ), ("y", NY)) if name in left)
            if axis == "z":
                lead = (NZ,) + lead
            shapes.append(pltpu.VMEM((SLOTS,) + lead + (rows, cols), jnp.bfloat16))
    return shapes


def rs_kernel(chunks, grads, small, output, tokens_grad, summed, small_sum, out_rows, grad_rows, *scratch):
    acc, near = scratch[:2]
    n = len(ROUTES)
    lands = scratch[2:2 + 3 * n]
    small_acc, small_c, small_x, small_y, small_z, send, recv, local, free, odd = scratch[2 + 3 * n:]
    place = Place()
    greet(place)
    scatter = Scatter(place, chunks, grads, summed, acc, near, lands[:n], lands[n:2 * n], lands[2 * n:], send, recv, local, free)

    def halves(n, source, target):
        return (
            pltpu.make_async_remote_copy(
                src_ref=source.at[1 - place.x], dst_ref=target.at[place.x],
                send_sem=odd.at[4 * n], recv_sem=odd.at[4 * n + 1],
                device_id=place.other("x"), device_id_type=MESH),
            pltpu.make_async_copy(source.at[place.x], target.at[place.x], odd.at[4 * n + 2]),
        )

    def small_copy(source, target, device, base, there=0):
        return pltpu.make_async_remote_copy(
            src_ref=source, dst_ref=target, send_sem=odd.at[8 + base], recv_sem=odd.at[16 + there],
            device_id=device, device_id_type=MESH)

    core = small_copy(small.at[1 - place.c], small_c, place.other("c"), 0, 0)
    over_x = small_copy(small_acc.at[1 - place.x], small_x, place.other("x"), 1, 1)
    over_y = small_copy(small_acc.at[place.x, 1 - place.y], small_y, place.other("y"), 2, 2)
    over_z = [
        small_copy(small_acc.at[place.x, place.y, place.along(k)], small_z.at[k - 1], place.device(z=place.along(k)), 2 + k, 2 + k)
        for k in (1, 2, 3)
    ]
    rows_copies = halves(0, output, out_rows) + halves(1, tokens_grad, grad_rows)
    for copy in rows_copies:
        copy.start()
    core.start()

    def tick(step, carry):
        @pl.when(step == 1)
        def _():
            core.wait()
            small_acc[...] = small[place.c] + small_c[...]
            over_x.start()

        @pl.when(step == 2)
        def _():
            over_x.wait()
            small_acc[place.x] = small_acc[place.x] + small_x[...]
            over_y.start()

        @pl.when(step == 3)
        def _():
            over_y.wait()
            small_acc[place.x, place.y] = small_acc[place.x, place.y] + small_y[...]
            for copy in over_z:
                copy.start()
        scatter.tick(step)
        return carry

    lax.fori_loop(0, scatter.ticks, tick, 0)
    for copy in over_z:
        copy.wait()
    small_sum[...] = small_acc[place.x, place.y, place.z] + small_z[0] + small_z[1] + small_z[2]
    for copy in rows_copies:
        copy.wait()


def scatter_all(grads, small, output, tokens_grad):
    layers = grads.shape[0]
    chunks = layers * PER_LAYER
    any_spec = pl.BlockSpec(memory_space=pl.ANY)
    vmem = pl.BlockSpec(memory_space=pltpu.VMEM)
    tail = small.shape[4:]
    return pl.pallas_call(
        functools.partial(rs_kernel, chunks),
        out_shape=(
            jax.ShapeDtypeStruct((layers, SHARD, COLS), jnp.float32),
            jax.ShapeDtypeStruct(tail, jnp.float32),
            jax.ShapeDtypeStruct(output.shape, output.dtype),
            jax.ShapeDtypeStruct(tokens_grad.shape, tokens_grad.dtype),
        ),
        in_specs=[any_spec, vmem, vmem, vmem],
        out_specs=(vmem, vmem, any_spec, any_spec),
        scratch_shapes=[
            pltpu.VMEM((SLOTS, NX, NZ, NY, SHARD, CHUNK), jnp.bfloat16),
            pltpu.VMEM((SLOTS, NX, NZ, NY, SHARD, CHUNK), jnp.bfloat16),
        ] + landing_shapes() + [
            pltpu.VMEM((NX, NY, NZ) + tail, jnp.float32),
            pltpu.VMEM((NX, NY, NZ) + tail, jnp.float32),
            pltpu.VMEM((NY, NZ) + tail, jnp.float32),
            pltpu.VMEM((NZ,) + tail, jnp.float32),
            pltpu.VMEM((3,) + tail, jnp.float32),
            pltpu.SemaphoreType.DMA((chunks, len(ROUTES) + 1, 6)),
            pltpu.SemaphoreType.DMA((chunks, len(ROUTES) + 1, 6)),
            pltpu.SemaphoreType.DMA((chunks,)),
            pltpu.SemaphoreType.REGULAR((7,)),
            pltpu.SemaphoreType.DMA((32,)),
        ],
        compiler_params=pltpu.CompilerParams(collective_id=2, has_side_effects=True, vmem_limit_bytes=56 * 1024 * 1024),
        name="scatter_all",
    )(grads, small, output, tokens_grad)


WINDOWS = ((0, 208), (208, 208), (416, 224))
PADDED = 640
HALF_PAD = 320


def pack_small(vectors, qv_bias, up_bias):
    flat = jnp.concatenate([vectors.reshape(-1), qv_bias.reshape(-1), up_bias.reshape(-1)])
    return jnp.pad(flat, (0, 2048 - flat.shape[0])).reshape(16, 128)


def placement(ids):
    same = ids[:, None] == ids[None, :]
    count = jnp.sum(same, axis=1)
    order = jnp.arange(ids.shape[0])
    before = order[None, :] < order[:, None]
    long = count > 100
    kind = (long[:, None] == long[None, :]) & before
    inside = jnp.sum(same & before, axis=1)
    earlier = jnp.sum(kind, axis=1) - inside
    return jnp.where(long, jnp.where(earlier > 0, 208, 0) + inside, 416 + earlier + inside)


def on_device_fast(
    tokens, segments, qkv_weight, out_weight, up_weight, down_weight, vectors, qv_bias, up_bias, cotangent
):
    layers = qkv_weight.shape[0]
    half = tokens.shape[1]
    width = tokens.shape[2]
    place_x = lax.axis_index("mp")
    shard = jnp.concatenate(
        [qkv_weight[:, 0], qkv_weight[:, 1], qkv_weight[:, 2], jnp.swapaxes(out_weight, 1, 2),
         up_weight, jnp.swapaxes(down_weight, 1, 2)], axis=2)
    extra = ((0, 0), (0, HALF_PAD - half), (0, 0))
    whole, small_all, mine, mine_grad = gather_all(
        shard, pack_small(vectors, qv_bias, up_bias), jnp.pad(tokens, extra), jnp.pad(cotangent, extra))
    weights = whole.reshape(layers, 2, width, COLS)
    small_flat = small_all.reshape(2, 16, 2048).astype(jnp.float32)
    vector_all = small_flat[0, :, :1024].reshape(16, layers, 8, 64).transpose(1, 2, 0, 3).reshape(layers, 8, width)
    qv_all = small_flat[:, :, 1024:1152].reshape(2, 16, layers, 2, 8, 4).transpose(2, 3, 0, 4, 1, 5).reshape(layers, 2, width)
    up_all = small_flat[:, :, 1152:1408].reshape(2, 16, layers, 32, 4).transpose(2, 0, 3, 1, 4).reshape(layers, 4096)

    ids = lax.dynamic_index_in_dim(segments, place_x, 0, keepdims=False)
    position = placement(ids)
    spread = jnp.concatenate([
        jnp.pad(position[:half], (0, HALF_PAD - half), constant_values=-1),
        jnp.pad(position[half:], (0, HALF_PAD - half), constant_values=-1)])
    to_place = (jnp.arange(PADDED)[:, None] == spread[None, :]).astype(jnp.bfloat16)
    new_ids = jnp.max(jnp.where(jnp.arange(PADDED)[:, None] == position[None, :], ids[None, :], -1), axis=1)

    def sort(rows):
        return jnp.dot(to_place, rows, preferred_element_type=jnp.float32)

    def unsort(rows):
        return jnp.dot(to_place.T, rows, preferred_element_type=jnp.float32).astype(jnp.bfloat16)

    resid = sort(mine.reshape(PADDED, width))
    upstream = sort(mine_grad.reshape(PADDED, width))
    masks = [(new_ids[a:a + n][:, None] == new_ids[a:a + n][None, :])[None] for a, n in WINDOWS]
    scale = 0.125

    def project(rows, weight):
        return jnp.einsum("rd,xdc->rxc", rows, weight, preferred_element_type=jnp.float32).reshape(rows.shape[0], -1)

    def project_t(rows, weight):
        return jnp.einsum("rxi,xoi->ro", rows.reshape(rows.shape[0], 2, -1), weight, preferred_element_type=jnp.float32)

    def heads(rows, a, n):
        return rows[a:a + n].reshape(n, 16, 64)

    def probabilities(query, keys, w):
        a, n = WINDOWS[w]
        raw = jnp.einsum("qhd,khd->hqk", heads(query, a, n), heads(keys, a, n), preferred_element_type=jnp.float32) * scale
        raw = jnp.where(masks[w], raw, -1e9)
        powers = jnp.exp(raw - jnp.max(raw, axis=-1, keepdims=True))
        return powers / jnp.sum(powers, axis=-1, keepdims=True)

    saves = []
    for layer in range(layers):
        w = weights[layer]
        vec = vector_all[layer]
        normed_in, n1, r1 = layer_norm(resid, vec[0], vec[1])
        first = normed_in.astype(jnp.bfloat16)
        query = (project(first, w[:, :, 0:512]) + qv_all[layer, 0]).astype(jnp.bfloat16)
        keys = project(first, w[:, :, 512:1024]).astype(jnp.bfloat16)
        values = (project(first, w[:, :, 1024:1536]) + qv_all[layer, 1]).astype(jnp.bfloat16)
        parts = []
        for i, (a, n) in enumerate(WINDOWS):
            probs = probabilities(query, keys, i).astype(jnp.bfloat16)
            parts.append(jnp.einsum("hqk,khd->qhd", probs, heads(values, a, n), preferred_element_type=jnp.float32).reshape(n, -1))
        attended = jnp.concatenate(parts).astype(jnp.bfloat16)
        projected = project_t(attended, w[:, :, 1536:2048])
        middle = resid + vec[3] * (projected + vec[2])
        normed_mid, n2, r2 = layer_norm(middle, vec[4], vec[5])
        second = normed_mid.astype(jnp.bfloat16)
        pre = project(second, w[:, :, 2048:4096]) + up_all[layer]
        hidden = (0.5 * pre * (1.0 + lax.erf(pre * INV_ROOT_TWO))).astype(jnp.bfloat16)
        returned = project_t(hidden, w[:, :, 4096:])
        resid = middle + vec[7] * (returned + vec[6])
        saves.append((n1, r1, first, query, keys, values, attended, projected, n2, r2, second, pre, hidden, returned))
    output = resid.astype(jnp.bfloat16)

    def grad_w(left, right):
        n = right.shape[1] // 2
        return jnp.einsum("rd,rxc->xdc", left, right.reshape(-1, 2, n), preferred_element_type=jnp.float32).astype(jnp.bfloat16)

    all_grads = [None] * layers
    small_grads = [None] * layers
    for layer in reversed(range(layers)):
        w = weights[layer]
        vec = vector_all[layer]
        n1, r1, first, query, keys, values, attended, projected, n2, r2, second, pre, hidden, returned = saves[layer]
        scaled_up = vec[7] * upstream
        g6 = jnp.sum(scaled_up, axis=0)
        g7 = jnp.sum(upstream * (returned + vec[6]), axis=0)
        d_returned = scaled_up.astype(jnp.bfloat16)
        grad_down = grad_w(d_returned, hidden)
        d_hidden = project(d_returned, w[:, :, 4096:])
        cdf = 0.5 * (1.0 + lax.erf(pre * INV_ROOT_TWO))
        pdf = jnp.exp(-0.5 * pre * pre) * INV_ROOT_TAU
        d_pre = (d_hidden * (cdf + pre * pdf)).astype(jnp.bfloat16)
        g_up_bias = jnp.sum(d_pre.astype(jnp.float32), axis=0)
        grad_up = grad_w(second, d_pre)
        d_second = project_t(d_pre, w[:, :, 2048:4096])
        d_mid, g4, g5 = norm_backward(d_second, n2, r2, vec[4])
        d_middle = upstream + d_mid
        scaled_mid = vec[3] * d_middle
        g2 = jnp.sum(scaled_mid, axis=0)
        g3 = jnp.sum(d_middle * (projected + vec[2]), axis=0)
        d_projected = scaled_mid.astype(jnp.bfloat16)
        grad_out = grad_w(d_projected, attended)
        d_attended = project(d_projected, w[:, :, 1536:2048]).astype(jnp.bfloat16)
        dq, dk, dv = [], [], []
        for i, (a, n) in enumerate(WINDOWS):
            p = probabilities(query, keys, i)
            da = heads(d_attended, a, n)
            dv.append(jnp.einsum("hqk,qhd->khd", p.astype(jnp.bfloat16), da, preferred_element_type=jnp.float32).reshape(n, -1))
            dp = jnp.einsum("qhd,khd->hqk", da, heads(values, a, n), preferred_element_type=jnp.float32)
            ds = (p * (dp - jnp.sum(p * dp, axis=-1, keepdims=True))).astype(jnp.bfloat16)
            dq.append((jnp.einsum("hqk,khd->qhd", ds, heads(keys, a, n), preferred_element_type=jnp.float32) * scale).reshape(n, -1))
            dk.append((jnp.einsum("hqk,qhd->khd", ds, heads(query, a, n), preferred_element_type=jnp.float32) * scale).reshape(n, -1))
        dq, dk, dv = [jnp.concatenate(v).astype(jnp.bfloat16) for v in (dq, dk, dv)]
        g_qv = jnp.stack([jnp.sum(dq.astype(jnp.float32), axis=0), jnp.sum(dv.astype(jnp.float32), axis=0)])
        d_first = project_t(dq, w[:, :, 0:512]) + project_t(dk, w[:, :, 512:1024]) + project_t(dv, w[:, :, 1024:1536])
        d_in, g0, g1 = norm_backward(d_first, n1, r1, vec[0])
        upstream = d_middle + d_in
        all_grads[layer] = jnp.concatenate(
            [grad_w(first, dq), grad_w(first, dk), grad_w(first, dv), grad_out, grad_up, grad_down], axis=2)
        small_grads[layer] = (jnp.stack([g0, g1, g2, g3, g4, g5, g6, g7]), g_qv, g_up_bias)
    grads = jnp.stack(all_grads).reshape(layers, NX, NZ, NY, NC, SHARD, COLS)
    return finish_fast(grads, small_grads, unsort(output), unsort(upstream.astype(jnp.bfloat16)), half)


def finish_fast(grads, small_grads, output, tokens_grad, half):
    layers = grads.shape[0]
    width = output.shape[1]
    vec = jnp.stack([s[0] for s in small_grads]).reshape(layers, 8, 16, 64).transpose(2, 0, 1, 3).reshape(1, 16, 1024)
    qv = jnp.stack([s[1] for s in small_grads]).reshape(layers, 2, 2, 8, 16, 4).transpose(2, 4, 0, 1, 3, 5).reshape(2, 16, 128)
    ups = jnp.stack([s[2] for s in small_grads]).reshape(layers, 2, 32, 16, 4).transpose(1, 3, 0, 2, 4).reshape(2, 16, 256)
    small = jnp.concatenate([jnp.broadcast_to(vec, (2, 16, 1024)), qv, ups, jnp.zeros((2, 16, 640), jnp.float32)], axis=2)
    small = small.reshape(NX, NZ, NY, NC, 16, 128).transpose(3, 0, 2, 1, 4, 5)
    summed, small_sum, out_rows, grad_rows = scatter_all(
        grads, small, output.reshape(2, HALF_PAD, width), tokens_grad.reshape(2, HALF_PAD, width))
    flat = small_sum.reshape(-1)
    return (
        out_rows[:, :half],
        grad_rows[:, :half].astype(jnp.float32),
        jnp.stack([summed[:, :, 0:512], summed[:, :, 512:1024], summed[:, :, 1024:1536]], axis=1),
        jnp.swapaxes(summed[:, :, 1536:2048], 1, 2),
        summed[:, :, 2048:4096],
        jnp.swapaxes(summed[:, :, 4096:], 1, 2),
        flat[:1024].reshape(layers, 8, 64),
        flat[1024:1152].reshape(layers, 2, 8, 4),
        flat[1152:1408].reshape(layers, 32, 4),
    )


def solution(mesh):
    placed = (
        P(None, ("dp", "mp"), None),
        P(None, "dp"),
        P(None, None, "dp", "mp"),
        P(None, "mp", "dp"),
        P(None, "dp", "mp"),
        P(None, "mp", "dp"),
        P(None, None, "dp"),
        P(None, None, "mp", "dp"),
        P(None, "mp", "dp"),
        P(None, ("dp", "mp"), None),
    )
    fast = dict(mesh.shape) == {"dp": NZ * NY * NC, "mp": NX}
    return jax.shard_map(
        on_device_fast if fast else on_device,
        mesh=mesh,
        in_specs=placed,
        out_specs=(
            P(None, ("dp", "mp"), None),
            P(None, ("dp", "mp"), None),
            P(None, None, "dp", "mp"),
            P(None, "mp", "dp"),
            P(None, "dp", "mp"),
            P(None, "mp", "dp"),
            P(None, None, "dp"),
            P(None, None, "mp", "dp"),
            P(None, "mp", "dp"),
        ),
        check_vma=False,
    )
```

```python
import functools
import math

import jax
import jax.numpy as jnp
from jax import lax
from jax.experimental import pallas as pl
from jax.experimental.pallas import tpu as pltpu
from jax.sharding import PartitionSpec as P

INV_ROOT_TWO = 0.7071067811865476
INV_ROOT_TAU = 0.3989422804014327


def layer_norm(values, gain, shift):
    centred = values - jnp.mean(values, axis=-1, keepdims=True)
    inverse = lax.rsqrt(jnp.mean(centred * centred, axis=-1, keepdims=True) + 1e-06)
    normed = centred * inverse
    return (normed * gain + shift, normed, inverse)


def norm_backward(upstream, normed, inverse, gain):
    scaled = upstream * gain
    inner = (
        scaled
        - jnp.mean(scaled, axis=-1, keepdims=True)
        - normed * jnp.mean(scaled * normed, axis=-1, keepdims=True)
    )
    return (inverse * inner, jnp.sum(upstream * normed, axis=0), jnp.sum(upstream, axis=0))


def contract_rows(left, right):
    return lax.dot_general(
        left, right, (((0,), (0,)), ((), ())), preferred_element_type=jnp.float32
    )


def against_rows(left, right):
    return lax.dot_general(
        left, right, (((1,), (1,)), ((), ())), preferred_element_type=jnp.float32
    )


def gather_normed(values):
    return lax.all_gather(values, "mp", axis=0, tiled=True)


def gather_upstream(values):
    return lax.all_gather(values, "mp", axis=0, tiled=True)


def branch_sum(term, count):
    return lax.psum_scatter(
        term(jnp.int32(0), count * lax.axis_size("mp")).astype(jnp.bfloat16),
        "mp",
        scatter_dimension=0,
        tiled=True,
    ).astype(jnp.float32)


def input_sum(term, count):
    return lax.psum_scatter(
        term(jnp.int32(0), count * lax.axis_size("mp")).astype(jnp.bfloat16),
        "mp",
        scatter_dimension=0,
        tiled=True,
    ).astype(jnp.float32)


def on_device(
    tokens,
    segments,
    qkv_weight,
    out_weight,
    up_weight,
    down_weight,
    vectors,
    qv_bias,
    up_bias,
    cotangent,
):
    layers = qkv_weight.shape[0]
    micro = tokens.shape[0]
    width = tokens.shape[2]
    head_dim = qv_bias.shape[3] * lax.axis_size("dp")
    scale = 1.0 / math.sqrt(head_dim)

    def attention_scores(query, keys, same_crop, heads):
        total_rows = query.shape[0]
        raw = (
            jnp.einsum(
                "qhd,khd->hqk",
                query.reshape(total_rows, heads, -1),
                keys.reshape(total_rows, heads, -1),
                preferred_element_type=jnp.float32,
            )
            * scale
        )
        return jnp.where(same_crop, raw, -1000000000.0)

    def forward_layer(resid, same_crop, whole):
        qkv_full, out_full, up_full, down_full, vector_half, qv_full, up_shift = whole
        vector_rows = vector_half.astype(jnp.float32)
        normed_in, first_normed, first_inverse = layer_norm(resid, vector_rows[0], vector_rows[1])
        first_all = gather_normed(normed_in.astype(jnp.bfloat16))
        total_rows = first_all.shape[0]
        heads = qv_full.shape[1]
        qv_flat = qv_full.astype(jnp.float32).reshape(2, -1)
        query = (
            jnp.dot(first_all, qkv_full[0], preferred_element_type=jnp.float32) + qv_flat[0]
        ).astype(jnp.bfloat16)
        keys = jnp.dot(first_all, qkv_full[1], preferred_element_type=jnp.float32).astype(
            jnp.bfloat16
        )
        values = (
            jnp.dot(first_all, qkv_full[2], preferred_element_type=jnp.float32) + qv_flat[1]
        ).astype(jnp.bfloat16)
        scores = attention_scores(query, keys, same_crop, heads)
        peak = jnp.max(scores, axis=-1, keepdims=True)
        powers = jnp.exp(scores - peak)
        totals = jnp.sum(powers, axis=-1, keepdims=True)
        probs = (powers / totals).astype(jnp.bfloat16)
        log_totals = peak + jnp.log(totals)
        attended = (
            jnp.einsum(
                "hqk,khd->qhd",
                probs,
                values.reshape(total_rows, heads, -1),
                preferred_element_type=jnp.float32,
            )
            .reshape(total_rows, -1)
            .astype(jnp.bfloat16)
        )

        def project_rows(start, size):
            return jnp.dot(attended, out_full, preferred_element_type=jnp.float32)

        projected = branch_sum(project_rows, resid.shape[0])
        middle = resid + vector_rows[3] * (projected + vector_rows[2])
        normed_mid, second_normed, second_inverse = layer_norm(
            middle, vector_rows[4], vector_rows[5]
        )
        second_all = gather_normed(normed_mid.astype(jnp.bfloat16))
        hidden_pre = jnp.dot(
            second_all, up_full, preferred_element_type=jnp.float32
        ) + up_shift.astype(jnp.float32).reshape(-1)
        hidden = (0.5 * hidden_pre * (1.0 + lax.erf(hidden_pre * INV_ROOT_TWO))).astype(
            jnp.bfloat16
        )

        def down_rows(start, size):
            return jnp.dot(hidden, down_full, preferred_element_type=jnp.float32)

        returned = branch_sum(down_rows, resid.shape[0])
        result = middle + vector_rows[7] * (returned + vector_rows[6])
        saved = (
            first_normed,
            first_inverse,
            first_all,
            query,
            keys,
            values,
            log_totals,
            attended,
            projected,
            second_normed,
            second_inverse,
            second_all,
            hidden_pre,
            hidden,
            returned,
        )
        return (result, saved)

    def backward_layer(upstream, same_crop, whole, saved):
        qkv_full, out_full, up_full, down_full, vector_half, qv_full, up_shift = whole
        (
            first_normed,
            first_inverse,
            first_all,
            query,
            keys,
            values,
            log_totals,
            attended,
            projected,
            second_normed,
            second_inverse,
            second_all,
            hidden_pre,
            hidden,
            returned,
        ) = saved
        vector_rows = vector_half.astype(jnp.float32)
        count = upstream.shape[0]
        total_rows = first_all.shape[0]
        heads = qv_full.shape[1]
        scaled_up = vector_rows[7] * upstream
        grad_shift_mlp = jnp.sum(scaled_up, axis=0)
        grad_scale_mlp = jnp.sum(upstream * (returned + vector_rows[6]), axis=0)
        returned_all = gather_upstream(scaled_up.astype(jnp.bfloat16))
        grad_down = contract_rows(hidden, returned_all)
        grad_hidden = against_rows(returned_all, down_full)
        normal_cdf = 0.5 * (1.0 + lax.erf(hidden_pre * INV_ROOT_TWO))
        normal_pdf = jnp.exp(-0.5 * hidden_pre * hidden_pre) * INV_ROOT_TAU
        grad_pre = (grad_hidden * (normal_cdf + hidden_pre * normal_pdf)).astype(jnp.bfloat16)
        grad_up_shift = jnp.sum(grad_pre.astype(jnp.float32), axis=0).reshape(-1, head_dim)
        grad_up = contract_rows(second_all, grad_pre)

        def up_rows(start, size):
            return against_rows(lax.dynamic_slice_in_dim(grad_pre, start, size, 0), up_full)

        grad_second = input_sum(up_rows, count)
        grad_mid_norm, grad_gain_two, grad_shift_two = norm_backward(
            grad_second, second_normed, second_inverse, vector_rows[4]
        )
        grad_middle = upstream + grad_mid_norm
        scaled_mid = vector_rows[3] * grad_middle
        grad_shift_attn = jnp.sum(scaled_mid, axis=0)
        grad_scale_attn = jnp.sum(grad_middle * (projected + vector_rows[2]), axis=0)
        projected_all = gather_upstream(scaled_mid.astype(jnp.bfloat16))
        grad_out = contract_rows(attended, projected_all)
        grad_attended = (
            against_rows(projected_all, out_full)
            .astype(jnp.bfloat16)
            .reshape(total_rows, heads, -1)
        )
        query_heads = query.reshape(total_rows, heads, -1)
        key_heads = keys.reshape(total_rows, heads, -1)
        value_heads = values.reshape(total_rows, heads, -1)
        scores = attention_scores(query, keys, same_crop, heads)
        probs = jnp.exp(scores - log_totals)
        grad_values = jnp.einsum(
            "hqk,qhd->khd",
            probs.astype(jnp.bfloat16),
            grad_attended,
            preferred_element_type=jnp.float32,
        )
        grad_probs = jnp.einsum(
            "qhd,khd->hqk", grad_attended, value_heads, preferred_element_type=jnp.float32
        )
        grad_scores = (
            probs * (grad_probs - jnp.sum(probs * grad_probs, axis=-1, keepdims=True))
        ).astype(jnp.bfloat16)
        grad_query = (
            jnp.einsum("hqk,khd->qhd", grad_scores, key_heads, preferred_element_type=jnp.float32)
            * scale
        )
        grad_keys = (
            jnp.einsum("hqk,qhd->khd", grad_scores, query_heads, preferred_element_type=jnp.float32)
            * scale
        )
        grad_project = (
            jnp.stack([grad_query, grad_keys, grad_values])
            .reshape(3, total_rows, -1)
            .astype(jnp.bfloat16)
        )
        grad_qv = jnp.stack(
            [
                jnp.sum(grad_project[0].astype(jnp.float32), axis=0),
                jnp.sum(grad_project[2].astype(jnp.float32), axis=0),
            ]
        ).reshape(2, heads, head_dim)
        grad_qkv = jnp.einsum(
            "rd,trc->tdc", first_all, grad_project, preferred_element_type=jnp.float32
        )

        def qkv_rows(start, size):
            return jnp.einsum(
                "trc,tdc->rd",
                lax.dynamic_slice_in_dim(grad_project, start, size, 1),
                qkv_full,
                preferred_element_type=jnp.float32,
            )

        grad_first = input_sum(qkv_rows, count)
        grad_in_norm, grad_gain_one, grad_shift_one = norm_backward(
            grad_first, first_normed, first_inverse, vector_rows[0]
        )
        grad_vectors = jnp.stack(
            [
                grad_gain_one,
                grad_shift_one,
                grad_shift_attn,
                grad_scale_attn,
                grad_gain_two,
                grad_shift_two,
                grad_shift_mlp,
                grad_scale_mlp,
            ]
        )
        parts = (grad_qkv, grad_out, grad_up, grad_down, grad_vectors, grad_qv, grad_up_shift)
        return (grad_middle + grad_in_norm, parts)

    shapes = [
        (3, width, qkv_weight.shape[3]),
        (out_weight.shape[1], width),
        (width, up_weight.shape[2]),
        (down_weight.shape[1], width),
        (8, width),
        (2, qv_bias.shape[2], head_dim),
        (up_bias.shape[1], head_dim),
    ]
    zeroed = tuple((jnp.zeros(shape, jnp.float32) for shape in shapes))
    start_sums = tuple((zeroed for layer in range(layers)))

    def one_micro(index, carry):
        sums, out_buffer, grad_buffer = carry
        resid = lax.dynamic_index_in_dim(tokens, index, 0, keepdims=False).astype(jnp.float32)
        crop_ids = lax.dynamic_index_in_dim(segments, index, 0, keepdims=False)
        same_crop = (crop_ids[:, None] == crop_ids[None, :])[None]
        wholes = []
        saves = []
        for layer in range(layers):
            whole = (
                lax.all_gather(qkv_weight[layer], "dp", axis=1, tiled=True),
                lax.all_gather(out_weight[layer], "dp", axis=1, tiled=True),
                lax.all_gather(up_weight[layer], "dp", axis=0, tiled=True),
                lax.all_gather(down_weight[layer], "dp", axis=1, tiled=True),
                lax.all_gather(vectors[layer], "dp", axis=1, tiled=True),
                lax.all_gather(qv_bias[layer], "dp", axis=2, tiled=True),
                lax.all_gather(up_bias[layer], "dp", axis=1, tiled=True),
            )
            resid, saved = forward_layer(resid, same_crop, whole)
            wholes.append(whole)
            saves.append(saved)
        out_buffer = lax.dynamic_update_index_in_dim(
            out_buffer, resid.astype(jnp.bfloat16), index, 0
        )
        upstream = lax.dynamic_index_in_dim(cotangent, index, 0, keepdims=False).astype(jnp.float32)
        new_sums = list(sums)
        for layer in reversed(range(layers)):
            whole = (
                lax.all_gather(qkv_weight[layer], "dp", axis=1, tiled=True),
                lax.all_gather(out_weight[layer], "dp", axis=1, tiled=True),
                lax.all_gather(up_weight[layer], "dp", axis=0, tiled=True),
                lax.all_gather(down_weight[layer], "dp", axis=1, tiled=True),
                lax.all_gather(vectors[layer], "dp", axis=1, tiled=True),
                lax.all_gather(qv_bias[layer], "dp", axis=2, tiled=True),
                lax.all_gather(up_bias[layer], "dp", axis=1, tiled=True),
            )
            upstream, parts = backward_layer(upstream, same_crop, whole, saves[layer])
            new_sums[layer] = tuple((total + piece for total, piece in zip(sums[layer], parts)))
        grad_buffer = lax.dynamic_update_index_in_dim(grad_buffer, upstream, index, 0)
        return (tuple(new_sums), out_buffer, grad_buffer)

    start = (
        start_sums,
        jnp.zeros(tokens.shape, jnp.bfloat16),
        jnp.zeros(tokens.shape, jnp.float32),
    )
    sums, output, tokens_grad = lax.fori_loop(0, micro, one_micro, start)
    reduced = []
    for layer in range(layers):
        totals = sums[layer]
        totals = (
            lax.psum_scatter(
                totals[0].astype(jnp.bfloat16), "dp", scatter_dimension=1, tiled=True
            ).astype(jnp.float32),
            lax.psum_scatter(
                totals[1].astype(jnp.bfloat16), "dp", scatter_dimension=1, tiled=True
            ).astype(jnp.float32),
            lax.psum_scatter(
                totals[2].astype(jnp.bfloat16), "dp", scatter_dimension=0, tiled=True
            ).astype(jnp.float32),
            lax.psum_scatter(
                totals[3].astype(jnp.bfloat16), "dp", scatter_dimension=1, tiled=True
            ).astype(jnp.float32),
            lax.psum_scatter(
                totals[4].astype(jnp.bfloat16), "dp", scatter_dimension=1, tiled=True
            ).astype(jnp.float32),
            lax.psum_scatter(
                totals[5].astype(jnp.bfloat16), "dp", scatter_dimension=2, tiled=True
            ).astype(jnp.float32),
            lax.psum_scatter(
                totals[6].astype(jnp.bfloat16), "dp", scatter_dimension=1, tiled=True
            ).astype(jnp.float32),
        )
        reduced.append(totals)
    stacked = [
        jnp.stack([reduced[layer][member] for layer in range(layers)]) for member in range(7)
    ]
    vector_total = lax.psum(stacked[4], "mp")
    return (
        output,
        tokens_grad,
        stacked[0],
        stacked[1],
        stacked[2],
        stacked[3],
        vector_total,
        stacked[5],
        stacked[6],
    )


MESH = pl.DeviceIdType.MESH
NZ, NY, NC, NX = 4, 2, 2, 2
SHARD = 64
COLS = 6144
CHUNK = 1024
PER_LAYER = COLS // CHUNK
ROUTES = (("zxy", 0, 16, 0, 1024), ("yzx", 16, 48, 0, 512), ("xzy", 16, 48, 512, 512))
LAG = 2


class Place:
    def __init__(self):
        dp = lax.axis_index("dp")
        self.x = lax.axis_index("mp")
        self.z = dp // 4
        self.y = lax.rem(dp // 2, 2)
        self.c = lax.rem(dp, 2)

    def device(self, x=None, z=None, y=None, c=None):
        x = self.x if x is None else x
        z = self.z if z is None else z
        y = self.y if y is None else y
        c = self.c if c is None else c
        return (z * 4 + y * 2 + c, x)

    def other(self, axis):
        if axis == "x":
            return self.device(x=1 - self.x)
        if axis == "y":
            return self.device(y=1 - self.y)
        return self.device(c=1 - self.c)

    def along(self, k):
        return lax.rem(self.z + k, NZ)


def greet(place):
    barrier = pltpu.get_barrier_semaphore()
    for axis in "cxy":
        pl.semaphore_signal(barrier, inc=1, device_id=place.other(axis), device_id_type=MESH)
    for k in (1, 2, 3):
        pl.semaphore_signal(
            barrier, inc=1, device_id=place.device(z=place.along(k)), device_id_type=MESH
        )
    pl.semaphore_wait(barrier, 6)


def block(place, filled, z=None):
    return (
        slice(None) if "x" in filled else place.x,
        slice(None) if "z" in filled else (place.z if z is None else z),
        slice(None) if "y" in filled else place.y,
        place.c,
    )


class Spread:
    def __init__(self, place, axis, source, target, send, recv, base):
        self.place, self.axis = place, axis
        self.source, self.target = source, target
        self.send, self.recv, self.base = send, recv, base

    def single(self):
        return pltpu.make_async_remote_copy(
            src_ref=self.source, dst_ref=self.target(None),
            send_sem=self.send(self.base), recv_sem=self.recv(self.base),
            device_id=self.place.other(self.axis), device_id_type=MESH)

    def direct(self, k):
        place = self.place
        return pltpu.make_async_remote_copy(
            src_ref=self.source, dst_ref=self.target(None),
            send_sem=self.send(self.base + k), recv_sem=self.recv(self.base + place.z),
            device_id=place.device(z=place.along(k)), device_id_type=MESH)

    def arrival(self, z):
        place = self.place
        return pltpu.make_async_remote_copy(
            src_ref=self.source, dst_ref=self.target(z),
            send_sem=self.send(self.base), recv_sem=self.recv(self.base + z),
            device_id=place.device(z=z), device_id_type=MESH)

    def passed(self):
        place = self.place
        origin = jnp.where(place.z == 2, 0, 3)
        return origin, pltpu.make_async_remote_copy(
            src_ref=self.target(origin), dst_ref=self.target(origin),
            send_sem=self.send(self.base), recv_sem=self.recv(self.base + origin),
            device_id=place.device(z=3 - origin), device_id_type=MESH)

    def start(self):
        if self.axis != "z":
            self.single().start()
            return
        for k in (1, 2, 3):
            if k == 2:
                self.direct(k).start()
            else:
                @pl.when(self.place.z != (3 if k == 1 else 0))
                def _():
                    self.direct(k).start()

    def relay(self):
        if self.axis != "z":
            return

        @pl.when((self.place.z == 1) | (self.place.z == 2))
        def _():
            origin, copy = self.passed()
            self.arrival(origin).wait_recv()
            copy.start()

    def arrive(self):
        if self.axis != "z":
            self.single().wait_recv()
            return
        z = self.place.z
        inner = (z == 1) | (z == 2)
        far = jnp.where(z == 2, 0, 3)
        for k in (1, 2, 3):
            origin = lax.rem(z + k, NZ)

            @pl.when(jnp.logical_not(inner & (origin == far)))
            def _():
                self.arrival(origin).wait_recv()

    def finish(self):
        if self.axis != "z":
            self.single().wait_send()
            return
        for k in (1, 2, 3):
            if k == 2:
                self.direct(k).wait_send()
            else:
                @pl.when(self.place.z != (3 if k == 1 else 0))
                def _():
                    self.direct(k).wait_send()

        @pl.when((self.place.z == 1) | (self.place.z == 2))
        def _():
            self.passed()[1].wait_send()


class Gather:
    def __init__(self, place, chunks, shard, whole, send, recv, sib, local):
        self.place, self.chunks = place, chunks
        self.shard, self.whole = shard, whole
        self.send, self.recv, self.sib, self.local = send, recv, sib, local

    def spot(self, step):
        return step // PER_LAYER, lax.rem(step, PER_LAYER) * CHUNK

    def spread(self, step, route, phase):
        order, row, rows, col, cols = ROUTES[route]
        layer, first = self.spot(step)
        area = (pl.ds(row, rows), pl.ds(pl.multiple_of(first + col, 128), cols))
        filled = order[:phase]
        target = lambda z: self.whole.at[(layer,) + block(self.place, filled, z) + area]
        source = self.shard.at[(layer,) + area] if phase == 0 else target(None)
        axis = order[phase]
        base = {"z": 0, "y": 4, "x": 5}[axis]
        return Spread(
            self.place, axis, source, target,
            lambda slot: self.send.at[step, route, slot], lambda slot: self.recv.at[step, route, slot], base)

    def own(self, step):
        layer, first = self.spot(step)
        cols = pl.ds(pl.multiple_of(first, CHUNK), CHUNK)
        return pltpu.make_async_copy(
            self.shard.at[layer, :, cols],
            self.whole.at[(layer,) + block(self.place, "") + (slice(None), cols)], self.local.at[step])

    def sibling(self, step):
        layer, first = self.spot(step)
        cols = pl.ds(pl.multiple_of(first, CHUNK), CHUNK)
        part = self.whole.at[(layer,) + block(self.place, "xyz") + (slice(None), cols)]
        return pltpu.make_async_remote_copy(
            src_ref=part, dst_ref=part, send_sem=self.sib.at[0, step], recv_sem=self.sib.at[1, step],
            device_id=self.place.other("c"), device_id_type=MESH)

    def phase(self, step, number):
        every = range(len(ROUTES))
        if number == 0:
            self.own(step).start()
        if number == 1:
            self.own(step).wait()
        for route in every:
            if 1 <= number <= 3:
                self.spread(step, route, number - 1).arrive()
            if number <= 2:
                self.spread(step, route, number).start()
        if number == 3:
            self.sibling(step).start()
        if number == 4:
            self.sibling(step).wait()
            for route in every:
                for phase in range(3):
                    self.spread(step, route, phase).finish()

    def tick(self, step):
        for number in range(5):
            at = step - LAG * number

            @pl.when((at >= 0) & (at < self.chunks))
            def _():
                self.phase(at, number)
            if number < 3:
                early = step - LAG * number - 1

                @pl.when((early >= 0) & (early < self.chunks))
                def _():
                    for route in range(len(ROUTES)):
                        self.spread(early, route, number).relay()

    @property
    def ticks(self):
        return self.chunks + 4 * LAG


def ag_kernel(chunks, shard, small, tokens, cotangent, whole, small_all, mine, mine_grad, send, recv, sib, local, odd):
    place = Place()
    greet(place)
    gather = Gather(place, chunks, shard, whole, send, recv, sib, local)

    def halves(n, source, target):
        return (
            pltpu.make_async_remote_copy(
                src_ref=source.at[1 - place.x], dst_ref=target.at[place.x],
                send_sem=odd.at[4 * n], recv_sem=odd.at[4 * n + 1],
                device_id=place.other("x"), device_id_type=MESH),
            pltpu.make_async_copy(source.at[place.x], target.at[place.x], odd.at[4 * n + 2]),
        )

    order = "zyx"

    def small_spread(phase):
        target = lambda z: small_all.at[block(place, order[:phase], z)]
        base = {"z": 0, "y": 4, "x": 5}[order[phase]]
        return Spread(
            place, order[phase], small if phase == 0 else target(None), target,
            lambda slot: odd.at[8 + slot], lambda slot: odd.at[16 + slot], base)

    part = small_all.at[block(place, "xyz")]
    small_sibling = pltpu.make_async_remote_copy(
        src_ref=part, dst_ref=part, send_sem=odd.at[24], recv_sem=odd.at[25],
        device_id=place.other("c"), device_id_type=MESH)
    small_own = pltpu.make_async_copy(small, small_all.at[block(place, "")], odd.at[26])
    token_copies = halves(0, tokens, mine)
    grad_copies = halves(1, cotangent, mine_grad)
    for copy in token_copies:
        copy.start()
    small_own.start()
    small_spread(0).start()

    def tick(step, carry):
        @pl.when(step == 1)
        def _():
            small_spread(0).relay()
            small_own.wait()

        for phase in (1, 2):
            @pl.when(step == 1 + phase)
            def _():
                small_spread(phase - 1).arrive()
                small_spread(phase).start()

        @pl.when(step == 4)
        def _():
            small_spread(2).arrive()
            small_sibling.start()
        gather.tick(step)

        @pl.when(step == chunks // 2)
        def _():
            for copy in grad_copies:
                copy.start()
        return carry

    lax.fori_loop(0, gather.ticks, tick, 0)
    small_sibling.wait()
    for phase in range(3):
        small_spread(phase).finish()
    for copy in token_copies + grad_copies:
        copy.wait()


def gather_all(shard, small, tokens, cotangent):
    layers = shard.shape[0]
    chunks = layers * PER_LAYER
    half = tokens.shape
    any_spec = pl.BlockSpec(memory_space=pl.ANY)
    return pl.pallas_call(
        functools.partial(ag_kernel, chunks),
        out_shape=(
            jax.ShapeDtypeStruct((layers, NX, NZ, NY, NC, SHARD, COLS), jnp.bfloat16),
            jax.ShapeDtypeStruct((NX, NZ, NY, NC) + small.shape, small.dtype),
            jax.ShapeDtypeStruct(half, jnp.bfloat16),
            jax.ShapeDtypeStruct(half, jnp.bfloat16),
        ),
        in_specs=[pl.BlockSpec(memory_space=pltpu.VMEM)] * 4,
        out_specs=(any_spec,) * 4,
        scratch_shapes=[
            pltpu.SemaphoreType.DMA((chunks, len(ROUTES), 6)),
            pltpu.SemaphoreType.DMA((chunks, len(ROUTES), 6)),
            pltpu.SemaphoreType.DMA((2, chunks)),
            pltpu.SemaphoreType.DMA((chunks,)),
            pltpu.SemaphoreType.DMA((32,)),
        ],
        compiler_params=pltpu.CompilerParams(collective_id=1, has_side_effects=True, vmem_limit_bytes=32 * 1024 * 1024),
        name="gather_all",
    )(shard, small, tokens, cotangent)
SLOTS = 5


class Scatter:
    def __init__(self, place, chunks, grads, summed, acc, near, first, second, third, send, recv, local, free):
        self.place, self.chunks = place, chunks
        self.grads, self.summed = grads, summed
        self.acc, self.near = acc, near
        self.landing = (first, second, third)
        self.send, self.recv, self.local, self.free = send, recv, local, free

    def spot(self, step):
        chunk = self.chunks - 1 - step
        return chunk // PER_LAYER, pl.multiple_of(lax.rem(chunk, PER_LAYER) * CHUNK, CHUNK)

    def slot(self, step):
        return lax.rem(step, SLOTS)

    def core_copies(self, step):
        layer, first = self.spot(step)
        cols = pl.ds(first, CHUNK)
        slot = self.slot(step)
        return (
            pltpu.make_async_remote_copy(
                src_ref=self.grads.at[layer, :, :, :, 1 - self.place.c, :, cols], dst_ref=self.acc.at[slot],
                send_sem=self.send.at[step, len(ROUTES), 0], recv_sem=self.recv.at[step, len(ROUTES), 0],
                device_id=self.place.other("c"), device_id_type=MESH),
            pltpu.make_async_copy(
                self.grads.at[layer, :, :, :, self.place.c, :, cols], self.near, self.local.at[step]),
        )

    def core_add(self, step):
        slot = self.slot(step)

        def one(n, carry):
            x, z, y = n // 8, lax.rem(n // 2, 4), lax.rem(n, 2)
            self.acc[slot, x, z, y] = self.acc[slot, x, z, y] + self.near[x, z, y]
            return carry

        lax.fori_loop(0, NX * NZ * NY, one, 0)

    def area(self, route):
        _, row, rows, col, cols = ROUTES[route]
        return (pl.ds(row, rows), pl.ds(col, cols))

    def index(self, route, phase, over):
        order = ROUTES[route][0]
        left = order[:2 - phase]
        place = self.place
        picked = []
        for axis, own in (("x", place.x), ("z", place.z), ("y", place.y)):
            picked.append(over[axis] if axis in over else (slice(None) if axis in left else own))
        return tuple(picked)

    def copy(self, step, route, phase, over, device, source_slot, sem):
        slot = self.slot(step)
        axis = ROUTES[route][0][2 - phase]
        land = self.landing[phase][route].at[slot]
        if axis == "z":
            land = land.at[source_slot]
        base = {"z": 0, "y": 4, "x": 5}[axis]
        return pltpu.make_async_remote_copy(
            src_ref=self.acc.at[(slot,) + self.index(route, phase, over) + self.area(route)], dst_ref=land,
            send_sem=self.send.at[step, route, base + sem], recv_sem=self.recv.at[step, route, base + source_slot],
            device_id=device, device_id_type=MESH)

    def single(self, step, route, phase):
        axis = ROUTES[route][0][2 - phase]
        own = self.place.x if axis == "x" else self.place.y
        return self.copy(step, route, phase, {axis: 1 - own}, self.place.other(axis), 0, 0)

    def along(self, step, route, phase, k):
        place = self.place
        z = place.along(k)
        far = (place.z + z == 3) & ((place.z == 0) | (place.z == 3))
        via = jnp.where(far, jnp.where(place.z == 0, 1, 2), z)
        return self.copy(
            step, route, phase, {"z": z}, place.device(z=via), jnp.where(far, via, place.z), k)

    def arrival(self, step, route, phase, z):
        return self.copy(step, route, phase, {"z": self.place.z}, self.place.device(z=lax.rem(z + 1, NZ)), z, 1)

    def start(self, step, route, phase):
        if ROUTES[route][0][2 - phase] != "z":
            self.single(step, route, phase).start()
            return
        z = self.place.z
        for k in (1, 2, 3):
            if k == 2:
                @pl.when((z == 0) | (z == 3))
                def _():
                    self.along(step, route, phase, k).start()
            else:
                self.along(step, route, phase, k).start()

    def relay(self, step, route, phase):
        if ROUTES[route][0][2 - phase] != "z":
            return
        z = self.place.z
        slot = self.slot(step)

        @pl.when((z == 1) | (z == 2))
        def _():
            self.arrival(step, route, phase, z).wait_recv()
            far = lax.rem(z + 2, NZ)
            at = (slot,) + self.index(route, phase, {"z": far}) + self.area(route)
            self.acc[at] = self.acc[at] + self.landing[phase][route][slot, z]
            self.along(step, route, phase, 2).start()

    def arrive(self, step, route, phase):
        slot = self.slot(step)
        area = self.area(route)
        axis = ROUTES[route][0][2 - phase]
        land = self.landing[phase][route]
        if axis != "z":
            self.single(step, route, phase).wait_recv()
            at = self.index(route, phase, {axis: self.place.x if axis == "x" else self.place.y})
            lead = [n for n, entry in enumerate(at) if isinstance(entry, slice)]
            extents = [(NX, NZ, NY)[n] for n in lead]
            total = 1
            for extent in extents:
                total *= extent

            def one(n, carry):
                part = []
                for extent in reversed(extents):
                    part.append(lax.rem(n, extent))
                    n = n // extent
                part.reverse()
                full = list(at)
                for position, value in zip(lead, part):
                    full[position] = value
                self.acc[(slot,) + tuple(full) + area] = (
                    self.acc[(slot,) + tuple(full) + area] + land[(slot,) + tuple(part)])
                return carry

            if total == 1:
                one(0, 0)
            else:
                lax.fori_loop(0, total, one, 0)
            return
        z = self.place.z
        ends = (z == 0) | (z == 3)
        at = (slot,) + self.index(route, phase, {"z": z}) + area
        for k in (1, 2, 3):
            origin = lax.rem(z + k, NZ)

            @pl.when(jnp.logical_not(ends & (z + origin == 3)))
            def _():
                self.arrival(step, route, phase, origin).wait_recv()
                self.acc[at] = self.acc[at] + land[slot, origin]

    def finish(self, step, route, phase):
        if ROUTES[route][0][2 - phase] != "z":
            self.single(step, route, phase).wait_send()
            return
        for k in (1, 2, 3):
            self.along(step, route, phase, k).wait_send()

    def others(self):
        place = self.place
        pairs = [(place.other(axis), n, n) for n, axis in enumerate("cxy")]
        for k in (1, 2, 3):
            z = place.along(k)
            pairs.append((place.device(z=z), 3 + place.z, 3 + z))
        return pairs

    def phase(self, step, number):
        every = range(len(ROUTES))
        if number == 0:
            @pl.when(step >= SLOTS)
            def _():
                for _, _, mine in self.others():
                    pl.semaphore_wait(self.free.at[mine], 1)
            for copy in self.core_copies(step):
                copy.start()
            return
        if number == 1:
            remote, own = self.core_copies(step)
            own.wait()
            remote.wait_recv()
            self.core_add(step)
        for route in every:
            if number >= 2:
                self.arrive(step, route, number - 2)
            if number <= 3:
                self.start(step, route, number - 1)
        if number == 4:
            slot = self.slot(step)
            layer, first = self.spot(step)
            place = self.place
            self.summed[layer, :, pl.ds(first, CHUNK)] = self.acc[slot, place.x, place.z, place.y]
            self.core_copies(step)[0].wait_send()
            for route in every:
                for phase in range(3):
                    self.finish(step, route, phase)

            @pl.when(step + SLOTS < self.chunks)
            def _():
                for device, there, _ in self.others():
                    pl.semaphore_signal(self.free.at[there], inc=1, device_id=device, device_id_type=MESH)

    def tick(self, step):
        for number in (4, 3, 2, 1, 0):
            at = step - number

            @pl.when((at >= 0) & (at < self.chunks))
            def _():
                self.phase(at, number)
        for number in (1, 2, 3):
            at = step - number

            @pl.when((at >= 0) & (at < self.chunks))
            def _():
                for route in range(len(ROUTES)):
                    self.relay(at, route, number - 1)

    @property
    def ticks(self):
        return self.chunks + 4


def landing_shapes():
    shapes = []
    for phase in range(3):
        for order, row, rows, col, cols in ROUTES:
            left = order[:2 - phase]
            axis = order[2 - phase]
            lead = tuple(extent for name, extent in (("x", NX), ("z", NZ), ("y", NY)) if name in left)
            if axis == "z":
                lead = (NZ,) + lead
            shapes.append(pltpu.VMEM((SLOTS,) + lead + (rows, cols), jnp.bfloat16))
    return shapes


WINDOWS = ((0, 208), (208, 208), (416, 224))
PADDED = 640
HALF_PAD = 320
PAIRS = 8
STEP = 32


def swap_halves(place, source, target, odd, n):
    return (
        pltpu.make_async_remote_copy(
            src_ref=source.at[1 - place.x], dst_ref=target.at[place.x],
            send_sem=odd.at[n], recv_sem=odd.at[n + 1],
            device_id=place.other("x"), device_id_type=MESH),
        pltpu.make_async_copy(source.at[place.x], target.at[place.x], odd.at[n + 2]),
    )


class Total:
    def __init__(self, place, value, landing, send, recv, base):
        self.place, self.value, self.landing = place, value, landing
        self.send, self.recv, self.base = send, recv, base

    def copies(self, number):
        place = self.place
        if number < 3:
            slots, devices = [number], [place.other("cxy"[number])]
        else:
            slots, devices = [3, 4, 5], [place.device(z=place.along(k)) for k in (1, 2, 3)]
        return [
            pltpu.make_async_remote_copy(
                src_ref=self.value, dst_ref=self.landing.at[slot],
                send_sem=self.send.at[self.base + slot], recv_sem=self.recv.at[self.base + slot],
                device_id=device, device_id_type=MESH)
            for slot, device in zip(slots, devices)
        ]

    def start(self, number):
        for copy in self.copies(number):
            copy.start()

    def add(self, number):
        for copy in self.copies(number):
            copy.wait()
        for slot in ([number] if number < 3 else [3, 4, 5]):
            self.value[...] = self.value[...] + self.landing[slot]


def dot_nn(left, right):
    return jnp.dot(left, right, preferred_element_type=jnp.float32)


def dot_nt(left, right):
    return lax.dot_general(left, right, (((1,), (1,)), ((), ())), preferred_element_type=jnp.float32)


def dot_tn(left, right):
    return lax.dot_general(left, right, (((0,), (0,)), ((), ())), preferred_element_type=jnp.float32)


def both_heads(rows):
    left = lax.broadcasted_iota(jnp.int32, rows.shape, 1) < 64
    zero = jnp.zeros_like(rows)
    return jnp.concatenate([jnp.where(left, rows, zero), jnp.where(left, zero, rows)], axis=0)


def one_head_each(rows):
    n = rows.shape[0] // 2
    left = lax.broadcasted_iota(jnp.int32, (n, rows.shape[1]), 1) < 64
    return jnp.where(left, rows[:n], rows[n:])


def window_probs(query, keys, other, n):
    raw = dot_nt(both_heads(query), keys) * 0.125
    apart = jnp.concatenate([other[:n, :n], other[:n, :n]], axis=0) > 0.5
    raw = jnp.where(apart, -1e9, raw)
    powers = jnp.exp(raw - jnp.max(raw, axis=1, keepdims=True))
    return powers * (1.0 / jnp.sum(powers, axis=1, keepdims=True))


def row_loop(body, size=STEP):
    @pl.loop(0, PADDED // size)
    def _(n):
        body(pl.ds(pl.multiple_of(n * size, size), size))


def normed_rows(values):
    centred = values - jnp.mean(values, axis=1, keepdims=True)
    inverse = lax.rsqrt(jnp.mean(centred * centred, axis=1, keepdims=True) + 1e-06)
    return centred * inverse, inverse


class Weights:
    def __init__(self, whole, held, sem):
        self.whole, self.held, self.sem = whole, held, sem

    def copy(self, layer, chunk, x):
        return pltpu.make_async_copy(
            self.whole.at[layer, x, :, :, :, :, pl.ds(chunk * CHUNK, CHUNK)], self.held.at[x], self.sem.at[x])

    def start(self, layer, chunk):
        for x in range(NX):
            self.copy(layer, chunk, x).start()

    def wait(self, layer, chunk, x):
        self.copy(layer, chunk, x).wait()

    def get(self, x, first=0, count=CHUNK):
        return self.held[x, :, :, :, :, first:first + count].reshape(NZ * NY * NC * SHARD, count)


def fwd_kernel(
    layers, shard, small, tokens, cotangent, to_place, other,
    whole, vec_out, grad_out, resid_out, middle_out, result_out, acts_out, hidden_out, slope_out,
    mine, mine_grad, vec, small_land, resid, normed, acts, hidden, slope, total, held,
    send, recv, sib, local, odd, small_send, small_recv, wsem, save,
):
    chunks = layers * PER_LAYER
    place = Place()
    greet(place)
    gather = Gather(place, chunks, shard, whole, send, recv, sib, local)
    weights = Weights(whole, held, wsem)
    token_copies = swap_halves(place, tokens, mine, odd, 0)
    grad_copies = swap_halves(place, cotangent, mine_grad, odd, 3)
    small_total = Total(place, vec, small_land, small_send, small_recv, 0)

    vec[...] = small[...].astype(jnp.float32)
    small_total.start(0)
    for copy in token_copies:
        copy.start()
    gather.tick(0)
    small_total.add(0)
    small_total.start(1)
    gather.tick(1)
    for number in (1, 2):
        small_total.add(number)
        small_total.start(number + 1)
    small_total.add(3)
    for copy in token_copies:
        copy.wait()
    for copy in grad_copies:
        copy.start()
    vec_copy = pltpu.make_async_copy(vec, vec_out, save.at[12])
    vec_copy.start()
    resid[...] = dot_nn(to_place[...], mine[...].reshape(PADDED, -1))

    def early(step, carry):
        gather.tick(step)
        return carry

    lax.fori_loop(2, 4 * LAG, early, 0)
    for copy in grad_copies:
        copy.wait()
    slope[0] = dot_nn(to_place[...], mine_grad[...].reshape(PADDED, -1)).astype(jnp.bfloat16)
    grad_copy = pltpu.make_async_copy(slope.at[0], grad_out, save.at[13])
    grad_copy.start()
    grad_copy.wait()

    def one_layer(layer, carry):
        base = layer * 16
        row = lambda n: vec[pl.ds(base + n, 1), :]

        def norm_into(gain, shift):
            def body(rows):
                values, _ = normed_rows(resid[rows, :])
                normed[rows, :] = (values * row(gain) + row(shift)).astype(jnp.bfloat16)
            row_loop(body)

        norm_into(0, 1)
        resid_copy = pltpu.make_async_copy(resid, resid_out.at[layer], save.at[0])
        resid_copy.start()
        gather.tick(layer * PER_LAYER + 4 * LAG)
        weights.start(layer, 0)
        for x in range(NX):
            half = slice(x * 512, x * 512 + 512)
            weights.wait(layer, 0, x)
            both = dot_nn(normed[...], weights.get(x))
            acts[0, :, half] = (both[:, :512] + row(8)[:, half]).astype(jnp.bfloat16)
            acts[1, :, half] = both[:, 512:].astype(jnp.bfloat16)
        gather.tick(layer * PER_LAYER + 4 * LAG + 1)
        weights.start(layer, 1)
        for x in range(NX):
            half = slice(x * 512, x * 512 + 512)
            weights.wait(layer, 1, x)
            acts[2, :, half] = (dot_nn(normed[...], weights.get(x, 0, 512)) + row(9)[:, half]).astype(jnp.bfloat16)

        @pl.loop(0, PAIRS)
        def _(pair):
            lanes = pl.ds(pl.multiple_of(pair * 128, 128), 128)
            for w, (first, n) in enumerate(WINDOWS):
                rows = pl.ds(first, n)
                probs = window_probs(acts[0, rows, lanes], acts[1, rows, lanes], other[w], n)
                sums = dot_nn(probs.astype(jnp.bfloat16), acts[2, rows, lanes])
                acts[3, rows, lanes] = one_head_each(sums).astype(jnp.bfloat16)

        acts_copy = pltpu.make_async_copy(acts, acts_out.at[layer], save.at[1])
        acts_copy.start()
        total[...] = dot_nt(acts[3, :, :512], weights.get(0, 512, 512)) + dot_nt(acts[3, :, 512:], weights.get(1, 512, 512))
        resid_copy.wait()

        def to_middle(rows):
            resid[rows, :] = resid[rows, :] + row(3) * (total[rows, :] + row(2))
        row_loop(to_middle)
        middle_copy = pltpu.make_async_copy(resid, middle_out.at[layer], save.at[2])
        middle_copy.start()
        norm_into(4, 5)
        for part in range(2):
            gather.tick(layer * PER_LAYER + 4 * LAG + 2 + part)
            weights.start(layer, 2 + part)
            for x in range(NX):
                unit = x * 2 + part
                weights.wait(layer, 2 + part, x)
                total[...] = dot_nn(normed[...], weights.get(x)) + row(10 + unit)
                slope_copy = pltpu.make_async_copy(slope.at[x], slope_out.at[layer, unit], save.at[4 + x])
                if part:
                    pltpu.make_async_copy(slope.at[x], slope_out.at[layer, unit - 1], save.at[4 + x]).wait()

                def activate(rows):
                    pre = total[rows, :]
                    cdf = 0.5 * (1.0 + lax.erf(pre * INV_ROOT_TWO))
                    pdf = jnp.exp(-0.5 * pre * pre) * INV_ROOT_TAU
                    hidden[unit, rows, :] = (pre * cdf).astype(jnp.bfloat16)
                    slope[x, rows, :] = (cdf + pre * pdf).astype(jnp.bfloat16)
                row_loop(activate, 16)
                slope_copy.start()
        hidden_copy = pltpu.make_async_copy(hidden, hidden_out.at[layer], save.at[3])
        hidden_copy.start()
        for part in range(2):
            gather.tick(layer * PER_LAYER + 4 * LAG + 4 + part)
            weights.start(layer, 4 + part)
            for x in range(NX):
                weights.wait(layer, 4 + part, x)
                term = dot_nt(hidden[x * 2 + part], weights.get(x))
                if part == 0 and x == 0:
                    total[...] = term
                else:
                    total[...] = total[...] + term
        middle_copy.wait()

        def to_result(rows):
            resid[rows, :] = resid[rows, :] + row(7) * (total[rows, :] + row(6))
        row_loop(to_result)
        acts_copy.wait()
        hidden_copy.wait()
        for x in range(NX):
            pltpu.make_async_copy(slope.at[x], slope_out.at[layer, x * 2 + 1], save.at[4 + x]).wait()
        return carry

    lax.fori_loop(0, layers, one_layer, 0)
    result_copy = pltpu.make_async_copy(resid, result_out, save.at[0])
    result_copy.start()
    result_copy.wait()
    vec_copy.wait()


def forward_all(shard, small, tokens, cotangent, to_place, other):
    layers = shard.shape[0]
    width = tokens.shape[2]
    chunks = layers * PER_LAYER
    any_spec = pl.BlockSpec(memory_space=pl.ANY)
    full = (PADDED, width)
    bf16, f32 = jnp.bfloat16, jnp.float32
    return pl.pallas_call(
        functools.partial(fwd_kernel, layers),
        out_shape=(
            jax.ShapeDtypeStruct((layers, NX, NZ, NY, NC, SHARD, COLS), bf16),
            jax.ShapeDtypeStruct(small.shape, f32),
            jax.ShapeDtypeStruct(full, bf16),
            jax.ShapeDtypeStruct((layers,) + full, f32),
            jax.ShapeDtypeStruct((layers,) + full, f32),
            jax.ShapeDtypeStruct(full, f32),
            jax.ShapeDtypeStruct((layers, 4) + full, bf16),
            jax.ShapeDtypeStruct((layers, 4) + full, bf16),
            jax.ShapeDtypeStruct((layers, 4) + full, bf16),
        ),
        in_specs=[pl.BlockSpec(memory_space=pltpu.VMEM)] * 6,
        out_specs=(any_spec,) * 9,
        scratch_shapes=[
            pltpu.VMEM(tokens.shape, bf16),
            pltpu.VMEM(tokens.shape, bf16),
            pltpu.VMEM(small.shape, f32),
            pltpu.VMEM((6,) + small.shape, f32),
            pltpu.VMEM(full, f32),
            pltpu.VMEM(full, bf16),
            pltpu.VMEM((4,) + full, bf16),
            pltpu.VMEM((4,) + full, bf16),
            pltpu.VMEM((2,) + full, bf16),
            pltpu.VMEM(full, f32),
            pltpu.VMEM((NX, NZ, NY, NC, SHARD, CHUNK), bf16),
            pltpu.SemaphoreType.DMA((chunks, len(ROUTES), 6)),
            pltpu.SemaphoreType.DMA((chunks, len(ROUTES), 6)),
            pltpu.SemaphoreType.DMA((2, chunks)),
            pltpu.SemaphoreType.DMA((chunks,)),
            pltpu.SemaphoreType.DMA((6,)),
            pltpu.SemaphoreType.DMA((6,)),
            pltpu.SemaphoreType.DMA((6,)),
            pltpu.SemaphoreType.DMA((2,)),
            pltpu.SemaphoreType.DMA((14,)),
        ],
        compiler_params=pltpu.CompilerParams(
            collective_id=1, has_side_effects=True, vmem_limit_bytes=60 * 1024 * 1024),
        name="forward_all",
    )(shard, small, tokens, cotangent, to_place, other)


def bwd_kernel(
    layers, whole, vec, grad_in, resid_in, middle_in, result, acts_in, hidden_in, slope_in, to_place, other,
    summed, small_sum, out_rows, grad_rows, grads, *scratch,
):
    n = len(ROUTES)
    acc, near = scratch[:2]
    lands = scratch[2:2 + 3 * n]
    (upstream, dy, normed, mid, total, pool, big, held, staged, rows_out, gsum, small_land,
     send, recv, local, free, odd, small_send, small_recv, wsem, load, stage) = scratch[2 + 3 * n:]
    chunks = layers * PER_LAYER
    place = Place()
    greet(place)
    scatter = Scatter(place, chunks, grads, summed, acc, near, lands[:n], lands[n:2 * n], lands[2 * n:], send, recv, local, free)
    weights = Weights(whole, held, wsem)
    out_copies = swap_halves(place, rows_out, out_rows, odd, 0)
    grad_copies = swap_halves(place, rows_out, grad_rows, odd, 3)
    small_total = Total(place, small_sum, small_land, small_send, small_recv, 0)

    def fetch(source, target, slot):
        return pltpu.make_async_copy(source, target, load.at[slot])

    def add_rows(kind, values):
        gsum[kind] = gsum[kind] + jnp.sum(values.reshape(-1, 8, values.shape[1]), axis=0)

    small_sum[...] = jnp.zeros_like(small_sum)
    copies = [fetch(result, total, 0), fetch(grad_in, dy, 1)]
    for copy in copies:
        copy.start()
    for copy in copies:
        copy.wait()
    upstream[...] = dy[...].astype(jnp.float32)
    pool[0] = total[...].astype(jnp.bfloat16)
    rows_out[...] = dot_tn(to_place[...], pool[0]).astype(jnp.bfloat16).reshape(rows_out.shape)
    for copy in out_copies:
        copy.start()

    def one_layer(turn, carry):
        layer = layers - 1 - turn
        base = layer * 16
        first_step = turn * PER_LAYER
        row = lambda n: vec[pl.ds(base + n, 1), :]
        gsum[...] = jnp.zeros_like(gsum)

        def keep(chunk, x):
            return pltpu.make_async_copy(
                staged, grads.at[layer, x, :, :, :, :, pl.ds(chunk * CHUNK, CHUNK)], stage.at[0])

        def store(first, values):
            staged[:, :, :, :, first:first + values.shape[1]] = values.astype(jnp.bfloat16).reshape(
                NZ, NY, NC, SHARD, values.shape[1])

        middle_copy = fetch(middle_in.at[layer], mid, 0)
        middle_copy.start()
        weights.start(layer, 5)
        middle_copy.wait()

        def first_rows(rows):
            up = upstream[rows, :]
            scaled = row(7) * up
            dy[rows, :] = scaled.astype(jnp.bfloat16)
            add_rows(6, scaled)
            middle = mid[rows, :]
            add_rows(7, up * (total[rows, :] - middle))
            hat, _ = normed_rows(middle)
            normed[rows, :] = (hat * row(4) + row(5)).astype(jnp.bfloat16)
        row_loop(first_rows)

        for turn_part, part in enumerate((1, 0)):
            reads = [
                (fetch(hidden_in.at[layer, x * 2 + part], pool.at[x], x),
                 fetch(slope_in.at[layer, x * 2 + part], pool.at[2 + x], 2 + x)) for x in range(NX)]
            for pair in reads:
                for copy in pair:
                    copy.start()
            if part == 0:
                weights.start(layer, 4)
            for x in range(NX):
                unit = x * 2 + part
                for copy in reads[x]:
                    copy.wait()
                weights.wait(layer, 4 + part, x)
                for side in range(2):
                    store(side * 512, dot_tn(dy[...], pool[x, :, side * 512:side * 512 + 512]))
                keep(4 + part, x).start()
                total[...] = dot_nn(dy[...], weights.get(x))

                def to_pre(rows):
                    grad = (total[rows, :] * pool[2 + x, rows, :].astype(jnp.float32)).astype(jnp.bfloat16)
                    big[unit, rows, :] = grad
                    add_rows(10 + unit, grad.astype(jnp.float32))
                row_loop(to_pre)
                keep(4 + part, x).wait()
            scatter.tick(first_step + turn_part)
        for turn_part, part in enumerate((1, 0)):
            weights.start(layer, 2 + part)
            for x in range(NX):
                unit = x * 2 + part
                for side in range(2):
                    store(side * 512, dot_tn(normed[...], big[unit, :, side * 512:side * 512 + 512]))
                keep(2 + part, x).start()
                weights.wait(layer, 2 + part, x)
                term = dot_nt(big[unit], weights.get(x))
                if turn_part == 0 and x == 0:
                    total[...] = term
                else:
                    total[...] = total[...] + term
                keep(2 + part, x).wait()
            scatter.tick(first_step + 2 + turn_part)
        acts_copy = fetch(acts_in.at[layer], big, 0)
        acts_copy.start()
        weights.start(layer, 1)

        def middle_rows(rows):
            grad = total[rows, :]
            hat, inverse = normed_rows(mid[rows, :])
            add_rows(4, grad * hat)
            add_rows(5, grad)
            scaled = grad * row(4)
            inner = (scaled - jnp.mean(scaled, axis=1, keepdims=True)
                     - hat * jnp.mean(scaled * hat, axis=1, keepdims=True))
            here = upstream[rows, :] + inverse * inner
            upstream[rows, :] = here
            scaled_mid = row(3) * here
            add_rows(2, scaled_mid)
            dy[rows, :] = scaled_mid.astype(jnp.bfloat16)
        row_loop(middle_rows)
        resid_copy = fetch(resid_in.at[layer], total, 1)
        resid_copy.start()
        for x in range(NX):
            weights.wait(layer, 1, x)
            pool[0, :, x * 512:x * 512 + 512] = dot_nn(dy[...], weights.get(x, 512, 512)).astype(jnp.bfloat16)
        resid_copy.wait()

        def resid_rows(rows):
            values = total[rows, :]
            add_rows(3, upstream[rows, :] * (mid[rows, :] - values))
            hat, _ = normed_rows(values)
            normed[rows, :] = (hat * row(0) + row(1)).astype(jnp.bfloat16)
        row_loop(resid_rows)
        acts_copy.wait()

        @pl.loop(0, PAIRS)
        def _(pair):
            lanes = pl.ds(pl.multiple_of(pair * 128, 128), 128)
            for w, (first, n) in enumerate(WINDOWS):
                rows = pl.ds(first, n)
                query, keys, values = big[0, rows, lanes], big[1, rows, lanes], big[2, rows, lanes]
                probs = window_probs(query, keys, other[w], n)
                grad = both_heads(pool[0, rows, lanes])
                pool[3, rows, lanes] = dot_tn(probs.astype(jnp.bfloat16), grad).astype(jnp.bfloat16)
                grad_probs = dot_nt(grad, values)
                inner = jnp.sum(probs * grad_probs, axis=1, keepdims=True)
                grad_scores = (probs * (grad_probs - inner)).astype(jnp.bfloat16)
                pool[1, rows, lanes] = (one_head_each(dot_nn(grad_scores, keys)) * 0.125).astype(jnp.bfloat16)
                pool[2, rows, lanes] = (dot_tn(grad_scores, both_heads(query)) * 0.125).astype(jnp.bfloat16)

        for x in range(NX):
            half = slice(x * 512, x * 512 + 512)
            store(0, dot_tn(normed[...], pool[3, :, half]))
            store(512, dot_tn(dy[...], big[3, :, half]))
            keep(1, x).start()
            term = dot_nt(pool[3, :, half], weights.get(x, 0, 512))
            mid[...] = term if x == 0 else mid[...] + term
            keep(1, x).wait()
        scatter.tick(first_step + 4)
        weights.start(layer, 0)

        def sum_rows(rows):
            add_rows(8, pool[1, rows, :].astype(jnp.float32))
            add_rows(9, pool[3, rows, :].astype(jnp.float32))
        row_loop(sum_rows)
        for x in range(NX):
            half = slice(x * 512, x * 512 + 512)
            store(0, dot_tn(normed[...], pool[1, :, half]))
            store(512, dot_tn(normed[...], pool[2, :, half]))
            keep(0, x).start()
            weights.wait(layer, 0, x)
            mid[...] = mid[...] + dot_nt(pool[1, :, half], weights.get(x, 0, 512))
            mid[...] = mid[...] + dot_nt(pool[2, :, half], weights.get(x, 512, 512))
            keep(0, x).wait()
        scatter.tick(first_step + 5)

        def input_rows(rows):
            grad = mid[rows, :]
            hat, inverse = normed_rows(total[rows, :])
            add_rows(0, grad * hat)
            add_rows(1, grad)
            scaled = grad * row(0)
            inner = (scaled - jnp.mean(scaled, axis=1, keepdims=True)
                     - hat * jnp.mean(scaled * hat, axis=1, keepdims=True))
            upstream[rows, :] = upstream[rows, :] + inverse * inner
        row_loop(input_rows)
        for kind in range(14):
            value = jnp.sum(gsum[kind], axis=0, keepdims=True)
            if kind == 3 or kind == 7:
                value = value / row(kind)
            small_sum[pl.ds(base + kind, 1), :] = value
        return carry

    lax.fori_loop(0, layers, one_layer, 0)
    small_total.start(0)
    for copy in out_copies:
        copy.wait()
    pool[0] = upstream[...].astype(jnp.bfloat16)
    rows_out[...] = dot_tn(to_place[...], pool[0]).astype(jnp.bfloat16).reshape(rows_out.shape)
    for copy in grad_copies:
        copy.start()
    for number in range(4):
        scatter.tick(chunks + number)
        small_total.add(number)
        if number < 3:
            small_total.start(number + 1)
    scatter.tick(chunks + 4)
    for copy in grad_copies:
        copy.wait()


def backward_all(whole, vec, grad_in, resids, middles, result, acts, hiddens, slopes, to_place, other):
    layers = whole.shape[0]
    full = grad_in.shape
    width = full[1]
    chunks = layers * PER_LAYER
    any_spec = pl.BlockSpec(memory_space=pl.ANY)
    vmem = pl.BlockSpec(memory_space=pltpu.VMEM)
    bf16, f32 = jnp.bfloat16, jnp.float32
    rows_shape = (2, HALF_PAD, width)
    return pl.pallas_call(
        functools.partial(bwd_kernel, layers),
        out_shape=(
            jax.ShapeDtypeStruct((layers, SHARD, COLS), bf16),
            jax.ShapeDtypeStruct(vec.shape, f32),
            jax.ShapeDtypeStruct(rows_shape, bf16),
            jax.ShapeDtypeStruct(rows_shape, bf16),
            jax.ShapeDtypeStruct(whole.shape, bf16),
        ),
        in_specs=[any_spec, vmem] + [any_spec] * 7 + [vmem, vmem],
        out_specs=(vmem, vmem, any_spec, any_spec, any_spec),
        scratch_shapes=[
            pltpu.VMEM((SLOTS, NX, NZ, NY, SHARD, CHUNK), bf16),
            pltpu.VMEM((NX, NZ, NY, SHARD, CHUNK), bf16),
        ] + landing_shapes() + [
            pltpu.VMEM(full, f32),
            pltpu.VMEM(full, bf16),
            pltpu.VMEM(full, bf16),
            pltpu.VMEM(full, f32),
            pltpu.VMEM(full, f32),
            pltpu.VMEM((4,) + full, bf16),
            pltpu.VMEM((4,) + full, bf16),
            pltpu.VMEM((NX, NZ, NY, NC, SHARD, CHUNK), bf16),
            pltpu.VMEM((NZ, NY, NC, SHARD, CHUNK), bf16),
            pltpu.VMEM(rows_shape, bf16),
            pltpu.VMEM((14, 8, width), f32),
            pltpu.VMEM((6,) + vec.shape, f32),
            pltpu.SemaphoreType.DMA((chunks, len(ROUTES) + 1, 6)),
            pltpu.SemaphoreType.DMA((chunks, len(ROUTES) + 1, 6)),
            pltpu.SemaphoreType.DMA((chunks,)),
            pltpu.SemaphoreType.REGULAR((7,)),
            pltpu.SemaphoreType.DMA((6,)),
            pltpu.SemaphoreType.DMA((6,)),
            pltpu.SemaphoreType.DMA((6,)),
            pltpu.SemaphoreType.DMA((2,)),
            pltpu.SemaphoreType.DMA((4,)),
            pltpu.SemaphoreType.DMA((1,)),
        ],
        compiler_params=pltpu.CompilerParams(
            collective_id=2, has_side_effects=True, vmem_limit_bytes=63 * 1024 * 1024),
        name="backward_all",
    )(whole, vec, grad_in, resids, middles, result, acts, hiddens, slopes, to_place, other)


def spread_small(vectors, qv_bias, up_bias):
    layers = vectors.shape[0]
    here = (jnp.arange(NZ * NY * NC) == lax.axis_index("dp"))
    side = (jnp.arange(NX) == lax.axis_index("mp"))
    vec = jnp.where(here[:, None] & side[0], vectors[:, :, None, :], 0).reshape(layers, 8, -1)
    qv = jnp.where(side[:, None, None, None] & here[:, None], qv_bias[:, :, None, :, None, :], 0).reshape(layers, 2, -1)
    up = jnp.where(side[:, None, None, None] & here[:, None], up_bias[:, None, :, None, :], 0).reshape(layers, 4, -1)
    rows = jnp.concatenate([vec, qv, up, jnp.zeros((layers, 2, vec.shape[2]), vec.dtype)], axis=1)
    return rows.reshape(layers * 16, -1)


def placement(ids):
    same = ids[:, None] == ids[None, :]
    count = jnp.sum(same, axis=1)
    order = jnp.arange(ids.shape[0])
    before = order[None, :] < order[:, None]
    long = count > 100
    kind = (long[:, None] == long[None, :]) & before
    inside = jnp.sum(same & before, axis=1)
    earlier = jnp.sum(kind, axis=1) - inside
    return jnp.where(long, jnp.where(earlier > 0, 208, 0) + inside, 416 + earlier + inside)


def on_device_fast(
    tokens, segments, qkv_weight, out_weight, up_weight, down_weight, vectors, qv_bias, up_bias, cotangent
):
    layers = qkv_weight.shape[0]
    half = tokens.shape[1]
    width = tokens.shape[2]
    place_x = lax.axis_index("mp")
    shard = jnp.concatenate(
        [qkv_weight[:, 0], qkv_weight[:, 1], qkv_weight[:, 2], jnp.swapaxes(out_weight, 1, 2),
         up_weight, jnp.swapaxes(down_weight, 1, 2)], axis=2)
    extra = ((0, 0), (0, HALF_PAD - half), (0, 0))
    ids = lax.dynamic_index_in_dim(segments, place_x, 0, keepdims=False)
    position = placement(ids)
    spread = jnp.concatenate([
        jnp.pad(position[:half], (0, HALF_PAD - half), constant_values=-1),
        jnp.pad(position[half:], (0, HALF_PAD - half), constant_values=-1)])
    to_place = (jnp.arange(PADDED)[:, None] == spread[None, :]).astype(jnp.bfloat16)
    new_ids = jnp.max(jnp.where(jnp.arange(PADDED)[:, None] == position[None, :], ids[None, :], -1), axis=1)
    other = jnp.stack([
        jnp.pad((new_ids[a:a + n][:, None] != new_ids[a:a + n][None, :]).astype(jnp.float32), ((0, 224 - n), (0, 224 - n)))
        for a, n in WINDOWS])
    whole, vec_rows, grad_in, resids, middles, result, acts, hiddens, slopes = forward_all(
        shard, spread_small(vectors, qv_bias, up_bias), jnp.pad(tokens, extra), jnp.pad(cotangent, extra), to_place, other)
    summed, small, out_rows, grad_rows, _ = backward_all(
        whole, vec_rows, grad_in, resids, middles, result, acts, hiddens, slopes, to_place, other)
    summed = summed.astype(jnp.float32)
    small = small.reshape(layers, 16, width)
    dp = lax.axis_index("dp")
    vec = lax.dynamic_index_in_dim(small[:, :8].reshape(layers, 8, -1, 64), dp, 2, keepdims=False)
    qv = small[:, 8:10].reshape(layers, 2, NX, -1, NZ * NY * NC, 4)
    qv = lax.dynamic_index_in_dim(lax.dynamic_index_in_dim(qv, dp, 4, keepdims=False), place_x, 2, keepdims=False)
    up = small[:, 10:14].reshape(layers, NX, -1, NZ * NY * NC, 4)
    up = lax.dynamic_index_in_dim(lax.dynamic_index_in_dim(up, dp, 3, keepdims=False), place_x, 1, keepdims=False)
    return (
        out_rows[:, :half],
        grad_rows[:, :half].astype(jnp.float32),
        jnp.stack([summed[:, :, 0:512], summed[:, :, 512:1024], summed[:, :, 1024:1536]], axis=1),
        jnp.swapaxes(summed[:, :, 1536:2048], 1, 2),
        summed[:, :, 2048:4096],
        jnp.swapaxes(summed[:, :, 4096:], 1, 2),
        vec,
        qv,
        up,
    )


def solution(mesh):
    placed = (
        P(None, ("dp", "mp"), None),
        P(None, "dp"),
        P(None, None, "dp", "mp"),
        P(None, "mp", "dp"),
        P(None, "dp", "mp"),
        P(None, "mp", "dp"),
        P(None, None, "dp"),
        P(None, None, "mp", "dp"),
        P(None, "mp", "dp"),
        P(None, ("dp", "mp"), None),
    )
    fast = dict(mesh.shape) == {"dp": NZ * NY * NC, "mp": NX}
    return jax.shard_map(
        on_device_fast if fast else on_device,
        mesh=mesh,
        in_specs=placed,
        out_specs=(
            P(None, ("dp", "mp"), None),
            P(None, ("dp", "mp"), None),
            P(None, None, "dp", "mp"),
            P(None, "mp", "dp"),
            P(None, "dp", "mp"),
            P(None, "mp", "dp"),
            P(None, None, "dp"),
            P(None, None, "mp", "dp"),
            P(None, "mp", "dp"),
        ),
        check_vma=False,
    )
```

```python
import functools
import math

import jax
import jax.numpy as jnp
from jax import lax
from jax.experimental import pallas as pl
from jax.experimental.pallas import tpu as pltpu
from jax.sharding import PartitionSpec as P

INV_ROOT_TWO = 0.7071067811865476
INV_ROOT_TAU = 0.3989422804014327


def layer_norm(values, gain, shift):
    centred = values - jnp.mean(values, axis=-1, keepdims=True)
    inverse = lax.rsqrt(jnp.mean(centred * centred, axis=-1, keepdims=True) + 1e-06)
    normed = centred * inverse
    return (normed * gain + shift, normed, inverse)


def norm_backward(upstream, normed, inverse, gain):
    scaled = upstream * gain
    inner = (
        scaled
        - jnp.mean(scaled, axis=-1, keepdims=True)
        - normed * jnp.mean(scaled * normed, axis=-1, keepdims=True)
    )
    return (inverse * inner, jnp.sum(upstream * normed, axis=0), jnp.sum(upstream, axis=0))


def contract_rows(left, right):
    return lax.dot_general(
        left, right, (((0,), (0,)), ((), ())), preferred_element_type=jnp.float32
    )


def against_rows(left, right):
    return lax.dot_general(
        left, right, (((1,), (1,)), ((), ())), preferred_element_type=jnp.float32
    )


def gather_normed(values):
    return lax.all_gather(values, "mp", axis=0, tiled=True)


def gather_upstream(values):
    return lax.all_gather(values, "mp", axis=0, tiled=True)


def branch_sum(term, count):
    return lax.psum_scatter(
        term(jnp.int32(0), count * lax.axis_size("mp")).astype(jnp.bfloat16),
        "mp",
        scatter_dimension=0,
        tiled=True,
    ).astype(jnp.float32)


def input_sum(term, count):
    return lax.psum_scatter(
        term(jnp.int32(0), count * lax.axis_size("mp")).astype(jnp.bfloat16),
        "mp",
        scatter_dimension=0,
        tiled=True,
    ).astype(jnp.float32)


def on_device(
    tokens,
    segments,
    qkv_weight,
    out_weight,
    up_weight,
    down_weight,
    vectors,
    qv_bias,
    up_bias,
    cotangent,
):
    layers = qkv_weight.shape[0]
    micro = tokens.shape[0]
    width = tokens.shape[2]
    head_dim = qv_bias.shape[3] * lax.axis_size("dp")
    scale = 1.0 / math.sqrt(head_dim)

    def attention_scores(query, keys, same_crop, heads):
        total_rows = query.shape[0]
        raw = (
            jnp.einsum(
                "qhd,khd->hqk",
                query.reshape(total_rows, heads, -1),
                keys.reshape(total_rows, heads, -1),
                preferred_element_type=jnp.float32,
            )
            * scale
        )
        return jnp.where(same_crop, raw, -1000000000.0)

    def forward_layer(resid, same_crop, whole):
        qkv_full, out_full, up_full, down_full, vector_half, qv_full, up_shift = whole
        vector_rows = vector_half.astype(jnp.float32)
        normed_in, first_normed, first_inverse = layer_norm(resid, vector_rows[0], vector_rows[1])
        first_all = gather_normed(normed_in.astype(jnp.bfloat16))
        total_rows = first_all.shape[0]
        heads = qv_full.shape[1]
        qv_flat = qv_full.astype(jnp.float32).reshape(2, -1)
        query = (
            jnp.dot(first_all, qkv_full[0], preferred_element_type=jnp.float32) + qv_flat[0]
        ).astype(jnp.bfloat16)
        keys = jnp.dot(first_all, qkv_full[1], preferred_element_type=jnp.float32).astype(
            jnp.bfloat16
        )
        values = (
            jnp.dot(first_all, qkv_full[2], preferred_element_type=jnp.float32) + qv_flat[1]
        ).astype(jnp.bfloat16)
        scores = attention_scores(query, keys, same_crop, heads)
        peak = jnp.max(scores, axis=-1, keepdims=True)
        powers = jnp.exp(scores - peak)
        totals = jnp.sum(powers, axis=-1, keepdims=True)
        probs = (powers / totals).astype(jnp.bfloat16)
        log_totals = peak + jnp.log(totals)
        attended = (
            jnp.einsum(
                "hqk,khd->qhd",
                probs,
                values.reshape(total_rows, heads, -1),
                preferred_element_type=jnp.float32,
            )
            .reshape(total_rows, -1)
            .astype(jnp.bfloat16)
        )

        def project_rows(start, size):
            return jnp.dot(attended, out_full, preferred_element_type=jnp.float32)

        projected = branch_sum(project_rows, resid.shape[0])
        middle = resid + vector_rows[3] * (projected + vector_rows[2])
        normed_mid, second_normed, second_inverse = layer_norm(
            middle, vector_rows[4], vector_rows[5]
        )
        second_all = gather_normed(normed_mid.astype(jnp.bfloat16))
        hidden_pre = jnp.dot(
            second_all, up_full, preferred_element_type=jnp.float32
        ) + up_shift.astype(jnp.float32).reshape(-1)
        hidden = (0.5 * hidden_pre * (1.0 + lax.erf(hidden_pre * INV_ROOT_TWO))).astype(
            jnp.bfloat16
        )

        def down_rows(start, size):
            return jnp.dot(hidden, down_full, preferred_element_type=jnp.float32)

        returned = branch_sum(down_rows, resid.shape[0])
        result = middle + vector_rows[7] * (returned + vector_rows[6])
        saved = (
            first_normed,
            first_inverse,
            first_all,
            query,
            keys,
            values,
            log_totals,
            attended,
            projected,
            second_normed,
            second_inverse,
            second_all,
            hidden_pre,
            hidden,
            returned,
        )
        return (result, saved)

    def backward_layer(upstream, same_crop, whole, saved):
        qkv_full, out_full, up_full, down_full, vector_half, qv_full, up_shift = whole
        (
            first_normed,
            first_inverse,
            first_all,
            query,
            keys,
            values,
            log_totals,
            attended,
            projected,
            second_normed,
            second_inverse,
            second_all,
            hidden_pre,
            hidden,
            returned,
        ) = saved
        vector_rows = vector_half.astype(jnp.float32)
        count = upstream.shape[0]
        total_rows = first_all.shape[0]
        heads = qv_full.shape[1]
        scaled_up = vector_rows[7] * upstream
        grad_shift_mlp = jnp.sum(scaled_up, axis=0)
        grad_scale_mlp = jnp.sum(upstream * (returned + vector_rows[6]), axis=0)
        returned_all = gather_upstream(scaled_up.astype(jnp.bfloat16))
        grad_down = contract_rows(hidden, returned_all)
        grad_hidden = against_rows(returned_all, down_full)
        normal_cdf = 0.5 * (1.0 + lax.erf(hidden_pre * INV_ROOT_TWO))
        normal_pdf = jnp.exp(-0.5 * hidden_pre * hidden_pre) * INV_ROOT_TAU
        grad_pre = (grad_hidden * (normal_cdf + hidden_pre * normal_pdf)).astype(jnp.bfloat16)
        grad_up_shift = jnp.sum(grad_pre.astype(jnp.float32), axis=0).reshape(-1, head_dim)
        grad_up = contract_rows(second_all, grad_pre)

        def up_rows(start, size):
            return against_rows(lax.dynamic_slice_in_dim(grad_pre, start, size, 0), up_full)

        grad_second = input_sum(up_rows, count)
        grad_mid_norm, grad_gain_two, grad_shift_two = norm_backward(
            grad_second, second_normed, second_inverse, vector_rows[4]
        )
        grad_middle = upstream + grad_mid_norm
        scaled_mid = vector_rows[3] * grad_middle
        grad_shift_attn = jnp.sum(scaled_mid, axis=0)
        grad_scale_attn = jnp.sum(grad_middle * (projected + vector_rows[2]), axis=0)
        projected_all = gather_upstream(scaled_mid.astype(jnp.bfloat16))
        grad_out = contract_rows(attended, projected_all)
        grad_attended = (
            against_rows(projected_all, out_full)
            .astype(jnp.bfloat16)
            .reshape(total_rows, heads, -1)
        )
        query_heads = query.reshape(total_rows, heads, -1)
        key_heads = keys.reshape(total_rows, heads, -1)
        value_heads = values.reshape(total_rows, heads, -1)
        scores = attention_scores(query, keys, same_crop, heads)
        probs = jnp.exp(scores - log_totals)
        grad_values = jnp.einsum(
            "hqk,qhd->khd",
            probs.astype(jnp.bfloat16),
            grad_attended,
            preferred_element_type=jnp.float32,
        )
        grad_probs = jnp.einsum(
            "qhd,khd->hqk", grad_attended, value_heads, preferred_element_type=jnp.float32
        )
        grad_scores = (
            probs * (grad_probs - jnp.sum(probs * grad_probs, axis=-1, keepdims=True))
        ).astype(jnp.bfloat16)
        grad_query = (
            jnp.einsum("hqk,khd->qhd", grad_scores, key_heads, preferred_element_type=jnp.float32)
            * scale
        )
        grad_keys = (
            jnp.einsum("hqk,qhd->khd", grad_scores, query_heads, preferred_element_type=jnp.float32)
            * scale
        )
        grad_project = (
            jnp.stack([grad_query, grad_keys, grad_values])
            .reshape(3, total_rows, -1)
            .astype(jnp.bfloat16)
        )
        grad_qv = jnp.stack(
            [
                jnp.sum(grad_project[0].astype(jnp.float32), axis=0),
                jnp.sum(grad_project[2].astype(jnp.float32), axis=0),
            ]
        ).reshape(2, heads, head_dim)
        grad_qkv = jnp.einsum(
            "rd,trc->tdc", first_all, grad_project, preferred_element_type=jnp.float32
        )

        def qkv_rows(start, size):
            return jnp.einsum(
                "trc,tdc->rd",
                lax.dynamic_slice_in_dim(grad_project, start, size, 1),
                qkv_full,
                preferred_element_type=jnp.float32,
            )

        grad_first = input_sum(qkv_rows, count)
        grad_in_norm, grad_gain_one, grad_shift_one = norm_backward(
            grad_first, first_normed, first_inverse, vector_rows[0]
        )
        grad_vectors = jnp.stack(
            [
                grad_gain_one,
                grad_shift_one,
                grad_shift_attn,
                grad_scale_attn,
                grad_gain_two,
                grad_shift_two,
                grad_shift_mlp,
                grad_scale_mlp,
            ]
        )
        parts = (grad_qkv, grad_out, grad_up, grad_down, grad_vectors, grad_qv, grad_up_shift)
        return (grad_middle + grad_in_norm, parts)

    shapes = [
        (3, width, qkv_weight.shape[3]),
        (out_weight.shape[1], width),
        (width, up_weight.shape[2]),
        (down_weight.shape[1], width),
        (8, width),
        (2, qv_bias.shape[2], head_dim),
        (up_bias.shape[1], head_dim),
    ]
    zeroed = tuple((jnp.zeros(shape, jnp.float32) for shape in shapes))
    start_sums = tuple((zeroed for layer in range(layers)))

    def one_micro(index, carry):
        sums, out_buffer, grad_buffer = carry
        resid = lax.dynamic_index_in_dim(tokens, index, 0, keepdims=False).astype(jnp.float32)
        crop_ids = lax.dynamic_index_in_dim(segments, index, 0, keepdims=False)
        same_crop = (crop_ids[:, None] == crop_ids[None, :])[None]
        wholes = []
        saves = []
        for layer in range(layers):
            whole = (
                lax.all_gather(qkv_weight[layer], "dp", axis=1, tiled=True),
                lax.all_gather(out_weight[layer], "dp", axis=1, tiled=True),
                lax.all_gather(up_weight[layer], "dp", axis=0, tiled=True),
                lax.all_gather(down_weight[layer], "dp", axis=1, tiled=True),
                lax.all_gather(vectors[layer], "dp", axis=1, tiled=True),
                lax.all_gather(qv_bias[layer], "dp", axis=2, tiled=True),
                lax.all_gather(up_bias[layer], "dp", axis=1, tiled=True),
            )
            resid, saved = forward_layer(resid, same_crop, whole)
            wholes.append(whole)
            saves.append(saved)
        out_buffer = lax.dynamic_update_index_in_dim(
            out_buffer, resid.astype(jnp.bfloat16), index, 0
        )
        upstream = lax.dynamic_index_in_dim(cotangent, index, 0, keepdims=False).astype(jnp.float32)
        new_sums = list(sums)
        for layer in reversed(range(layers)):
            whole = (
                lax.all_gather(qkv_weight[layer], "dp", axis=1, tiled=True),
                lax.all_gather(out_weight[layer], "dp", axis=1, tiled=True),
                lax.all_gather(up_weight[layer], "dp", axis=0, tiled=True),
                lax.all_gather(down_weight[layer], "dp", axis=1, tiled=True),
                lax.all_gather(vectors[layer], "dp", axis=1, tiled=True),
                lax.all_gather(qv_bias[layer], "dp", axis=2, tiled=True),
                lax.all_gather(up_bias[layer], "dp", axis=1, tiled=True),
            )
            upstream, parts = backward_layer(upstream, same_crop, whole, saves[layer])
            new_sums[layer] = tuple((total + piece for total, piece in zip(sums[layer], parts)))
        grad_buffer = lax.dynamic_update_index_in_dim(grad_buffer, upstream, index, 0)
        return (tuple(new_sums), out_buffer, grad_buffer)

    start = (
        start_sums,
        jnp.zeros(tokens.shape, jnp.bfloat16),
        jnp.zeros(tokens.shape, jnp.float32),
    )
    sums, output, tokens_grad = lax.fori_loop(0, micro, one_micro, start)
    reduced = []
    for layer in range(layers):
        totals = sums[layer]
        totals = (
            lax.psum_scatter(
                totals[0].astype(jnp.bfloat16), "dp", scatter_dimension=1, tiled=True
            ).astype(jnp.float32),
            lax.psum_scatter(
                totals[1].astype(jnp.bfloat16), "dp", scatter_dimension=1, tiled=True
            ).astype(jnp.float32),
            lax.psum_scatter(
                totals[2].astype(jnp.bfloat16), "dp", scatter_dimension=0, tiled=True
            ).astype(jnp.float32),
            lax.psum_scatter(
                totals[3].astype(jnp.bfloat16), "dp", scatter_dimension=1, tiled=True
            ).astype(jnp.float32),
            lax.psum_scatter(
                totals[4].astype(jnp.bfloat16), "dp", scatter_dimension=1, tiled=True
            ).astype(jnp.float32),
            lax.psum_scatter(
                totals[5].astype(jnp.bfloat16), "dp", scatter_dimension=2, tiled=True
            ).astype(jnp.float32),
            lax.psum_scatter(
                totals[6].astype(jnp.bfloat16), "dp", scatter_dimension=1, tiled=True
            ).astype(jnp.float32),
        )
        reduced.append(totals)
    stacked = [
        jnp.stack([reduced[layer][member] for layer in range(layers)]) for member in range(7)
    ]
    vector_total = lax.psum(stacked[4], "mp")
    return (
        output,
        tokens_grad,
        stacked[0],
        stacked[1],
        stacked[2],
        stacked[3],
        vector_total,
        stacked[5],
        stacked[6],
    )


MESH = pl.DeviceIdType.MESH
NZ, NY, NC, NX = 4, 2, 2, 2
SHARD = 64
COLS = 6144
CHUNK = 1024
PER_LAYER = COLS // CHUNK
ROUTES = (("zxy", 0, 16, 0, 1024), ("yzx", 16, 48, 0, 512), ("xzy", 16, 48, 512, 512))
LAG = 2


class Place:
    def __init__(self):
        dp = lax.axis_index("dp")
        self.x = lax.axis_index("mp")
        self.z = dp // 4
        self.y = lax.rem(dp // 2, 2)
        self.c = lax.rem(dp, 2)

    def device(self, x=None, z=None, y=None, c=None):
        x = self.x if x is None else x
        z = self.z if z is None else z
        y = self.y if y is None else y
        c = self.c if c is None else c
        return (z * 4 + y * 2 + c, x)

    def other(self, axis):
        if axis == "x":
            return self.device(x=1 - self.x)
        if axis == "y":
            return self.device(y=1 - self.y)
        return self.device(c=1 - self.c)

    def along(self, k):
        return lax.rem(self.z + k, NZ)


def greet(place):
    barrier = pltpu.get_barrier_semaphore()
    for axis in "cxy":
        pl.semaphore_signal(barrier, inc=1, device_id=place.other(axis), device_id_type=MESH)
    for k in (1, 2, 3):
        pl.semaphore_signal(
            barrier, inc=1, device_id=place.device(z=place.along(k)), device_id_type=MESH
        )
    pl.semaphore_wait(barrier, 6)


def block(place, filled, z=None):
    return (
        slice(None) if "x" in filled else place.x,
        slice(None) if "z" in filled else (place.z if z is None else z),
        slice(None) if "y" in filled else place.y,
        place.c,
    )


class Spread:
    def __init__(self, place, axis, source, target, send, recv, base):
        self.place, self.axis = place, axis
        self.source, self.target = source, target
        self.send, self.recv, self.base = send, recv, base

    def single(self):
        return pltpu.make_async_remote_copy(
            src_ref=self.source, dst_ref=self.target(None),
            send_sem=self.send(self.base), recv_sem=self.recv(self.base),
            device_id=self.place.other(self.axis), device_id_type=MESH)

    def direct(self, k):
        place = self.place
        return pltpu.make_async_remote_copy(
            src_ref=self.source, dst_ref=self.target(None),
            send_sem=self.send(self.base + k), recv_sem=self.recv(self.base + place.z),
            device_id=place.device(z=place.along(k)), device_id_type=MESH)

    def arrival(self, z):
        place = self.place
        return pltpu.make_async_remote_copy(
            src_ref=self.source, dst_ref=self.target(z),
            send_sem=self.send(self.base), recv_sem=self.recv(self.base + z),
            device_id=place.device(z=z), device_id_type=MESH)

    def passed(self):
        place = self.place
        origin = jnp.where(place.z == 2, 0, 3)
        return origin, pltpu.make_async_remote_copy(
            src_ref=self.target(origin), dst_ref=self.target(origin),
            send_sem=self.send(self.base), recv_sem=self.recv(self.base + origin),
            device_id=place.device(z=3 - origin), device_id_type=MESH)

    def start(self):
        if self.axis != "z":
            self.single().start()
            return
        for k in (1, 2, 3):
            if k == 2:
                self.direct(k).start()
            else:
                @pl.when(self.place.z != (3 if k == 1 else 0))
                def _():
                    self.direct(k).start()

    def relay(self):
        if self.axis != "z":
            return

        @pl.when((self.place.z == 1) | (self.place.z == 2))
        def _():
            origin, copy = self.passed()
            self.arrival(origin).wait_recv()
            copy.start()

    def arrive(self):
        if self.axis != "z":
            self.single().wait_recv()
            return
        z = self.place.z
        inner = (z == 1) | (z == 2)
        far = jnp.where(z == 2, 0, 3)
        for k in (1, 2, 3):
            origin = lax.rem(z + k, NZ)

            @pl.when(jnp.logical_not(inner & (origin == far)))
            def _():
                self.arrival(origin).wait_recv()

    def finish(self):
        if self.axis != "z":
            self.single().wait_send()
            return
        for k in (1, 2, 3):
            if k == 2:
                self.direct(k).wait_send()
            else:
                @pl.when(self.place.z != (3 if k == 1 else 0))
                def _():
                    self.direct(k).wait_send()

        @pl.when((self.place.z == 1) | (self.place.z == 2))
        def _():
            self.passed()[1].wait_send()


class Gather:
    def __init__(self, place, chunks, shard, whole, send, recv, sib, local):
        self.place, self.chunks = place, chunks
        self.shard, self.whole = shard, whole
        self.send, self.recv, self.sib, self.local = send, recv, sib, local

    def spot(self, step):
        return step // PER_LAYER, lax.rem(step, PER_LAYER) * CHUNK

    def spread(self, step, route, phase):
        order, row, rows, col, cols = ROUTES[route]
        layer, first = self.spot(step)
        area = (pl.ds(row, rows), pl.ds(pl.multiple_of(first + col, 128), cols))
        filled = order[:phase]
        target = lambda z: self.whole.at[(layer,) + block(self.place, filled, z) + area]
        source = self.shard.at[(layer,) + area] if phase == 0 else target(None)
        axis = order[phase]
        base = {"z": 0, "y": 4, "x": 5}[axis]
        return Spread(
            self.place, axis, source, target,
            lambda slot: self.send.at[step, route, slot], lambda slot: self.recv.at[step, route, slot], base)

    def own(self, step):
        layer, first = self.spot(step)
        cols = pl.ds(pl.multiple_of(first, CHUNK), CHUNK)
        return pltpu.make_async_copy(
            self.shard.at[layer, :, cols],
            self.whole.at[(layer,) + block(self.place, "") + (slice(None), cols)], self.local.at[step])

    def sibling(self, step):
        layer, first = self.spot(step)
        cols = pl.ds(pl.multiple_of(first, CHUNK), CHUNK)
        part = self.whole.at[(layer,) + block(self.place, "xyz") + (slice(None), cols)]
        return pltpu.make_async_remote_copy(
            src_ref=part, dst_ref=part, send_sem=self.sib.at[0, step], recv_sem=self.sib.at[1, step],
            device_id=self.place.other("c"), device_id_type=MESH)

    def phase(self, step, number):
        every = range(len(ROUTES))
        if number == 0:
            self.own(step).start()
        if number == 1:
            self.own(step).wait()
        for route in every:
            if 1 <= number <= 3:
                self.spread(step, route, number - 1).arrive()
            if number <= 2:
                self.spread(step, route, number).start()
        if number == 3:
            self.sibling(step).start()
        if number == 4:
            self.sibling(step).wait()
            for route in every:
                for phase in range(3):
                    self.spread(step, route, phase).finish()

    def tick(self, step):
        for number in range(5):
            at = step - LAG * number

            @pl.when((at >= 0) & (at < self.chunks))
            def _():
                self.phase(at, number)
            if number < 3:
                early = step - LAG * number - 1

                @pl.when((early >= 0) & (early < self.chunks))
                def _():
                    for route in range(len(ROUTES)):
                        self.spread(early, route, number).relay()

    @property
    def ticks(self):
        return self.chunks + 4 * LAG


def ag_kernel(chunks, shard, small, tokens, cotangent, whole, small_all, mine, mine_grad, send, recv, sib, local, odd):
    place = Place()
    greet(place)
    gather = Gather(place, chunks, shard, whole, send, recv, sib, local)

    def halves(n, source, target):
        return (
            pltpu.make_async_remote_copy(
                src_ref=source.at[1 - place.x], dst_ref=target.at[place.x],
                send_sem=odd.at[4 * n], recv_sem=odd.at[4 * n + 1],
                device_id=place.other("x"), device_id_type=MESH),
            pltpu.make_async_copy(source.at[place.x], target.at[place.x], odd.at[4 * n + 2]),
        )

    order = "zyx"

    def small_spread(phase):
        target = lambda z: small_all.at[block(place, order[:phase], z)]
        base = {"z": 0, "y": 4, "x": 5}[order[phase]]
        return Spread(
            place, order[phase], small if phase == 0 else target(None), target,
            lambda slot: odd.at[8 + slot], lambda slot: odd.at[16 + slot], base)

    part = small_all.at[block(place, "xyz")]
    small_sibling = pltpu.make_async_remote_copy(
        src_ref=part, dst_ref=part, send_sem=odd.at[24], recv_sem=odd.at[25],
        device_id=place.other("c"), device_id_type=MESH)
    small_own = pltpu.make_async_copy(small, small_all.at[block(place, "")], odd.at[26])
    token_copies = halves(0, tokens, mine)
    grad_copies = halves(1, cotangent, mine_grad)
    for copy in token_copies:
        copy.start()
    small_own.start()
    small_spread(0).start()

    def tick(step, carry):
        @pl.when(step == 1)
        def _():
            small_spread(0).relay()
            small_own.wait()

        for phase in (1, 2):
            @pl.when(step == 1 + phase)
            def _():
                small_spread(phase - 1).arrive()
                small_spread(phase).start()

        @pl.when(step == 4)
        def _():
            small_spread(2).arrive()
            small_sibling.start()
        gather.tick(step)

        @pl.when(step == chunks // 2)
        def _():
            for copy in grad_copies:
                copy.start()
        return carry

    lax.fori_loop(0, gather.ticks, tick, 0)
    small_sibling.wait()
    for phase in range(3):
        small_spread(phase).finish()
    for copy in token_copies + grad_copies:
        copy.wait()


def gather_all(shard, small, tokens, cotangent):
    layers = shard.shape[0]
    chunks = layers * PER_LAYER
    half = tokens.shape
    any_spec = pl.BlockSpec(memory_space=pl.ANY)
    return pl.pallas_call(
        functools.partial(ag_kernel, chunks),
        out_shape=(
            jax.ShapeDtypeStruct((layers, NX, NZ, NY, NC, SHARD, COLS), jnp.bfloat16),
            jax.ShapeDtypeStruct((NX, NZ, NY, NC) + small.shape, small.dtype),
            jax.ShapeDtypeStruct(half, jnp.bfloat16),
            jax.ShapeDtypeStruct(half, jnp.bfloat16),
        ),
        in_specs=[pl.BlockSpec(memory_space=pltpu.VMEM)] * 4,
        out_specs=(any_spec,) * 4,
        scratch_shapes=[
            pltpu.SemaphoreType.DMA((chunks, len(ROUTES), 6)),
            pltpu.SemaphoreType.DMA((chunks, len(ROUTES), 6)),
            pltpu.SemaphoreType.DMA((2, chunks)),
            pltpu.SemaphoreType.DMA((chunks,)),
            pltpu.SemaphoreType.DMA((32,)),
        ],
        compiler_params=pltpu.CompilerParams(collective_id=1, has_side_effects=True, vmem_limit_bytes=32 * 1024 * 1024),
        name="gather_all",
    )(shard, small, tokens, cotangent)
SLOTS = 5


class Scatter:
    def __init__(self, place, chunks, grads, summed, acc, near, first, second, third, send, recv, local, free):
        self.place, self.chunks = place, chunks
        self.grads, self.summed = grads, summed
        self.acc, self.near = acc, near
        self.landing = (first, second, third)
        self.send, self.recv, self.local, self.free = send, recv, local, free

    def spot(self, step):
        chunk = self.chunks - 1 - step
        return chunk // PER_LAYER, pl.multiple_of(lax.rem(chunk, PER_LAYER) * CHUNK, CHUNK)

    def slot(self, step):
        return lax.rem(step, SLOTS)

    def core_copies(self, step):
        layer, first = self.spot(step)
        cols = pl.ds(first, CHUNK)
        slot = self.slot(step)
        return (
            pltpu.make_async_remote_copy(
                src_ref=self.grads.at[layer, :, :, :, 1 - self.place.c, :, cols], dst_ref=self.acc.at[slot],
                send_sem=self.send.at[step, len(ROUTES), 0], recv_sem=self.recv.at[step, len(ROUTES), 0],
                device_id=self.place.other("c"), device_id_type=MESH),
            pltpu.make_async_copy(
                self.grads.at[layer, :, :, :, self.place.c, :, cols], self.near, self.local.at[step]),
        )

    def core_add(self, step):
        slot = self.slot(step)

        def one(n, carry):
            x, z, y = n // 8, lax.rem(n // 2, 4), lax.rem(n, 2)
            self.acc[slot, x, z, y] = self.acc[slot, x, z, y] + self.near[x, z, y]
            return carry

        lax.fori_loop(0, NX * NZ * NY, one, 0)

    def area(self, route):
        _, row, rows, col, cols = ROUTES[route]
        return (pl.ds(row, rows), pl.ds(col, cols))

    def index(self, route, phase, over):
        order = ROUTES[route][0]
        left = order[:2 - phase]
        place = self.place
        picked = []
        for axis, own in (("x", place.x), ("z", place.z), ("y", place.y)):
            picked.append(over[axis] if axis in over else (slice(None) if axis in left else own))
        return tuple(picked)

    def copy(self, step, route, phase, over, device, source_slot, sem):
        slot = self.slot(step)
        axis = ROUTES[route][0][2 - phase]
        land = self.landing[phase][route].at[slot]
        if axis == "z":
            land = land.at[source_slot]
        base = {"z": 0, "y": 4, "x": 5}[axis]
        return pltpu.make_async_remote_copy(
            src_ref=self.acc.at[(slot,) + self.index(route, phase, over) + self.area(route)], dst_ref=land,
            send_sem=self.send.at[step, route, base + sem], recv_sem=self.recv.at[step, route, base + source_slot],
            device_id=device, device_id_type=MESH)

    def single(self, step, route, phase):
        axis = ROUTES[route][0][2 - phase]
        own = self.place.x if axis == "x" else self.place.y
        return self.copy(step, route, phase, {axis: 1 - own}, self.place.other(axis), 0, 0)

    def along(self, step, route, phase, k):
        place = self.place
        z = place.along(k)
        far = (place.z + z == 3) & ((place.z == 0) | (place.z == 3))
        via = jnp.where(far, jnp.where(place.z == 0, 1, 2), z)
        return self.copy(
            step, route, phase, {"z": z}, place.device(z=via), jnp.where(far, via, place.z), k)

    def arrival(self, step, route, phase, z):
        return self.copy(step, route, phase, {"z": self.place.z}, self.place.device(z=lax.rem(z + 1, NZ)), z, 1)

    def start(self, step, route, phase):
        if ROUTES[route][0][2 - phase] != "z":
            self.single(step, route, phase).start()
            return
        z = self.place.z
        for k in (1, 2, 3):
            if k == 2:
                @pl.when((z == 0) | (z == 3))
                def _():
                    self.along(step, route, phase, k).start()
            else:
                self.along(step, route, phase, k).start()

    def relay(self, step, route, phase):
        if ROUTES[route][0][2 - phase] != "z":
            return
        z = self.place.z
        slot = self.slot(step)

        @pl.when((z == 1) | (z == 2))
        def _():
            self.arrival(step, route, phase, z).wait_recv()
            far = lax.rem(z + 2, NZ)
            at = (slot,) + self.index(route, phase, {"z": far}) + self.area(route)
            self.acc[at] = self.acc[at] + self.landing[phase][route][slot, z]
            self.along(step, route, phase, 2).start()

    def arrive(self, step, route, phase):
        slot = self.slot(step)
        area = self.area(route)
        axis = ROUTES[route][0][2 - phase]
        land = self.landing[phase][route]
        if axis != "z":
            self.single(step, route, phase).wait_recv()
            at = self.index(route, phase, {axis: self.place.x if axis == "x" else self.place.y})
            lead = [n for n, entry in enumerate(at) if isinstance(entry, slice)]
            extents = [(NX, NZ, NY)[n] for n in lead]
            total = 1
            for extent in extents:
                total *= extent

            def one(n, carry):
                part = []
                for extent in reversed(extents):
                    part.append(lax.rem(n, extent))
                    n = n // extent
                part.reverse()
                full = list(at)
                for position, value in zip(lead, part):
                    full[position] = value
                self.acc[(slot,) + tuple(full) + area] = (
                    self.acc[(slot,) + tuple(full) + area] + land[(slot,) + tuple(part)])
                return carry

            if total == 1:
                one(0, 0)
            else:
                lax.fori_loop(0, total, one, 0)
            return
        z = self.place.z
        ends = (z == 0) | (z == 3)
        at = (slot,) + self.index(route, phase, {"z": z}) + area
        for k in (1, 2, 3):
            origin = lax.rem(z + k, NZ)

            @pl.when(jnp.logical_not(ends & (z + origin == 3)))
            def _():
                self.arrival(step, route, phase, origin).wait_recv()
                self.acc[at] = self.acc[at] + land[slot, origin]

    def finish(self, step, route, phase):
        if ROUTES[route][0][2 - phase] != "z":
            self.single(step, route, phase).wait_send()
            return
        for k in (1, 2, 3):
            self.along(step, route, phase, k).wait_send()

    def others(self):
        place = self.place
        pairs = [(place.other(axis), n, n) for n, axis in enumerate("cxy")]
        for k in (1, 2, 3):
            z = place.along(k)
            pairs.append((place.device(z=z), 3 + place.z, 3 + z))
        return pairs

    def phase(self, step, number):
        every = range(len(ROUTES))
        if number == 0:
            @pl.when(step >= SLOTS)
            def _():
                for _, _, mine in self.others():
                    pl.semaphore_wait(self.free.at[mine], 1)
            for copy in self.core_copies(step):
                copy.start()
            return
        if number == 1:
            remote, own = self.core_copies(step)
            own.wait()
            remote.wait_recv()
            self.core_add(step)
        for route in every:
            if number >= 2:
                self.arrive(step, route, number - 2)
            if number <= 3:
                self.start(step, route, number - 1)
        if number == 4:
            slot = self.slot(step)
            layer, first = self.spot(step)
            place = self.place
            self.summed[layer, :, pl.ds(first, CHUNK)] = self.acc[slot, place.x, place.z, place.y]
            self.core_copies(step)[0].wait_send()
            for route in every:
                for phase in range(3):
                    self.finish(step, route, phase)

            @pl.when(step + SLOTS < self.chunks)
            def _():
                for device, there, _ in self.others():
                    pl.semaphore_signal(self.free.at[there], inc=1, device_id=device, device_id_type=MESH)

    def tick(self, step):
        for number in (4, 3, 2, 1, 0):
            at = step - number

            @pl.when((at >= 0) & (at < self.chunks))
            def _():
                self.phase(at, number)

    def pass_on(self, step):
        for number in (1, 2, 3):
            at = step - number

            @pl.when((at >= 0) & (at < self.chunks))
            def _():
                for route in range(len(ROUTES)):
                    self.relay(at, route, number - 1)

    @property
    def ticks(self):
        return self.chunks + 4


def landing_shapes():
    shapes = []
    for phase in range(3):
        for order, row, rows, col, cols in ROUTES:
            left = order[:2 - phase]
            axis = order[2 - phase]
            lead = tuple(extent for name, extent in (("x", NX), ("z", NZ), ("y", NY)) if name in left)
            if axis == "z":
                lead = (NZ,) + lead
            shapes.append(pltpu.VMEM((SLOTS,) + lead + (rows, cols), jnp.bfloat16))
    return shapes


WINDOWS = ((0, 208), (208, 208), (416, 224))
PADDED = 640
HALF_PAD = 320
PAIRS = 8
STEP = 160


def swap_halves(place, source, target, odd, n):
    return (
        pltpu.make_async_remote_copy(
            src_ref=source.at[1 - place.x], dst_ref=target.at[place.x],
            send_sem=odd.at[n], recv_sem=odd.at[n + 1],
            device_id=place.other("x"), device_id_type=MESH),
        pltpu.make_async_copy(source.at[place.x], target.at[place.x], odd.at[n + 2]),
    )


class Total:
    def __init__(self, place, value, landing, send, recv, base):
        self.place, self.value, self.landing = place, value, landing
        self.send, self.recv, self.base = send, recv, base

    def copies(self, number):
        place = self.place
        if number < 3:
            slots, devices = [number], [place.other("cxy"[number])]
        else:
            slots, devices = [3, 4, 5], [place.device(z=place.along(k)) for k in (1, 2, 3)]
        return [
            pltpu.make_async_remote_copy(
                src_ref=self.value, dst_ref=self.landing.at[slot],
                send_sem=self.send.at[self.base + slot], recv_sem=self.recv.at[self.base + slot],
                device_id=device, device_id_type=MESH)
            for slot, device in zip(slots, devices)
        ]

    def start(self, number):
        for copy in self.copies(number):
            copy.start()

    def add(self, number):
        for copy in self.copies(number):
            copy.wait()
        for slot in ([number] if number < 3 else [3, 4, 5]):
            self.value[...] = self.value[...] + self.landing[slot]


def dot_nn(left, right):
    return jnp.dot(left, right, preferred_element_type=jnp.float32)


def dot_nt(left, right):
    return lax.dot_general(left, right, (((1,), (1,)), ((), ())), preferred_element_type=jnp.float32)


def dot_tn(left, right):
    return lax.dot_general(left, right, (((0,), (0,)), ((), ())), preferred_element_type=jnp.float32)


def both_heads(rows):
    left = lax.broadcasted_iota(jnp.int32, rows.shape, 1) < 64
    zero = jnp.zeros_like(rows)
    return jnp.concatenate([jnp.where(left, rows, zero), jnp.where(left, zero, rows)], axis=0)


def one_head_each(rows):
    n = rows.shape[0] // 2
    left = lax.broadcasted_iota(jnp.int32, (n, rows.shape[1]), 1) < 64
    return jnp.where(left, rows[:n], rows[n:])


def window_probs(query, keys, other, n):
    raw = dot_nt(both_heads(query), keys) * 0.125
    apart = jnp.concatenate([other[:n, :n], other[:n, :n]], axis=0) > 0.5
    raw = jnp.where(apart, -1e9, raw)
    powers = jnp.exp(raw - jnp.max(raw, axis=1, keepdims=True))
    return powers * (1.0 / jnp.sum(powers, axis=1, keepdims=True))


def row_loop(body, size=STEP):
    @pl.loop(0, PADDED // size)
    def _(n):
        body(pl.ds(pl.multiple_of(n * size, size), size))


def normed_rows(values):
    centred = values - jnp.mean(values, axis=1, keepdims=True)
    inverse = lax.rsqrt(jnp.mean(centred * centred, axis=1, keepdims=True) + 1e-06)
    return centred * inverse, inverse


class Weights:
    def __init__(self, whole, held, sem):
        self.whole, self.held, self.sem = whole, held, sem

    def copy(self, layer, chunk, x):
        return pltpu.make_async_copy(
            self.whole.at[layer, x, :, :, :, :, pl.ds(chunk * CHUNK, CHUNK)], self.held.at[x], self.sem.at[x])

    def start(self, layer, chunk):
        for x in range(NX):
            self.copy(layer, chunk, x).start()

    def wait(self, layer, chunk, x):
        self.copy(layer, chunk, x).wait()

    def get(self, x, first=0, count=CHUNK):
        return self.held[x, :, :, :, :, first:first + count].reshape(NZ * NY * NC * SHARD, count)


def fwd_kernel(
    layers, shard, small, tokens, cotangent, to_place, other,
    whole, vec_out, grad_out, resid_out, middle_out, result_out, acts_out, hidden_out, slope_out,
    mine, mine_grad, vec, small_sum, small_land, resid, normed, acts, hidden, slope, total, held,
    send, recv, sib, local, odd, small_send, small_recv, wsem, save,
):
    chunks = layers * PER_LAYER
    place = Place()
    greet(place)
    gather = Gather(place, chunks, shard, whole, send, recv, sib, local)
    weights = Weights(whole, held, wsem)
    token_copies = swap_halves(place, tokens, mine, odd, 0)
    grad_copies = swap_halves(place, cotangent, mine_grad, odd, 3)
    small_total = Total(place, small_sum, small_land, small_send, small_recv, 0)

    small_sum[...] = small[...]
    small_total.start(0)
    gather.tick(0)
    gather.tick(1)
    small_total.add(0)
    small_total.start(1)
    for copy in token_copies:
        copy.start()
    gather.tick(2)
    gather.tick(3)
    small_total.add(1)
    small_total.start(2)
    gather.tick(4)
    small_total.add(2)
    small_total.start(3)
    gather.tick(5)
    gather.tick(6)
    for copy in token_copies:
        copy.wait()
    for copy in grad_copies:
        copy.start()
    gather.tick(7)
    small_total.add(3)
    vec[...] = small_sum[...].astype(jnp.float32)
    vec_copy = pltpu.make_async_copy(vec, vec_out, save.at[12])
    vec_copy.start()
    resid[...] = dot_nn(to_place[...], mine[...].reshape(PADDED, -1))
    grad_copy = pltpu.make_async_copy(slope.at[0], grad_out, save.at[13])

    def one_layer(layer, carry):
        base = layer * 16
        row = lambda n: vec[pl.ds(base + n, 1), :]

        def norm_into(gain, shift):
            def body(rows):
                values, _ = normed_rows(resid[rows, :])
                normed[rows, :] = (values * row(gain) + row(shift)).astype(jnp.bfloat16)
            row_loop(body)

        norm_into(0, 1)
        resid_copy = pltpu.make_async_copy(resid, resid_out.at[layer], save.at[0])
        resid_copy.start()

        @pl.when(layer == layers - 1)
        def _():
            for copy in grad_copies:
                copy.wait()
            slope[0] = dot_nn(to_place[...], mine_grad[...].reshape(PADDED, -1)).astype(jnp.bfloat16)
            grad_copy.start()
            grad_copy.wait()

        gather.tick(layer * PER_LAYER + 4 * LAG)
        weights.start(layer, 0)
        for x in range(NX):
            half = slice(x * 512, x * 512 + 512)
            weights.wait(layer, 0, x)
            both = dot_nn(normed[...], weights.get(x))
            acts[0, :, half] = (both[:, :512] + row(8)[:, half]).astype(jnp.bfloat16)
            acts[1, :, half] = both[:, 512:].astype(jnp.bfloat16)
        gather.tick(layer * PER_LAYER + 4 * LAG + 1)
        weights.start(layer, 1)
        for x in range(NX):
            half = slice(x * 512, x * 512 + 512)
            weights.wait(layer, 1, x)
            acts[2, :, half] = (dot_nn(normed[...], weights.get(x, 0, 512)) + row(9)[:, half]).astype(jnp.bfloat16)

        @pl.loop(0, PAIRS)
        def _(pair):
            lanes = pl.ds(pl.multiple_of(pair * 128, 128), 128)
            for w, (first, n) in enumerate(WINDOWS):
                rows = pl.ds(first, n)
                probs = window_probs(acts[0, rows, lanes], acts[1, rows, lanes], other[w], n)
                sums = dot_nn(probs.astype(jnp.bfloat16), acts[2, rows, lanes])
                acts[3, rows, lanes] = one_head_each(sums).astype(jnp.bfloat16)

        acts_copy = pltpu.make_async_copy(acts, acts_out.at[layer], save.at[1])
        acts_copy.start()
        total[...] = dot_nt(acts[3, :, :512], weights.get(0, 512, 512)) + dot_nt(acts[3, :, 512:], weights.get(1, 512, 512))
        resid_copy.wait()

        def to_middle(rows):
            resid[rows, :] = resid[rows, :] + row(3) * (total[rows, :] + row(2))
        row_loop(to_middle)
        middle_copy = pltpu.make_async_copy(resid, middle_out.at[layer], save.at[2])
        middle_copy.start()
        norm_into(4, 5)
        for part in range(2):
            gather.tick(layer * PER_LAYER + 4 * LAG + 2 + part)
            weights.start(layer, 2 + part)
            for x in range(NX):
                unit = x * 2 + part
                weights.wait(layer, 2 + part, x)
                total[...] = dot_nn(normed[...], weights.get(x)) + row(10 + unit)
                slope_copy = pltpu.make_async_copy(slope.at[x], slope_out.at[layer, unit], save.at[4 + x])
                if part:
                    pltpu.make_async_copy(slope.at[x], slope_out.at[layer, unit - 1], save.at[4 + x]).wait()

                def activate(rows):
                    pre = total[rows, :]
                    cdf = 0.5 * (1.0 + lax.erf(pre * INV_ROOT_TWO))
                    pdf = jnp.exp(-0.5 * pre * pre) * INV_ROOT_TAU
                    hidden[unit, rows, :] = (pre * cdf).astype(jnp.bfloat16)
                    slope[x, rows, :] = (cdf + pre * pdf).astype(jnp.bfloat16)
                row_loop(activate, 64)
                slope_copy.start()
        hidden_copy = pltpu.make_async_copy(hidden, hidden_out.at[layer], save.at[3])
        hidden_copy.start()
        for part in range(2):
            gather.tick(layer * PER_LAYER + 4 * LAG + 4 + part)
            weights.start(layer, 4 + part)
            for x in range(NX):
                weights.wait(layer, 4 + part, x)
                term = dot_nt(hidden[x * 2 + part], weights.get(x))
                if part == 0 and x == 0:
                    total[...] = term
                else:
                    total[...] = total[...] + term
        middle_copy.wait()

        def to_result(rows):
            resid[rows, :] = resid[rows, :] + row(7) * (total[rows, :] + row(6))
        row_loop(to_result)
        acts_copy.wait()
        hidden_copy.wait()
        for x in range(NX):
            pltpu.make_async_copy(slope.at[x], slope_out.at[layer, x * 2 + 1], save.at[4 + x]).wait()
        return carry

    lax.fori_loop(0, layers, one_layer, 0)
    result_copy = pltpu.make_async_copy(resid, result_out, save.at[0])
    result_copy.start()
    result_copy.wait()
    vec_copy.wait()


def forward_all(shard, small, tokens, cotangent, to_place, other):
    layers = shard.shape[0]
    width = tokens.shape[2]
    chunks = layers * PER_LAYER
    any_spec = pl.BlockSpec(memory_space=pl.ANY)
    full = (PADDED, width)
    bf16, f32 = jnp.bfloat16, jnp.float32
    return pl.pallas_call(
        functools.partial(fwd_kernel, layers),
        out_shape=(
            jax.ShapeDtypeStruct((layers, NX, NZ, NY, NC, SHARD, COLS), bf16),
            jax.ShapeDtypeStruct(small.shape, f32),
            jax.ShapeDtypeStruct(full, bf16),
            jax.ShapeDtypeStruct((layers,) + full, f32),
            jax.ShapeDtypeStruct((layers,) + full, f32),
            jax.ShapeDtypeStruct(full, f32),
            jax.ShapeDtypeStruct((layers, 4) + full, bf16),
            jax.ShapeDtypeStruct((layers, 4) + full, bf16),
            jax.ShapeDtypeStruct((layers, 4) + full, bf16),
        ),
        in_specs=[pl.BlockSpec(memory_space=pltpu.VMEM)] * 6,
        out_specs=(any_spec,) * 9,
        scratch_shapes=[
            pltpu.VMEM(tokens.shape, bf16),
            pltpu.VMEM(tokens.shape, bf16),
            pltpu.VMEM(small.shape, f32),
            pltpu.VMEM(small.shape, bf16),
            pltpu.VMEM((6,) + small.shape, bf16),
            pltpu.VMEM(full, f32),
            pltpu.VMEM(full, bf16),
            pltpu.VMEM((4,) + full, bf16),
            pltpu.VMEM((4,) + full, bf16),
            pltpu.VMEM((2,) + full, bf16),
            pltpu.VMEM(full, f32),
            pltpu.VMEM((NX, NZ, NY, NC, SHARD, CHUNK), bf16),
            pltpu.SemaphoreType.DMA((chunks, len(ROUTES), 6)),
            pltpu.SemaphoreType.DMA((chunks, len(ROUTES), 6)),
            pltpu.SemaphoreType.DMA((2, chunks)),
            pltpu.SemaphoreType.DMA((chunks,)),
            pltpu.SemaphoreType.DMA((6,)),
            pltpu.SemaphoreType.DMA((6,)),
            pltpu.SemaphoreType.DMA((6,)),
            pltpu.SemaphoreType.DMA((2,)),
            pltpu.SemaphoreType.DMA((14,)),
        ],
        compiler_params=pltpu.CompilerParams(
            collective_id=1, has_side_effects=True, vmem_limit_bytes=60 * 1024 * 1024),
        name="forward_all",
    )(shard, small, tokens, cotangent, to_place, other)


def bwd_kernel(
    layers, whole, vec, grad_in, resid_in, middle_in, result, acts_in, hidden_in, slope_in, to_place, other,
    summed, small_sum, out_rows, grad_rows, grads, *scratch,
):
    n = len(ROUTES)
    acc, near = scratch[:2]
    lands = scratch[2:2 + 3 * n]
    (upstream, dy, normed, mid, total, pool, big, held, staged, rows_out, gsum, small_land,
     send, recv, local, free, odd, small_send, small_recv, wsem, load, stage) = scratch[2 + 3 * n:]
    chunks = layers * PER_LAYER
    place = Place()
    greet(place)
    scatter = Scatter(place, chunks, grads, summed, acc, near, lands[:n], lands[n:2 * n], lands[2 * n:], send, recv, local, free)
    weights = Weights(whole, held, wsem)
    out_copies = swap_halves(place, rows_out, out_rows, odd, 0)
    grad_copies = swap_halves(place, rows_out, grad_rows, odd, 3)
    small_total = Total(place, small_sum, small_land, small_send, small_recv, 0)

    def fetch(source, target, slot):
        return pltpu.make_async_copy(source, target, load.at[slot])

    def add_rows(kind, values):
        gsum[kind] = gsum[kind] + jnp.sum(values.reshape(-1, 8, values.shape[1]), axis=0)

    small_sum[...] = jnp.zeros_like(small_sum)
    copies = [fetch(result, total, 0), fetch(grad_in, dy, 1)]
    for copy in copies:
        copy.start()
    for copy in copies:
        copy.wait()
    upstream[...] = dy[...].astype(jnp.float32)
    pool[0] = total[...].astype(jnp.bfloat16)
    rows_out[...] = dot_tn(to_place[...], pool[0]).astype(jnp.bfloat16).reshape(rows_out.shape)
    for copy in out_copies:
        copy.start()

    def one_layer(turn, carry):
        layer = layers - 1 - turn
        base = layer * 16
        first_step = turn * PER_LAYER
        row = lambda n: vec[pl.ds(base + n, 1), :]
        gsum[...] = jnp.zeros_like(gsum)

        def keep(chunk, x):
            return pltpu.make_async_copy(
                staged, grads.at[layer, x, :, :, :, :, pl.ds(chunk * CHUNK, CHUNK)], stage.at[0])

        def store(first, values):
            staged[:, :, :, :, first:first + values.shape[1]] = values.astype(jnp.bfloat16).reshape(
                NZ, NY, NC, SHARD, values.shape[1])

        middle_copy = fetch(middle_in.at[layer], mid, 0)
        middle_copy.start()

        def reads(part, x):
            return (fetch(hidden_in.at[layer, x * 2 + part], pool.at[x], 4 + x),
                    fetch(slope_in.at[layer, x * 2 + part], pool.at[2 + x], 2 + x))

        for x in range(NX):
            for copy in reads(1, x):
                copy.start()
        weights.start(layer, 5)
        middle_copy.wait()

        def first_rows(rows):
            up = upstream[rows, :]
            scaled = row(7) * up
            dy[rows, :] = scaled.astype(jnp.bfloat16)
            add_rows(6, scaled)
            middle = mid[rows, :]
            add_rows(7, up * (total[rows, :] - middle))
            hat, _ = normed_rows(middle)
            normed[rows, :] = (hat * row(4) + row(5)).astype(jnp.bfloat16)
        row_loop(first_rows)

        for turn_part, part in enumerate((1, 0)):
            for x in range(NX):
                unit = x * 2 + part
                hidden_copy, slope_copy = reads(part, x)
                hidden_copy.wait()
                for side in range(2):
                    store(side * 512, dot_tn(dy[...], pool[x, :, side * 512:side * 512 + 512]))
                keep(4 + part, x).start()
                if part == 1:
                    reads(0, x)[0].start()
                weights.wait(layer, 4 + part, x)
                total[...] = dot_nn(dy[...], weights.get(x))
                weights.copy(layer, 3 + part, x).start()
                if x == 0:
                    scatter.pass_on(first_step + turn_part - 1)
                slope_copy.wait()

                def to_pre(rows):
                    grad = (total[rows, :] * pool[2 + x, rows, :].astype(jnp.float32)).astype(jnp.bfloat16)
                    big[unit, rows, :] = grad
                    add_rows(10 + unit, grad.astype(jnp.float32))
                row_loop(to_pre)
                if part == 1:
                    reads(0, x)[1].start()
                keep(4 + part, x).wait()
            scatter.tick(first_step + turn_part)
        for turn_part, part in enumerate((1, 0)):
            for x in range(NX):
                unit = x * 2 + part
                for side in range(2):
                    store(side * 512, dot_tn(normed[...], big[unit, :, side * 512:side * 512 + 512]))
                keep(2 + part, x).start()
                if x == 0:
                    scatter.pass_on(first_step + 1 + turn_part)
                weights.wait(layer, 2 + part, x)
                term = dot_nt(big[unit], weights.get(x))
                weights.copy(layer, 1 + part, x).start()
                if turn_part == 0 and x == 0:
                    total[...] = term
                else:
                    total[...] = total[...] + term
                keep(2 + part, x).wait()
            scatter.tick(first_step + 2 + turn_part)
        acts_copy = fetch(acts_in.at[layer], big, 0)
        acts_copy.start()

        def middle_rows(rows):
            grad = total[rows, :]
            hat, inverse = normed_rows(mid[rows, :])
            add_rows(4, grad * hat)
            add_rows(5, grad)
            scaled = grad * row(4)
            inner = (scaled - jnp.mean(scaled, axis=1, keepdims=True)
                     - hat * jnp.mean(scaled * hat, axis=1, keepdims=True))
            here = upstream[rows, :] + inverse * inner
            upstream[rows, :] = here
            scaled_mid = row(3) * here
            add_rows(2, scaled_mid)
            dy[rows, :] = scaled_mid.astype(jnp.bfloat16)
        row_loop(middle_rows)
        resid_copy = fetch(resid_in.at[layer], total, 1)
        resid_copy.start()
        for x in range(NX):
            weights.wait(layer, 1, x)
            pool[0, :, x * 512:x * 512 + 512] = dot_nn(dy[...], weights.get(x, 512, 512)).astype(jnp.bfloat16)
        resid_copy.wait()

        def resid_rows(rows):
            values = total[rows, :]
            add_rows(3, upstream[rows, :] * (mid[rows, :] - values))
            hat, _ = normed_rows(values)
            normed[rows, :] = (hat * row(0) + row(1)).astype(jnp.bfloat16)
        row_loop(resid_rows)
        scatter.pass_on(first_step + 3)
        acts_copy.wait()

        @pl.loop(0, PAIRS)
        def _(pair):
            lanes = pl.ds(pl.multiple_of(pair * 128, 128), 128)
            for w, (first, n) in enumerate(WINDOWS):
                rows = pl.ds(first, n)
                query, keys, values = big[0, rows, lanes], big[1, rows, lanes], big[2, rows, lanes]
                probs = window_probs(query, keys, other[w], n)
                grad = both_heads(pool[0, rows, lanes])
                pool[3, rows, lanes] = dot_tn(probs.astype(jnp.bfloat16), grad).astype(jnp.bfloat16)
                grad_probs = dot_nt(grad, values)
                inner = jnp.sum(probs * grad_probs, axis=1, keepdims=True)
                grad_scores = (probs * (grad_probs - inner)).astype(jnp.bfloat16)
                pool[1, rows, lanes] = (one_head_each(dot_nn(grad_scores, keys)) * 0.125).astype(jnp.bfloat16)
                pool[2, rows, lanes] = (dot_tn(grad_scores, both_heads(query)) * 0.125).astype(jnp.bfloat16)

        for x in range(NX):
            half = slice(x * 512, x * 512 + 512)
            store(0, dot_tn(normed[...], pool[3, :, half]))
            store(512, dot_tn(dy[...], big[3, :, half]))
            keep(1, x).start()
            term = dot_nt(pool[3, :, half], weights.get(x, 0, 512))
            weights.copy(layer, 0, x).start()
            mid[...] = term if x == 0 else mid[...] + term
            keep(1, x).wait()
        scatter.tick(first_step + 4)

        def sum_rows(rows):
            add_rows(8, pool[1, rows, :].astype(jnp.float32))
            add_rows(9, pool[3, rows, :].astype(jnp.float32))
        row_loop(sum_rows)
        for x in range(NX):
            half = slice(x * 512, x * 512 + 512)
            store(0, dot_tn(normed[...], pool[1, :, half]))
            store(512, dot_tn(normed[...], pool[2, :, half]))
            keep(0, x).start()
            if x == 0:
                scatter.pass_on(first_step + 4)
            weights.wait(layer, 0, x)
            mid[...] = mid[...] + dot_nt(pool[1, :, half], weights.get(x, 0, 512))
            mid[...] = mid[...] + dot_nt(pool[2, :, half], weights.get(x, 512, 512))
            keep(0, x).wait()
        scatter.tick(first_step + 5)

        def input_rows(rows):
            grad = mid[rows, :]
            hat, inverse = normed_rows(total[rows, :])
            add_rows(0, grad * hat)
            add_rows(1, grad)
            scaled = grad * row(0)
            inner = (scaled - jnp.mean(scaled, axis=1, keepdims=True)
                     - hat * jnp.mean(scaled * hat, axis=1, keepdims=True))
            upstream[rows, :] = upstream[rows, :] + inverse * inner
        row_loop(input_rows)
        for kind in range(14):
            value = jnp.sum(gsum[kind], axis=0, keepdims=True)
            if kind == 3 or kind == 7:
                value = value / row(kind)
            small_sum[pl.ds(base + kind, 1), :] = value
        return carry

    lax.fori_loop(0, layers, one_layer, 0)
    small_total.start(0)
    for copy in out_copies:
        copy.wait()
    pool[0] = upstream[...].astype(jnp.bfloat16)
    rows_out[...] = dot_tn(to_place[...], pool[0]).astype(jnp.bfloat16).reshape(rows_out.shape)
    for copy in grad_copies:
        copy.start()
    for number in range(4):
        scatter.pass_on(chunks + number - 1)
        scatter.tick(chunks + number)
        small_total.add(number)
        if number < 3:
            small_total.start(number + 1)
    scatter.pass_on(chunks + 3)
    scatter.tick(chunks + 4)
    for copy in grad_copies:
        copy.wait()


def backward_all(whole, vec, grad_in, resids, middles, result, acts, hiddens, slopes, to_place, other):
    layers = whole.shape[0]
    full = grad_in.shape
    width = full[1]
    chunks = layers * PER_LAYER
    any_spec = pl.BlockSpec(memory_space=pl.ANY)
    vmem = pl.BlockSpec(memory_space=pltpu.VMEM)
    bf16, f32 = jnp.bfloat16, jnp.float32
    rows_shape = (2, HALF_PAD, width)
    return pl.pallas_call(
        functools.partial(bwd_kernel, layers),
        out_shape=(
            jax.ShapeDtypeStruct((layers, SHARD, COLS), bf16),
            jax.ShapeDtypeStruct(vec.shape, f32),
            jax.ShapeDtypeStruct(rows_shape, bf16),
            jax.ShapeDtypeStruct(rows_shape, bf16),
            jax.ShapeDtypeStruct(whole.shape, bf16),
        ),
        in_specs=[any_spec, vmem] + [any_spec] * 7 + [vmem, vmem],
        out_specs=(vmem, vmem, any_spec, any_spec, any_spec),
        scratch_shapes=[
            pltpu.VMEM((SLOTS, NX, NZ, NY, SHARD, CHUNK), bf16),
            pltpu.VMEM((NX, NZ, NY, SHARD, CHUNK), bf16),
        ] + landing_shapes() + [
            pltpu.VMEM(full, f32),
            pltpu.VMEM(full, bf16),
            pltpu.VMEM(full, bf16),
            pltpu.VMEM(full, f32),
            pltpu.VMEM(full, f32),
            pltpu.VMEM((4,) + full, bf16),
            pltpu.VMEM((4,) + full, bf16),
            pltpu.VMEM((NX, NZ, NY, NC, SHARD, CHUNK), bf16),
            pltpu.VMEM((NZ, NY, NC, SHARD, CHUNK), bf16),
            pltpu.VMEM(rows_shape, bf16),
            pltpu.VMEM((14, 8, width), f32),
            pltpu.VMEM((6,) + vec.shape, f32),
            pltpu.SemaphoreType.DMA((chunks, len(ROUTES) + 1, 6)),
            pltpu.SemaphoreType.DMA((chunks, len(ROUTES) + 1, 6)),
            pltpu.SemaphoreType.DMA((chunks,)),
            pltpu.SemaphoreType.REGULAR((7,)),
            pltpu.SemaphoreType.DMA((6,)),
            pltpu.SemaphoreType.DMA((6,)),
            pltpu.SemaphoreType.DMA((6,)),
            pltpu.SemaphoreType.DMA((2,)),
            pltpu.SemaphoreType.DMA((6,)),
            pltpu.SemaphoreType.DMA((1,)),
        ],
        compiler_params=pltpu.CompilerParams(
            collective_id=2, has_side_effects=True, vmem_limit_bytes=63 * 1024 * 1024),
        name="backward_all",
    )(whole, vec, grad_in, resids, middles, result, acts, hiddens, slopes, to_place, other)


def spread_small(vectors, qv_bias, up_bias):
    layers = vectors.shape[0]
    here = (jnp.arange(NZ * NY * NC) == lax.axis_index("dp"))
    side = (jnp.arange(NX) == lax.axis_index("mp"))
    vec = jnp.where(here[:, None] & side[0], vectors[:, :, None, :], 0).reshape(layers, 8, -1)
    qv = jnp.where(side[:, None, None, None] & here[:, None], qv_bias[:, :, None, :, None, :], 0).reshape(layers, 2, -1)
    up = jnp.where(side[:, None, None, None] & here[:, None], up_bias[:, None, :, None, :], 0).reshape(layers, 4, -1)
    rows = jnp.concatenate([vec, qv, up, jnp.zeros((layers, 2, vec.shape[2]), vec.dtype)], axis=1)
    return rows.reshape(layers * 16, -1)


def placement(ids):
    same = ids[:, None] == ids[None, :]
    count = jnp.sum(same, axis=1)
    order = jnp.arange(ids.shape[0])
    before = order[None, :] < order[:, None]
    long = count > 100
    kind = (long[:, None] == long[None, :]) & before
    inside = jnp.sum(same & before, axis=1)
    earlier = jnp.sum(kind, axis=1) - inside
    return jnp.where(long, jnp.where(earlier > 0, 208, 0) + inside, 416 + earlier + inside)


def on_device_fast(
    tokens, segments, qkv_weight, out_weight, up_weight, down_weight, vectors, qv_bias, up_bias, cotangent
):
    layers = qkv_weight.shape[0]
    half = tokens.shape[1]
    width = tokens.shape[2]
    place_x = lax.axis_index("mp")
    shard = jnp.concatenate(
        [qkv_weight[:, 0], qkv_weight[:, 1], qkv_weight[:, 2], jnp.swapaxes(out_weight, 1, 2),
         up_weight, jnp.swapaxes(down_weight, 1, 2)], axis=2)
    extra = ((0, 0), (0, HALF_PAD - half), (0, 0))
    ids = lax.dynamic_index_in_dim(segments, place_x, 0, keepdims=False)
    position = placement(ids)
    spread = jnp.concatenate([
        jnp.pad(position[:half], (0, HALF_PAD - half), constant_values=-1),
        jnp.pad(position[half:], (0, HALF_PAD - half), constant_values=-1)])
    to_place = (jnp.arange(PADDED)[:, None] == spread[None, :]).astype(jnp.bfloat16)
    new_ids = jnp.max(jnp.where(jnp.arange(PADDED)[:, None] == position[None, :], ids[None, :], -1), axis=1)
    other = jnp.stack([
        jnp.pad((new_ids[a:a + n][:, None] != new_ids[a:a + n][None, :]).astype(jnp.float32), ((0, 224 - n), (0, 224 - n)))
        for a, n in WINDOWS])
    whole, vec_rows, grad_in, resids, middles, result, acts, hiddens, slopes = forward_all(
        shard, spread_small(vectors, qv_bias, up_bias), jnp.pad(tokens, extra), jnp.pad(cotangent, extra), to_place, other)
    summed, small, out_rows, grad_rows, _ = backward_all(
        whole, vec_rows, grad_in, resids, middles, result, acts, hiddens, slopes, to_place, other)
    summed = summed.astype(jnp.float32)
    small = small.reshape(layers, 16, width)
    dp = lax.axis_index("dp")
    vec = lax.dynamic_index_in_dim(small[:, :8].reshape(layers, 8, -1, 64), dp, 2, keepdims=False)
    qv = small[:, 8:10].reshape(layers, 2, NX, -1, NZ * NY * NC, 4)
    qv = lax.dynamic_index_in_dim(lax.dynamic_index_in_dim(qv, dp, 4, keepdims=False), place_x, 2, keepdims=False)
    up = small[:, 10:14].reshape(layers, NX, -1, NZ * NY * NC, 4)
    up = lax.dynamic_index_in_dim(lax.dynamic_index_in_dim(up, dp, 3, keepdims=False), place_x, 1, keepdims=False)
    return (
        out_rows[:, :half],
        grad_rows[:, :half].astype(jnp.float32),
        jnp.stack([summed[:, :, 0:512], summed[:, :, 512:1024], summed[:, :, 1024:1536]], axis=1),
        jnp.swapaxes(summed[:, :, 1536:2048], 1, 2),
        summed[:, :, 2048:4096],
        jnp.swapaxes(summed[:, :, 4096:], 1, 2),
        vec,
        qv,
        up,
    )


def solution(mesh):
    placed = (
        P(None, ("dp", "mp"), None),
        P(None, "dp"),
        P(None, None, "dp", "mp"),
        P(None, "mp", "dp"),
        P(None, "dp", "mp"),
        P(None, "mp", "dp"),
        P(None, None, "dp"),
        P(None, None, "mp", "dp"),
        P(None, "mp", "dp"),
        P(None, ("dp", "mp"), None),
    )
    fast = dict(mesh.shape) == {"dp": NZ * NY * NC, "mp": NX}
    return jax.shard_map(
        on_device_fast if fast else on_device,
        mesh=mesh,
        in_specs=placed,
        out_specs=(
            P(None, ("dp", "mp"), None),
            P(None, ("dp", "mp"), None),
            P(None, None, "dp", "mp"),
            P(None, "mp", "dp"),
            P(None, "dp", "mp"),
            P(None, "mp", "dp"),
            P(None, None, "dp"),
            P(None, None, "mp", "dp"),
            P(None, "mp", "dp"),
        ),
        check_vma=False,
    )
```

```python
import functools
import math

import jax
import jax.numpy as jnp
from jax import lax
from jax.experimental import pallas as pl
from jax.experimental.pallas import tpu as pltpu
from jax.sharding import PartitionSpec as P

INV_ROOT_TWO = 0.7071067811865476
INV_ROOT_TAU = 0.3989422804014327


def layer_norm(values, gain, shift):
    centred = values - jnp.mean(values, axis=-1, keepdims=True)
    inverse = lax.rsqrt(jnp.mean(centred * centred, axis=-1, keepdims=True) + 1e-06)
    normed = centred * inverse
    return (normed * gain + shift, normed, inverse)


def norm_backward(upstream, normed, inverse, gain):
    scaled = upstream * gain
    inner = (
        scaled
        - jnp.mean(scaled, axis=-1, keepdims=True)
        - normed * jnp.mean(scaled * normed, axis=-1, keepdims=True)
    )
    return (inverse * inner, jnp.sum(upstream * normed, axis=0), jnp.sum(upstream, axis=0))


def contract_rows(left, right):
    return lax.dot_general(
        left, right, (((0,), (0,)), ((), ())), preferred_element_type=jnp.float32
    )


def against_rows(left, right):
    return lax.dot_general(
        left, right, (((1,), (1,)), ((), ())), preferred_element_type=jnp.float32
    )


def gather_normed(values):
    return lax.all_gather(values, "mp", axis=0, tiled=True)


def gather_upstream(values):
    return lax.all_gather(values, "mp", axis=0, tiled=True)


def branch_sum(term, count):
    return lax.psum_scatter(
        term(jnp.int32(0), count * lax.axis_size("mp")).astype(jnp.bfloat16),
        "mp",
        scatter_dimension=0,
        tiled=True,
    ).astype(jnp.float32)


def input_sum(term, count):
    return lax.psum_scatter(
        term(jnp.int32(0), count * lax.axis_size("mp")).astype(jnp.bfloat16),
        "mp",
        scatter_dimension=0,
        tiled=True,
    ).astype(jnp.float32)


def on_device(
    tokens,
    segments,
    qkv_weight,
    out_weight,
    up_weight,
    down_weight,
    vectors,
    qv_bias,
    up_bias,
    cotangent,
):
    layers = qkv_weight.shape[0]
    micro = tokens.shape[0]
    width = tokens.shape[2]
    head_dim = qv_bias.shape[3] * lax.axis_size("dp")
    scale = 1.0 / math.sqrt(head_dim)

    def attention_scores(query, keys, same_crop, heads):
        total_rows = query.shape[0]
        raw = (
            jnp.einsum(
                "qhd,khd->hqk",
                query.reshape(total_rows, heads, -1),
                keys.reshape(total_rows, heads, -1),
                preferred_element_type=jnp.float32,
            )
            * scale
        )
        return jnp.where(same_crop, raw, -1000000000.0)

    def forward_layer(resid, same_crop, whole):
        qkv_full, out_full, up_full, down_full, vector_half, qv_full, up_shift = whole
        vector_rows = vector_half.astype(jnp.float32)
        normed_in, first_normed, first_inverse = layer_norm(resid, vector_rows[0], vector_rows[1])
        first_all = gather_normed(normed_in.astype(jnp.bfloat16))
        total_rows = first_all.shape[0]
        heads = qv_full.shape[1]
        qv_flat = qv_full.astype(jnp.float32).reshape(2, -1)
        query = (
            jnp.dot(first_all, qkv_full[0], preferred_element_type=jnp.float32) + qv_flat[0]
        ).astype(jnp.bfloat16)
        keys = jnp.dot(first_all, qkv_full[1], preferred_element_type=jnp.float32).astype(
            jnp.bfloat16
        )
        values = (
            jnp.dot(first_all, qkv_full[2], preferred_element_type=jnp.float32) + qv_flat[1]
        ).astype(jnp.bfloat16)
        scores = attention_scores(query, keys, same_crop, heads)
        peak = jnp.max(scores, axis=-1, keepdims=True)
        powers = jnp.exp(scores - peak)
        totals = jnp.sum(powers, axis=-1, keepdims=True)
        probs = (powers / totals).astype(jnp.bfloat16)
        log_totals = peak + jnp.log(totals)
        attended = (
            jnp.einsum(
                "hqk,khd->qhd",
                probs,
                values.reshape(total_rows, heads, -1),
                preferred_element_type=jnp.float32,
            )
            .reshape(total_rows, -1)
            .astype(jnp.bfloat16)
        )

        def project_rows(start, size):
            return jnp.dot(attended, out_full, preferred_element_type=jnp.float32)

        projected = branch_sum(project_rows, resid.shape[0])
        middle = resid + vector_rows[3] * (projected + vector_rows[2])
        normed_mid, second_normed, second_inverse = layer_norm(
            middle, vector_rows[4], vector_rows[5]
        )
        second_all = gather_normed(normed_mid.astype(jnp.bfloat16))
        hidden_pre = jnp.dot(
            second_all, up_full, preferred_element_type=jnp.float32
        ) + up_shift.astype(jnp.float32).reshape(-1)
        hidden = (0.5 * hidden_pre * (1.0 + lax.erf(hidden_pre * INV_ROOT_TWO))).astype(
            jnp.bfloat16
        )

        def down_rows(start, size):
            return jnp.dot(hidden, down_full, preferred_element_type=jnp.float32)

        returned = branch_sum(down_rows, resid.shape[0])
        result = middle + vector_rows[7] * (returned + vector_rows[6])
        saved = (
            first_normed,
            first_inverse,
            first_all,
            query,
            keys,
            values,
            log_totals,
            attended,
            projected,
            second_normed,
            second_inverse,
            second_all,
            hidden_pre,
            hidden,
            returned,
        )
        return (result, saved)

    def backward_layer(upstream, same_crop, whole, saved):
        qkv_full, out_full, up_full, down_full, vector_half, qv_full, up_shift = whole
        (
            first_normed,
            first_inverse,
            first_all,
            query,
            keys,
            values,
            log_totals,
            attended,
            projected,
            second_normed,
            second_inverse,
            second_all,
            hidden_pre,
            hidden,
            returned,
        ) = saved
        vector_rows = vector_half.astype(jnp.float32)
        count = upstream.shape[0]
        total_rows = first_all.shape[0]
        heads = qv_full.shape[1]
        scaled_up = vector_rows[7] * upstream
        grad_shift_mlp = jnp.sum(scaled_up, axis=0)
        grad_scale_mlp = jnp.sum(upstream * (returned + vector_rows[6]), axis=0)
        returned_all = gather_upstream(scaled_up.astype(jnp.bfloat16))
        grad_down = contract_rows(hidden, returned_all)
        grad_hidden = against_rows(returned_all, down_full)
        normal_cdf = 0.5 * (1.0 + lax.erf(hidden_pre * INV_ROOT_TWO))
        normal_pdf = jnp.exp(-0.5 * hidden_pre * hidden_pre) * INV_ROOT_TAU
        grad_pre = (grad_hidden * (normal_cdf + hidden_pre * normal_pdf)).astype(jnp.bfloat16)
        grad_up_shift = jnp.sum(grad_pre.astype(jnp.float32), axis=0).reshape(-1, head_dim)
        grad_up = contract_rows(second_all, grad_pre)

        def up_rows(start, size):
            return against_rows(lax.dynamic_slice_in_dim(grad_pre, start, size, 0), up_full)

        grad_second = input_sum(up_rows, count)
        grad_mid_norm, grad_gain_two, grad_shift_two = norm_backward(
            grad_second, second_normed, second_inverse, vector_rows[4]
        )
        grad_middle = upstream + grad_mid_norm
        scaled_mid = vector_rows[3] * grad_middle
        grad_shift_attn = jnp.sum(scaled_mid, axis=0)
        grad_scale_attn = jnp.sum(grad_middle * (projected + vector_rows[2]), axis=0)
        projected_all = gather_upstream(scaled_mid.astype(jnp.bfloat16))
        grad_out = contract_rows(attended, projected_all)
        grad_attended = (
            against_rows(projected_all, out_full)
            .astype(jnp.bfloat16)
            .reshape(total_rows, heads, -1)
        )
        query_heads = query.reshape(total_rows, heads, -1)
        key_heads = keys.reshape(total_rows, heads, -1)
        value_heads = values.reshape(total_rows, heads, -1)
        scores = attention_scores(query, keys, same_crop, heads)
        probs = jnp.exp(scores - log_totals)
        grad_values = jnp.einsum(
            "hqk,qhd->khd",
            probs.astype(jnp.bfloat16),
            grad_attended,
            preferred_element_type=jnp.float32,
        )
        grad_probs = jnp.einsum(
            "qhd,khd->hqk", grad_attended, value_heads, preferred_element_type=jnp.float32
        )
        grad_scores = (
            probs * (grad_probs - jnp.sum(probs * grad_probs, axis=-1, keepdims=True))
        ).astype(jnp.bfloat16)
        grad_query = (
            jnp.einsum("hqk,khd->qhd", grad_scores, key_heads, preferred_element_type=jnp.float32)
            * scale
        )
        grad_keys = (
            jnp.einsum("hqk,qhd->khd", grad_scores, query_heads, preferred_element_type=jnp.float32)
            * scale
        )
        grad_project = (
            jnp.stack([grad_query, grad_keys, grad_values])
            .reshape(3, total_rows, -1)
            .astype(jnp.bfloat16)
        )
        grad_qv = jnp.stack(
            [
                jnp.sum(grad_project[0].astype(jnp.float32), axis=0),
                jnp.sum(grad_project[2].astype(jnp.float32), axis=0),
            ]
        ).reshape(2, heads, head_dim)
        grad_qkv = jnp.einsum(
            "rd,trc->tdc", first_all, grad_project, preferred_element_type=jnp.float32
        )

        def qkv_rows(start, size):
            return jnp.einsum(
                "trc,tdc->rd",
                lax.dynamic_slice_in_dim(grad_project, start, size, 1),
                qkv_full,
                preferred_element_type=jnp.float32,
            )

        grad_first = input_sum(qkv_rows, count)
        grad_in_norm, grad_gain_one, grad_shift_one = norm_backward(
            grad_first, first_normed, first_inverse, vector_rows[0]
        )
        grad_vectors = jnp.stack(
            [
                grad_gain_one,
                grad_shift_one,
                grad_shift_attn,
                grad_scale_attn,
                grad_gain_two,
                grad_shift_two,
                grad_shift_mlp,
                grad_scale_mlp,
            ]
        )
        parts = (grad_qkv, grad_out, grad_up, grad_down, grad_vectors, grad_qv, grad_up_shift)
        return (grad_middle + grad_in_norm, parts)

    shapes = [
        (3, width, qkv_weight.shape[3]),
        (out_weight.shape[1], width),
        (width, up_weight.shape[2]),
        (down_weight.shape[1], width),
        (8, width),
        (2, qv_bias.shape[2], head_dim),
        (up_bias.shape[1], head_dim),
    ]
    zeroed = tuple((jnp.zeros(shape, jnp.float32) for shape in shapes))
    start_sums = tuple((zeroed for layer in range(layers)))

    def one_micro(index, carry):
        sums, out_buffer, grad_buffer = carry
        resid = lax.dynamic_index_in_dim(tokens, index, 0, keepdims=False).astype(jnp.float32)
        crop_ids = lax.dynamic_index_in_dim(segments, index, 0, keepdims=False)
        same_crop = (crop_ids[:, None] == crop_ids[None, :])[None]
        wholes = []
        saves = []
        for layer in range(layers):
            whole = (
                lax.all_gather(qkv_weight[layer], "dp", axis=1, tiled=True),
                lax.all_gather(out_weight[layer], "dp", axis=1, tiled=True),
                lax.all_gather(up_weight[layer], "dp", axis=0, tiled=True),
                lax.all_gather(down_weight[layer], "dp", axis=1, tiled=True),
                lax.all_gather(vectors[layer], "dp", axis=1, tiled=True),
                lax.all_gather(qv_bias[layer], "dp", axis=2, tiled=True),
                lax.all_gather(up_bias[layer], "dp", axis=1, tiled=True),
            )
            resid, saved = forward_layer(resid, same_crop, whole)
            wholes.append(whole)
            saves.append(saved)
        out_buffer = lax.dynamic_update_index_in_dim(
            out_buffer, resid.astype(jnp.bfloat16), index, 0
        )
        upstream = lax.dynamic_index_in_dim(cotangent, index, 0, keepdims=False).astype(jnp.float32)
        new_sums = list(sums)
        for layer in reversed(range(layers)):
            whole = (
                lax.all_gather(qkv_weight[layer], "dp", axis=1, tiled=True),
                lax.all_gather(out_weight[layer], "dp", axis=1, tiled=True),
                lax.all_gather(up_weight[layer], "dp", axis=0, tiled=True),
                lax.all_gather(down_weight[layer], "dp", axis=1, tiled=True),
                lax.all_gather(vectors[layer], "dp", axis=1, tiled=True),
                lax.all_gather(qv_bias[layer], "dp", axis=2, tiled=True),
                lax.all_gather(up_bias[layer], "dp", axis=1, tiled=True),
            )
            upstream, parts = backward_layer(upstream, same_crop, whole, saves[layer])
            new_sums[layer] = tuple((total + piece for total, piece in zip(sums[layer], parts)))
        grad_buffer = lax.dynamic_update_index_in_dim(grad_buffer, upstream, index, 0)
        return (tuple(new_sums), out_buffer, grad_buffer)

    start = (
        start_sums,
        jnp.zeros(tokens.shape, jnp.bfloat16),
        jnp.zeros(tokens.shape, jnp.float32),
    )
    sums, output, tokens_grad = lax.fori_loop(0, micro, one_micro, start)
    reduced = []
    for layer in range(layers):
        totals = sums[layer]
        totals = (
            lax.psum_scatter(
                totals[0].astype(jnp.bfloat16), "dp", scatter_dimension=1, tiled=True
            ).astype(jnp.float32),
            lax.psum_scatter(
                totals[1].astype(jnp.bfloat16), "dp", scatter_dimension=1, tiled=True
            ).astype(jnp.float32),
            lax.psum_scatter(
                totals[2].astype(jnp.bfloat16), "dp", scatter_dimension=0, tiled=True
            ).astype(jnp.float32),
            lax.psum_scatter(
                totals[3].astype(jnp.bfloat16), "dp", scatter_dimension=1, tiled=True
            ).astype(jnp.float32),
            lax.psum_scatter(
                totals[4].astype(jnp.bfloat16), "dp", scatter_dimension=1, tiled=True
            ).astype(jnp.float32),
            lax.psum_scatter(
                totals[5].astype(jnp.bfloat16), "dp", scatter_dimension=2, tiled=True
            ).astype(jnp.float32),
            lax.psum_scatter(
                totals[6].astype(jnp.bfloat16), "dp", scatter_dimension=1, tiled=True
            ).astype(jnp.float32),
        )
        reduced.append(totals)
    stacked = [
        jnp.stack([reduced[layer][member] for layer in range(layers)]) for member in range(7)
    ]
    vector_total = lax.psum(stacked[4], "mp")
    return (
        output,
        tokens_grad,
        stacked[0],
        stacked[1],
        stacked[2],
        stacked[3],
        vector_total,
        stacked[5],
        stacked[6],
    )


MESH = pl.DeviceIdType.MESH
NZ, NY, NC, NX = 4, 2, 2, 2
SHARD = 64
COLS = 6144
CHUNK = 1024
PER_LAYER = COLS // CHUNK
ROUTES = (("zxy", 0, 16, 0, 1024), ("yzx", 16, 48, 0, 512), ("xzy", 16, 48, 512, 512))
LAG = 2


class Place:
    def __init__(self):
        dp = lax.axis_index("dp")
        self.x = lax.axis_index("mp")
        self.z = dp // 4
        self.y = lax.rem(dp // 2, 2)
        self.c = lax.rem(dp, 2)

    def device(self, x=None, z=None, y=None, c=None):
        x = self.x if x is None else x
        z = self.z if z is None else z
        y = self.y if y is None else y
        c = self.c if c is None else c
        return (z * 4 + y * 2 + c, x)

    def other(self, axis):
        if axis == "x":
            return self.device(x=1 - self.x)
        if axis == "y":
            return self.device(y=1 - self.y)
        return self.device(c=1 - self.c)

    def along(self, k):
        return lax.rem(self.z + k, NZ)


def greet(place):
    barrier = pltpu.get_barrier_semaphore()
    for axis in "cxy":
        pl.semaphore_signal(barrier, inc=1, device_id=place.other(axis), device_id_type=MESH)
    for k in (1, 2, 3):
        pl.semaphore_signal(
            barrier, inc=1, device_id=place.device(z=place.along(k)), device_id_type=MESH
        )
    pl.semaphore_wait(barrier, 6)


def block(place, filled, z=None):
    return (
        slice(None) if "x" in filled else place.x,
        slice(None) if "z" in filled else (place.z if z is None else z),
        slice(None) if "y" in filled else place.y,
        place.c,
    )


class Spread:
    def __init__(self, place, axis, source, target, send, recv, base):
        self.place, self.axis = place, axis
        self.source, self.target = source, target
        self.send, self.recv, self.base = send, recv, base

    def single(self):
        return pltpu.make_async_remote_copy(
            src_ref=self.source, dst_ref=self.target(None),
            send_sem=self.send(self.base), recv_sem=self.recv(self.base),
            device_id=self.place.other(self.axis), device_id_type=MESH)

    def direct(self, k):
        place = self.place
        return pltpu.make_async_remote_copy(
            src_ref=self.source, dst_ref=self.target(None),
            send_sem=self.send(self.base + k), recv_sem=self.recv(self.base + place.z),
            device_id=place.device(z=place.along(k)), device_id_type=MESH)

    def arrival(self, z):
        place = self.place
        return pltpu.make_async_remote_copy(
            src_ref=self.source, dst_ref=self.target(z),
            send_sem=self.send(self.base), recv_sem=self.recv(self.base + z),
            device_id=place.device(z=z), device_id_type=MESH)

    def passed(self):
        place = self.place
        origin = jnp.where(place.z == 2, 0, 3)
        return origin, pltpu.make_async_remote_copy(
            src_ref=self.target(origin), dst_ref=self.target(origin),
            send_sem=self.send(self.base), recv_sem=self.recv(self.base + origin),
            device_id=place.device(z=3 - origin), device_id_type=MESH)

    def start(self):
        if self.axis != "z":
            self.single().start()
            return
        for k in (1, 2, 3):
            if k == 2:
                self.direct(k).start()
            else:
                @pl.when(self.place.z != (3 if k == 1 else 0))
                def _():
                    self.direct(k).start()

    def relay(self):
        if self.axis != "z":
            return

        @pl.when((self.place.z == 1) | (self.place.z == 2))
        def _():
            origin, copy = self.passed()
            self.arrival(origin).wait_recv()
            copy.start()

    def arrive(self):
        if self.axis != "z":
            self.single().wait_recv()
            return
        z = self.place.z
        inner = (z == 1) | (z == 2)
        far = jnp.where(z == 2, 0, 3)
        for k in (1, 2, 3):
            origin = lax.rem(z + k, NZ)

            @pl.when(jnp.logical_not(inner & (origin == far)))
            def _():
                self.arrival(origin).wait_recv()

    def finish(self):
        if self.axis != "z":
            self.single().wait_send()
            return
        for k in (1, 2, 3):
            if k == 2:
                self.direct(k).wait_send()
            else:
                @pl.when(self.place.z != (3 if k == 1 else 0))
                def _():
                    self.direct(k).wait_send()

        @pl.when((self.place.z == 1) | (self.place.z == 2))
        def _():
            self.passed()[1].wait_send()


class Gather:
    def __init__(self, place, chunks, shard, whole, send, recv, sib, local):
        self.place, self.chunks = place, chunks
        self.shard, self.whole = shard, whole
        self.send, self.recv, self.sib, self.local = send, recv, sib, local

    def spot(self, step):
        return step // PER_LAYER, lax.rem(step, PER_LAYER) * CHUNK

    def spread(self, step, route, phase):
        order, row, rows, col, cols = ROUTES[route]
        layer, first = self.spot(step)
        area = (pl.ds(row, rows), pl.ds(pl.multiple_of(first + col, 128), cols))
        filled = order[:phase]
        target = lambda z: self.whole.at[(layer,) + block(self.place, filled, z) + area]
        source = self.shard.at[(layer,) + area] if phase == 0 else target(None)
        axis = order[phase]
        base = {"z": 0, "y": 4, "x": 5}[axis]
        return Spread(
            self.place, axis, source, target,
            lambda slot: self.send.at[step, route, slot], lambda slot: self.recv.at[step, route, slot], base)

    def own(self, step):
        layer, first = self.spot(step)
        cols = pl.ds(pl.multiple_of(first, CHUNK), CHUNK)
        return pltpu.make_async_copy(
            self.shard.at[layer, :, cols],
            self.whole.at[(layer,) + block(self.place, "") + (slice(None), cols)], self.local.at[step])

    def sibling(self, step):
        layer, first = self.spot(step)
        cols = pl.ds(pl.multiple_of(first, CHUNK), CHUNK)
        part = self.whole.at[(layer,) + block(self.place, "xyz") + (slice(None), cols)]
        return pltpu.make_async_remote_copy(
            src_ref=part, dst_ref=part, send_sem=self.sib.at[0, step], recv_sem=self.sib.at[1, step],
            device_id=self.place.other("c"), device_id_type=MESH)

    def phase(self, step, number):
        every = range(len(ROUTES))
        if number == 0:
            self.own(step).start()
        if number == 1:
            self.own(step).wait()
        for route in every:
            if 1 <= number <= 3:
                self.spread(step, route, number - 1).arrive()
            if number <= 2:
                self.spread(step, route, number).start()
        if number == 3:
            self.sibling(step).start()
        if number == 4:
            self.sibling(step).wait()
            for route in every:
                for phase in range(3):
                    self.spread(step, route, phase).finish()

    def tick(self, step):
        for number in range(5):
            at = step - LAG * number

            @pl.when((at >= 0) & (at < self.chunks))
            def _():
                self.phase(at, number)
            if number < 3:
                early = step - LAG * number - 1

                @pl.when((early >= 0) & (early < self.chunks))
                def _():
                    for route in range(len(ROUTES)):
                        self.spread(early, route, number).relay()

    @property
    def ticks(self):
        return self.chunks + 4 * LAG


def ag_kernel(chunks, shard, small, tokens, cotangent, whole, small_all, mine, mine_grad, send, recv, sib, local, odd):
    place = Place()
    greet(place)
    gather = Gather(place, chunks, shard, whole, send, recv, sib, local)

    def halves(n, source, target):
        return (
            pltpu.make_async_remote_copy(
                src_ref=source.at[1 - place.x], dst_ref=target.at[place.x],
                send_sem=odd.at[4 * n], recv_sem=odd.at[4 * n + 1],
                device_id=place.other("x"), device_id_type=MESH),
            pltpu.make_async_copy(source.at[place.x], target.at[place.x], odd.at[4 * n + 2]),
        )

    order = "zyx"

    def small_spread(phase):
        target = lambda z: small_all.at[block(place, order[:phase], z)]
        base = {"z": 0, "y": 4, "x": 5}[order[phase]]
        return Spread(
            place, order[phase], small if phase == 0 else target(None), target,
            lambda slot: odd.at[8 + slot], lambda slot: odd.at[16 + slot], base)

    part = small_all.at[block(place, "xyz")]
    small_sibling = pltpu.make_async_remote_copy(
        src_ref=part, dst_ref=part, send_sem=odd.at[24], recv_sem=odd.at[25],
        device_id=place.other("c"), device_id_type=MESH)
    small_own = pltpu.make_async_copy(small, small_all.at[block(place, "")], odd.at[26])
    token_copies = halves(0, tokens, mine)
    grad_copies = halves(1, cotangent, mine_grad)
    for copy in token_copies:
        copy.start()
    small_own.start()
    small_spread(0).start()

    def tick(step, carry):
        @pl.when(step == 1)
        def _():
            small_spread(0).relay()
            small_own.wait()

        for phase in (1, 2):
            @pl.when(step == 1 + phase)
            def _():
                small_spread(phase - 1).arrive()
                small_spread(phase).start()

        @pl.when(step == 4)
        def _():
            small_spread(2).arrive()
            small_sibling.start()
        gather.tick(step)

        @pl.when(step == chunks // 2)
        def _():
            for copy in grad_copies:
                copy.start()
        return carry

    lax.fori_loop(0, gather.ticks, tick, 0)
    small_sibling.wait()
    for phase in range(3):
        small_spread(phase).finish()
    for copy in token_copies + grad_copies:
        copy.wait()


def gather_all(shard, small, tokens, cotangent):
    layers = shard.shape[0]
    chunks = layers * PER_LAYER
    half = tokens.shape
    any_spec = pl.BlockSpec(memory_space=pl.ANY)
    return pl.pallas_call(
        functools.partial(ag_kernel, chunks),
        out_shape=(
            jax.ShapeDtypeStruct((layers, NX, NZ, NY, NC, SHARD, COLS), jnp.bfloat16),
            jax.ShapeDtypeStruct((NX, NZ, NY, NC) + small.shape, small.dtype),
            jax.ShapeDtypeStruct(half, jnp.bfloat16),
            jax.ShapeDtypeStruct(half, jnp.bfloat16),
        ),
        in_specs=[pl.BlockSpec(memory_space=pltpu.VMEM)] * 4,
        out_specs=(any_spec,) * 4,
        scratch_shapes=[
            pltpu.SemaphoreType.DMA((chunks, len(ROUTES), 6)),
            pltpu.SemaphoreType.DMA((chunks, len(ROUTES), 6)),
            pltpu.SemaphoreType.DMA((2, chunks)),
            pltpu.SemaphoreType.DMA((chunks,)),
            pltpu.SemaphoreType.DMA((32,)),
        ],
        compiler_params=pltpu.CompilerParams(collective_id=1, has_side_effects=True, vmem_limit_bytes=32 * 1024 * 1024),
        name="gather_all",
    )(shard, small, tokens, cotangent)
SLOTS = 5


class Scatter:
    def __init__(self, place, chunks, grads, summed, acc, near, first, second, third, send, recv, local, free):
        self.place, self.chunks = place, chunks
        self.grads, self.summed = grads, summed
        self.acc, self.near = acc, near
        self.landing = (first, second, third)
        self.send, self.recv, self.local, self.free = send, recv, local, free

    def spot(self, step):
        chunk = self.chunks - 1 - step
        return chunk // PER_LAYER, pl.multiple_of(lax.rem(chunk, PER_LAYER) * CHUNK, CHUNK)

    def slot(self, step):
        return lax.rem(step, SLOTS)

    def core_copies(self, step):
        layer, first = self.spot(step)
        cols = pl.ds(first, CHUNK)
        slot = self.slot(step)
        return (
            pltpu.make_async_remote_copy(
                src_ref=self.grads.at[layer, :, :, :, 1 - self.place.c, :, cols], dst_ref=self.acc.at[slot],
                send_sem=self.send.at[step, len(ROUTES), 0], recv_sem=self.recv.at[step, len(ROUTES), 0],
                device_id=self.place.other("c"), device_id_type=MESH),
            pltpu.make_async_copy(
                self.grads.at[layer, :, :, :, self.place.c, :, cols], self.near, self.local.at[step]),
        )

    def core_add(self, step):
        slot = self.slot(step)

        def one(n, carry):
            x, z, y = n // 8, lax.rem(n // 2, 4), lax.rem(n, 2)
            self.acc[slot, x, z, y] = self.acc[slot, x, z, y] + self.near[x, z, y]
            return carry

        lax.fori_loop(0, NX * NZ * NY, one, 0)

    def area(self, route):
        _, row, rows, col, cols = ROUTES[route]
        return (pl.ds(row, rows), pl.ds(col, cols))

    def index(self, route, phase, over):
        order = ROUTES[route][0]
        left = order[:2 - phase]
        place = self.place
        picked = []
        for axis, own in (("x", place.x), ("z", place.z), ("y", place.y)):
            picked.append(over[axis] if axis in over else (slice(None) if axis in left else own))
        return tuple(picked)

    def copy(self, step, route, phase, over, device, source_slot, sem):
        slot = self.slot(step)
        axis = ROUTES[route][0][2 - phase]
        land = self.landing[phase][route].at[slot]
        if axis == "z":
            land = land.at[source_slot]
        base = {"z": 0, "y": 4, "x": 5}[axis]
        return pltpu.make_async_remote_copy(
            src_ref=self.acc.at[(slot,) + self.index(route, phase, over) + self.area(route)], dst_ref=land,
            send_sem=self.send.at[step, route, base + sem], recv_sem=self.recv.at[step, route, base + source_slot],
            device_id=device, device_id_type=MESH)

    def single(self, step, route, phase):
        axis = ROUTES[route][0][2 - phase]
        own = self.place.x if axis == "x" else self.place.y
        return self.copy(step, route, phase, {axis: 1 - own}, self.place.other(axis), 0, 0)

    def along(self, step, route, phase, k):
        place = self.place
        z = place.along(k)
        far = (place.z + z == 3) & ((place.z == 0) | (place.z == 3))
        via = jnp.where(far, jnp.where(place.z == 0, 1, 2), z)
        return self.copy(
            step, route, phase, {"z": z}, place.device(z=via), jnp.where(far, via, place.z), k)

    def arrival(self, step, route, phase, z):
        return self.copy(step, route, phase, {"z": self.place.z}, self.place.device(z=lax.rem(z + 1, NZ)), z, 1)

    def start(self, step, route, phase):
        if ROUTES[route][0][2 - phase] != "z":
            self.single(step, route, phase).start()
            return
        z = self.place.z
        for k in (1, 2, 3):
            if k == 2:
                @pl.when((z == 0) | (z == 3))
                def _():
                    self.along(step, route, phase, k).start()
            else:
                self.along(step, route, phase, k).start()

    def relay(self, step, route, phase):
        if ROUTES[route][0][2 - phase] != "z":
            return
        z = self.place.z
        slot = self.slot(step)

        @pl.when((z == 1) | (z == 2))
        def _():
            self.arrival(step, route, phase, z).wait_recv()
            far = lax.rem(z + 2, NZ)
            at = (slot,) + self.index(route, phase, {"z": far}) + self.area(route)
            self.acc[at] = self.acc[at] + self.landing[phase][route][slot, z]
            self.along(step, route, phase, 2).start()

    def arrive(self, step, route, phase):
        slot = self.slot(step)
        area = self.area(route)
        axis = ROUTES[route][0][2 - phase]
        land = self.landing[phase][route]
        if axis != "z":
            self.single(step, route, phase).wait_recv()
            at = self.index(route, phase, {axis: self.place.x if axis == "x" else self.place.y})
            lead = [n for n, entry in enumerate(at) if isinstance(entry, slice)]
            extents = [(NX, NZ, NY)[n] for n in lead]
            total = 1
            for extent in extents:
                total *= extent

            def one(n, carry):
                part = []
                for extent in reversed(extents):
                    part.append(lax.rem(n, extent))
                    n = n // extent
                part.reverse()
                full = list(at)
                for position, value in zip(lead, part):
                    full[position] = value
                self.acc[(slot,) + tuple(full) + area] = (
                    self.acc[(slot,) + tuple(full) + area] + land[(slot,) + tuple(part)])
                return carry

            if total == 1:
                one(0, 0)
            else:
                lax.fori_loop(0, total, one, 0)
            return
        z = self.place.z
        ends = (z == 0) | (z == 3)
        at = (slot,) + self.index(route, phase, {"z": z}) + area
        for k in (1, 2, 3):
            origin = lax.rem(z + k, NZ)

            @pl.when(jnp.logical_not(ends & (z + origin == 3)))
            def _():
                self.arrival(step, route, phase, origin).wait_recv()
                self.acc[at] = self.acc[at] + land[slot, origin]

    def finish(self, step, route, phase):
        if ROUTES[route][0][2 - phase] != "z":
            self.single(step, route, phase).wait_send()
            return
        for k in (1, 2, 3):
            self.along(step, route, phase, k).wait_send()

    def others(self):
        place = self.place
        pairs = [(place.other(axis), n, n) for n, axis in enumerate("cxy")]
        for k in (1, 2, 3):
            z = place.along(k)
            pairs.append((place.device(z=z), 3 + place.z, 3 + z))
        return pairs

    def phase(self, step, number):
        every = range(len(ROUTES))
        if number == 0:
            @pl.when(step >= SLOTS)
            def _():
                for _, _, mine in self.others():
                    pl.semaphore_wait(self.free.at[mine], 1)
            for copy in self.core_copies(step):
                copy.start()
            return
        if number == 1:
            remote, own = self.core_copies(step)
            own.wait()
            remote.wait_recv()
            self.core_add(step)
        for route in every:
            if number >= 2:
                self.arrive(step, route, number - 2)
            if number <= 3:
                self.start(step, route, number - 1)
        if number == 4:
            slot = self.slot(step)
            layer, first = self.spot(step)
            place = self.place
            self.store(layer, lax.rem(self.chunks - 1 - step, PER_LAYER), self.acc[slot, place.x, place.z, place.y])
            self.core_copies(step)[0].wait_send()
            for route in every:
                for phase in range(3):
                    self.finish(step, route, phase)

            @pl.when(step + SLOTS < self.chunks)
            def _():
                for device, there, _ in self.others():
                    pl.semaphore_signal(self.free.at[there], inc=1, device_id=device, device_id_type=MESH)

    def store(self, layer, chunk, values):
        qkv, out, up, down = self.summed
        side = CHUNK // 2

        @pl.when(chunk == 0)
        def _():
            qkv[layer, 0] = values[:, :side]
            qkv[layer, 1] = values[:, side:]

        @pl.when(chunk == 1)
        def _():
            qkv[layer, 2] = values[:, :side]
            out[layer] = values[:, side:].astype(jnp.float32).T.astype(jnp.bfloat16)

        @pl.when((chunk == 2) | (chunk == 3))
        def _():
            up[layer, :, pl.ds(pl.multiple_of((chunk - 2) * CHUNK, CHUNK), CHUNK)] = values

        @pl.when(chunk >= 4)
        def _():
            down[layer, pl.ds(pl.multiple_of((chunk - 4) * CHUNK, CHUNK), CHUNK), :] = (
                values.astype(jnp.float32).T.astype(jnp.bfloat16))

    def tick(self, step):
        for number in (4, 3, 2, 1, 0):
            at = step - number

            @pl.when((at >= 0) & (at < self.chunks))
            def _():
                self.phase(at, number)

    def pass_on(self, step):
        for number in (1, 2, 3):
            at = step - number

            @pl.when((at >= 0) & (at < self.chunks))
            def _():
                for route in range(len(ROUTES)):
                    self.relay(at, route, number - 1)

    @property
    def ticks(self):
        return self.chunks + 4


def landing_shapes():
    shapes = []
    for phase in range(3):
        for order, row, rows, col, cols in ROUTES:
            left = order[:2 - phase]
            axis = order[2 - phase]
            lead = tuple(extent for name, extent in (("x", NX), ("z", NZ), ("y", NY)) if name in left)
            if axis == "z":
                lead = (NZ,) + lead
            shapes.append(pltpu.VMEM((SLOTS,) + lead + (rows, cols), jnp.bfloat16))
    return shapes


WINDOWS = ((0, 208), (208, 208), (416, 224))
PADDED = 640
HALF_PAD = 320
PAIRS = 8
STEP = 160


def swap_halves(place, source, target, odd, n):
    return (
        pltpu.make_async_remote_copy(
            src_ref=source.at[1 - place.x], dst_ref=target.at[place.x],
            send_sem=odd.at[n], recv_sem=odd.at[n + 1],
            device_id=place.other("x"), device_id_type=MESH),
        pltpu.make_async_copy(source.at[place.x], target.at[place.x], odd.at[n + 2]),
    )


class Total:
    def __init__(self, place, value, landing, send, recv, base):
        self.place, self.value, self.landing = place, value, landing
        self.send, self.recv, self.base = send, recv, base

    def copies(self, number):
        place = self.place
        if number < 3:
            slots, devices = [number], [place.other("cxy"[number])]
        else:
            slots, devices = [3, 4, 5], [place.device(z=place.along(k)) for k in (1, 2, 3)]
        return [
            pltpu.make_async_remote_copy(
                src_ref=self.value, dst_ref=self.landing.at[slot],
                send_sem=self.send.at[self.base + slot], recv_sem=self.recv.at[self.base + slot],
                device_id=device, device_id_type=MESH)
            for slot, device in zip(slots, devices)
        ]

    def start(self, number):
        for copy in self.copies(number):
            copy.start()

    def add(self, number):
        for copy in self.copies(number):
            copy.wait()
        for slot in ([number] if number < 3 else [3, 4, 5]):
            self.value[...] = self.value[...] + self.landing[slot]


def dot_nn(left, right):
    return jnp.dot(left, right, preferred_element_type=jnp.float32)


def dot_nt(left, right):
    return lax.dot_general(left, right, (((1,), (1,)), ((), ())), preferred_element_type=jnp.float32)


def dot_tn(left, right):
    return lax.dot_general(left, right, (((0,), (0,)), ((), ())), preferred_element_type=jnp.float32)


def both_heads(rows):
    left = lax.broadcasted_iota(jnp.int32, rows.shape, 1) < 64
    zero = jnp.zeros_like(rows)
    return jnp.concatenate([jnp.where(left, rows, zero), jnp.where(left, zero, rows)], axis=0)


def one_head_each(rows):
    n = rows.shape[0] // 2
    left = lax.broadcasted_iota(jnp.int32, (n, rows.shape[1]), 1) < 64
    return jnp.where(left, rows[:n], rows[n:])


def window_probs(query, keys, other, n):
    raw = dot_nt(both_heads(query), keys) * 0.125
    apart = jnp.concatenate([other[:n, :n], other[:n, :n]], axis=0) > 0.5
    raw = jnp.where(apart, -1e9, raw)
    powers = jnp.exp(raw - jnp.max(raw, axis=1, keepdims=True))
    return powers * (1.0 / jnp.sum(powers, axis=1, keepdims=True))


def row_loop(body, size=STEP):
    @pl.loop(0, PADDED // size)
    def _(n):
        body(pl.ds(pl.multiple_of(n * size, size), size))


def normed_rows(values):
    centred = values - jnp.mean(values, axis=1, keepdims=True)
    inverse = lax.rsqrt(jnp.mean(centred * centred, axis=1, keepdims=True) + 1e-06)
    return centred * inverse, inverse


class Weights:
    def __init__(self, whole, held, sem):
        self.whole, self.held, self.sem = whole, held, sem

    def copy(self, layer, chunk, x):
        return pltpu.make_async_copy(
            self.whole.at[layer, x, :, :, :, :, pl.ds(chunk * CHUNK, CHUNK)], self.held.at[x], self.sem.at[x])

    def start(self, layer, chunk):
        for x in range(NX):
            self.copy(layer, chunk, x).start()

    def wait(self, layer, chunk, x):
        self.copy(layer, chunk, x).wait()

    def get(self, x, first=0, count=CHUNK):
        return self.held[x, :, :, :, :, first:first + count].reshape(NZ * NY * NC * SHARD, count)


def fwd_kernel(
    layers, shard, small, tokens, cotangent, to_place, other,
    whole, vec_out, grad_out, resid_out, middle_out, result_out, acts_out, hidden_out, slope_out,
    mine, mine_grad, vec, small_sum, small_land, resid, normed, acts, hidden, slope, total, held,
    send, recv, sib, local, odd, small_send, small_recv, wsem, save,
):
    chunks = layers * PER_LAYER
    place = Place()
    greet(place)
    gather = Gather(place, chunks, shard, whole, send, recv, sib, local)
    weights = Weights(whole, held, wsem)
    token_copies = swap_halves(place, tokens, mine, odd, 0)
    grad_copies = swap_halves(place, cotangent, mine_grad, odd, 3)
    small_total = Total(place, small_sum, small_land, small_send, small_recv, 0)

    small_sum[...] = small[...]
    small_total.start(0)
    gather.tick(0)
    gather.tick(1)
    small_total.add(0)
    small_total.start(1)
    for copy in token_copies:
        copy.start()
    gather.tick(2)
    gather.tick(3)
    small_total.add(1)
    small_total.start(2)
    gather.tick(4)
    small_total.add(2)
    small_total.start(3)
    gather.tick(5)
    gather.tick(6)
    for copy in token_copies:
        copy.wait()
    for copy in grad_copies:
        copy.start()
    gather.tick(7)
    small_total.add(3)
    vec[...] = small_sum[...].astype(jnp.float32)
    vec_copy = pltpu.make_async_copy(vec, vec_out, save.at[12])
    vec_copy.start()
    resid[...] = dot_nn(to_place[...], mine[...].reshape(PADDED, -1))
    grad_copy = pltpu.make_async_copy(slope.at[0], grad_out, save.at[13])

    def one_layer(layer, carry):
        base = layer * 16
        row = lambda n: vec[pl.ds(base + n, 1), :]

        def norm_into(gain, shift):
            def body(rows):
                values, _ = normed_rows(resid[rows, :])
                normed[rows, :] = (values * row(gain) + row(shift)).astype(jnp.bfloat16)
            row_loop(body)

        norm_into(0, 1)
        resid_copy = pltpu.make_async_copy(resid, resid_out.at[layer], save.at[0])
        resid_copy.start()

        @pl.when(layer == layers - 1)
        def _():
            for copy in grad_copies:
                copy.wait()
            slope[0] = dot_nn(to_place[...], mine_grad[...].reshape(PADDED, -1)).astype(jnp.bfloat16)
            grad_copy.start()
            grad_copy.wait()

        gather.tick(layer * PER_LAYER + 4 * LAG)
        weights.start(layer, 0)
        for x in range(NX):
            half = slice(x * 512, x * 512 + 512)
            weights.wait(layer, 0, x)
            both = dot_nn(normed[...], weights.get(x))
            acts[0, :, half] = (both[:, :512] + row(8)[:, half]).astype(jnp.bfloat16)
            acts[1, :, half] = both[:, 512:].astype(jnp.bfloat16)
        gather.tick(layer * PER_LAYER + 4 * LAG + 1)
        weights.start(layer, 1)
        for x in range(NX):
            half = slice(x * 512, x * 512 + 512)
            weights.wait(layer, 1, x)
            acts[2, :, half] = (dot_nn(normed[...], weights.get(x, 0, 512)) + row(9)[:, half]).astype(jnp.bfloat16)

        @pl.loop(0, PAIRS)
        def _(pair):
            lanes = pl.ds(pl.multiple_of(pair * 128, 128), 128)
            for w, (first, n) in enumerate(WINDOWS):
                rows = pl.ds(first, n)
                probs = window_probs(acts[0, rows, lanes], acts[1, rows, lanes], other[w], n)
                sums = dot_nn(probs.astype(jnp.bfloat16), acts[2, rows, lanes])
                acts[3, rows, lanes] = one_head_each(sums).astype(jnp.bfloat16)

        acts_copy = pltpu.make_async_copy(acts, acts_out.at[layer], save.at[1])
        acts_copy.start()
        total[...] = dot_nt(acts[3, :, :512], weights.get(0, 512, 512)) + dot_nt(acts[3, :, 512:], weights.get(1, 512, 512))
        resid_copy.wait()

        def to_middle(rows):
            resid[rows, :] = resid[rows, :] + row(3) * (total[rows, :] + row(2))
        row_loop(to_middle)
        middle_copy = pltpu.make_async_copy(resid, middle_out.at[layer], save.at[2])
        middle_copy.start()
        norm_into(4, 5)
        for part in range(2):
            gather.tick(layer * PER_LAYER + 4 * LAG + 2 + part)
            weights.start(layer, 2 + part)
            for x in range(NX):
                unit = x * 2 + part
                weights.wait(layer, 2 + part, x)
                total[...] = dot_nn(normed[...], weights.get(x)) + row(10 + unit)
                slope_copy = pltpu.make_async_copy(slope.at[x], slope_out.at[layer, unit], save.at[4 + x])
                if part:
                    pltpu.make_async_copy(slope.at[x], slope_out.at[layer, unit - 1], save.at[4 + x]).wait()

                def activate(rows):
                    pre = total[rows, :]
                    cdf = 0.5 * (1.0 + lax.erf(pre * INV_ROOT_TWO))
                    pdf = jnp.exp(-0.5 * pre * pre) * INV_ROOT_TAU
                    hidden[unit, rows, :] = (pre * cdf).astype(jnp.bfloat16)
                    slope[x, rows, :] = (cdf + pre * pdf).astype(jnp.bfloat16)
                row_loop(activate, 64)
                slope_copy.start()
        hidden_copy = pltpu.make_async_copy(hidden, hidden_out.at[layer], save.at[3])
        hidden_copy.start()
        for part in range(2):
            gather.tick(layer * PER_LAYER + 4 * LAG + 4 + part)
            weights.start(layer, 4 + part)
            for x in range(NX):
                weights.wait(layer, 4 + part, x)
                term = dot_nt(hidden[x * 2 + part], weights.get(x))
                if part == 0 and x == 0:
                    total[...] = term
                else:
                    total[...] = total[...] + term
        middle_copy.wait()

        def to_result(rows):
            resid[rows, :] = resid[rows, :] + row(7) * (total[rows, :] + row(6))
        row_loop(to_result)
        acts_copy.wait()
        hidden_copy.wait()
        for x in range(NX):
            pltpu.make_async_copy(slope.at[x], slope_out.at[layer, x * 2 + 1], save.at[4 + x]).wait()
        return carry

    lax.fori_loop(0, layers, one_layer, 0)
    result_copy = pltpu.make_async_copy(resid, result_out, save.at[0])
    result_copy.start()
    result_copy.wait()
    vec_copy.wait()


def forward_all(shard, small, tokens, cotangent, to_place, other):
    layers = shard.shape[0]
    width = tokens.shape[2]
    chunks = layers * PER_LAYER
    any_spec = pl.BlockSpec(memory_space=pl.ANY)
    full = (PADDED, width)
    bf16, f32 = jnp.bfloat16, jnp.float32
    return pl.pallas_call(
        functools.partial(fwd_kernel, layers),
        out_shape=(
            jax.ShapeDtypeStruct((layers, NX, NZ, NY, NC, SHARD, COLS), bf16),
            jax.ShapeDtypeStruct(small.shape, f32),
            jax.ShapeDtypeStruct(full, bf16),
            jax.ShapeDtypeStruct((layers,) + full, f32),
            jax.ShapeDtypeStruct((layers,) + full, f32),
            jax.ShapeDtypeStruct(full, f32),
            jax.ShapeDtypeStruct((layers, 4) + full, bf16),
            jax.ShapeDtypeStruct((layers, 4) + full, bf16),
            jax.ShapeDtypeStruct((layers, 4) + full, bf16),
        ),
        in_specs=[pl.BlockSpec(memory_space=pltpu.VMEM)] * 6,
        out_specs=(any_spec,) * 9,
        scratch_shapes=[
            pltpu.VMEM(tokens.shape, bf16),
            pltpu.VMEM(tokens.shape, bf16),
            pltpu.VMEM(small.shape, f32),
            pltpu.VMEM(small.shape, bf16),
            pltpu.VMEM((6,) + small.shape, bf16),
            pltpu.VMEM(full, f32),
            pltpu.VMEM(full, bf16),
            pltpu.VMEM((4,) + full, bf16),
            pltpu.VMEM((4,) + full, bf16),
            pltpu.VMEM((2,) + full, bf16),
            pltpu.VMEM(full, f32),
            pltpu.VMEM((NX, NZ, NY, NC, SHARD, CHUNK), bf16),
            pltpu.SemaphoreType.DMA((chunks, len(ROUTES), 6)),
            pltpu.SemaphoreType.DMA((chunks, len(ROUTES), 6)),
            pltpu.SemaphoreType.DMA((2, chunks)),
            pltpu.SemaphoreType.DMA((chunks,)),
            pltpu.SemaphoreType.DMA((6,)),
            pltpu.SemaphoreType.DMA((6,)),
            pltpu.SemaphoreType.DMA((6,)),
            pltpu.SemaphoreType.DMA((2,)),
            pltpu.SemaphoreType.DMA((14,)),
        ],
        compiler_params=pltpu.CompilerParams(
            collective_id=1, has_side_effects=True, vmem_limit_bytes=60 * 1024 * 1024),
        name="forward_all",
    )(shard, small, tokens, cotangent, to_place, other)


def bwd_kernel(
    layers, whole, vec, grad_in, resid_in, middle_in, result, acts_in, hidden_in, slope_in, to_place, other,
    qkv_sum, out_sum, up_sum, down_sum, small_sum, out_rows, grad_rows, grads, *scratch,
):
    n = len(ROUTES)
    acc, near = scratch[:2]
    lands = scratch[2:2 + 3 * n]
    (upstream, dy, normed, mid, total, pool, big, held, staged, rows_out, gsum, small_land,
     send, recv, local, free, odd, small_send, small_recv, wsem, load, stage) = scratch[2 + 3 * n:]
    chunks = layers * PER_LAYER
    place = Place()
    greet(place)
    scatter = Scatter(
        place, chunks, grads, (qkv_sum, out_sum, up_sum, down_sum), acc, near,
         lands[:n], lands[n:2 * n], lands[2 * n:], send, recv, local, free)
    weights = Weights(whole, held, wsem)
    out_copies = swap_halves(place, rows_out, out_rows, odd, 0)
    grad_copies = swap_halves(place, rows_out, grad_rows, odd, 3)
    small_total = Total(place, small_sum, small_land, small_send, small_recv, 0)

    def fetch(source, target, slot):
        return pltpu.make_async_copy(source, target, load.at[slot])

    def add_rows(kind, values):
        gsum[kind] = gsum[kind] + jnp.sum(values.reshape(-1, 8, values.shape[1]), axis=0)

    small_sum[...] = jnp.zeros_like(small_sum)
    copies = [fetch(result, total, 0), fetch(grad_in, dy, 1)]
    for copy in copies:
        copy.start()
    for copy in copies:
        copy.wait()
    upstream[...] = dy[...].astype(jnp.float32)
    pool[0] = total[...].astype(jnp.bfloat16)
    rows_out[...] = dot_tn(to_place[...], pool[0]).astype(jnp.bfloat16).reshape(rows_out.shape)
    for copy in out_copies:
        copy.start()

    def one_layer(turn, carry):
        layer = layers - 1 - turn
        base = layer * 16
        first_step = turn * PER_LAYER
        row = lambda n: vec[pl.ds(base + n, 1), :]
        gsum[...] = jnp.zeros_like(gsum)

        def keep(chunk, x):
            return pltpu.make_async_copy(
                staged, grads.at[layer, x, :, :, :, :, pl.ds(chunk * CHUNK, CHUNK)], stage.at[0])

        def store(first, values):
            staged[:, :, :, :, first:first + values.shape[1]] = values.astype(jnp.bfloat16).reshape(
                NZ, NY, NC, SHARD, values.shape[1])

        middle_copy = fetch(middle_in.at[layer], mid, 0)
        middle_copy.start()

        def reads(part, x):
            return (fetch(hidden_in.at[layer, x * 2 + part], pool.at[x], 4 + x),
                    fetch(slope_in.at[layer, x * 2 + part], pool.at[2 + x], 2 + x))

        for x in range(NX):
            for copy in reads(1, x):
                copy.start()
        weights.start(layer, 5)
        middle_copy.wait()

        def first_rows(rows):
            up = upstream[rows, :]
            scaled = row(7) * up
            dy[rows, :] = scaled.astype(jnp.bfloat16)
            add_rows(6, scaled)
            middle = mid[rows, :]
            add_rows(7, up * (total[rows, :] - middle))
            hat, _ = normed_rows(middle)
            normed[rows, :] = (hat * row(4) + row(5)).astype(jnp.bfloat16)
        row_loop(first_rows)

        for turn_part, part in enumerate((1, 0)):
            for x in range(NX):
                unit = x * 2 + part
                hidden_copy, slope_copy = reads(part, x)
                hidden_copy.wait()
                for side in range(2):
                    store(side * 512, dot_tn(dy[...], pool[x, :, side * 512:side * 512 + 512]))
                keep(4 + part, x).start()
                if part == 1:
                    reads(0, x)[0].start()
                weights.wait(layer, 4 + part, x)
                total[...] = dot_nn(dy[...], weights.get(x))
                weights.copy(layer, 3 + part, x).start()
                if x == 0:
                    scatter.pass_on(first_step + turn_part - 1)
                slope_copy.wait()

                def to_pre(rows):
                    grad = (total[rows, :] * pool[2 + x, rows, :].astype(jnp.float32)).astype(jnp.bfloat16)
                    big[unit, rows, :] = grad
                    add_rows(10 + unit, grad.astype(jnp.float32))
                row_loop(to_pre)
                if part == 1:
                    reads(0, x)[1].start()
                keep(4 + part, x).wait()
            scatter.tick(first_step + turn_part)
        for turn_part, part in enumerate((1, 0)):
            for x in range(NX):
                unit = x * 2 + part
                for side in range(2):
                    store(side * 512, dot_tn(normed[...], big[unit, :, side * 512:side * 512 + 512]))
                keep(2 + part, x).start()
                if x == 0:
                    scatter.pass_on(first_step + 1 + turn_part)
                weights.wait(layer, 2 + part, x)
                term = dot_nt(big[unit], weights.get(x))
                weights.copy(layer, 1 + part, x).start()
                if turn_part == 0 and x == 0:
                    total[...] = term
                else:
                    total[...] = total[...] + term
                keep(2 + part, x).wait()
            scatter.tick(first_step + 2 + turn_part)
        acts_copy = fetch(acts_in.at[layer], big, 0)
        acts_copy.start()

        def middle_rows(rows):
            grad = total[rows, :]
            hat, inverse = normed_rows(mid[rows, :])
            add_rows(4, grad * hat)
            add_rows(5, grad)
            scaled = grad * row(4)
            inner = (scaled - jnp.mean(scaled, axis=1, keepdims=True)
                     - hat * jnp.mean(scaled * hat, axis=1, keepdims=True))
            here = upstream[rows, :] + inverse * inner
            upstream[rows, :] = here
            scaled_mid = row(3) * here
            add_rows(2, scaled_mid)
            dy[rows, :] = scaled_mid.astype(jnp.bfloat16)
        row_loop(middle_rows)
        resid_copy = fetch(resid_in.at[layer], total, 1)
        resid_copy.start()
        for x in range(NX):
            weights.wait(layer, 1, x)
            pool[0, :, x * 512:x * 512 + 512] = dot_nn(dy[...], weights.get(x, 512, 512)).astype(jnp.bfloat16)
        resid_copy.wait()

        def resid_rows(rows):
            values = total[rows, :]
            add_rows(3, upstream[rows, :] * (mid[rows, :] - values))
            hat, _ = normed_rows(values)
            normed[rows, :] = (hat * row(0) + row(1)).astype(jnp.bfloat16)
        row_loop(resid_rows)
        scatter.pass_on(first_step + 3)
        acts_copy.wait()

        @pl.loop(0, PAIRS)
        def _(pair):
            lanes = pl.ds(pl.multiple_of(pair * 128, 128), 128)
            for w, (first, n) in enumerate(WINDOWS):
                rows = pl.ds(first, n)
                query, keys, values = big[0, rows, lanes], big[1, rows, lanes], big[2, rows, lanes]
                probs = window_probs(query, keys, other[w], n)
                grad = both_heads(pool[0, rows, lanes])
                pool[3, rows, lanes] = dot_tn(probs.astype(jnp.bfloat16), grad).astype(jnp.bfloat16)
                grad_probs = dot_nt(grad, values)
                inner = jnp.sum(probs * grad_probs, axis=1, keepdims=True)
                grad_scores = (probs * (grad_probs - inner)).astype(jnp.bfloat16)
                pool[1, rows, lanes] = (one_head_each(dot_nn(grad_scores, keys)) * 0.125).astype(jnp.bfloat16)
                pool[2, rows, lanes] = (dot_tn(grad_scores, both_heads(query)) * 0.125).astype(jnp.bfloat16)

        for x in range(NX):
            half = slice(x * 512, x * 512 + 512)
            store(0, dot_tn(normed[...], pool[3, :, half]))
            store(512, dot_tn(dy[...], big[3, :, half]))
            keep(1, x).start()
            term = dot_nt(pool[3, :, half], weights.get(x, 0, 512))
            weights.copy(layer, 0, x).start()
            mid[...] = term if x == 0 else mid[...] + term
            keep(1, x).wait()
        scatter.tick(first_step + 4)

        def sum_rows(rows):
            add_rows(8, pool[1, rows, :].astype(jnp.float32))
            add_rows(9, pool[3, rows, :].astype(jnp.float32))
        row_loop(sum_rows)
        for x in range(NX):
            half = slice(x * 512, x * 512 + 512)
            store(0, dot_tn(normed[...], pool[1, :, half]))
            store(512, dot_tn(normed[...], pool[2, :, half]))
            keep(0, x).start()
            if x == 0:
                scatter.pass_on(first_step + 4)
            weights.wait(layer, 0, x)
            mid[...] = mid[...] + dot_nt(pool[1, :, half], weights.get(x, 0, 512))
            mid[...] = mid[...] + dot_nt(pool[2, :, half], weights.get(x, 512, 512))
            keep(0, x).wait()
        scatter.tick(first_step + 5)

        def input_rows(rows):
            grad = mid[rows, :]
            hat, inverse = normed_rows(total[rows, :])
            add_rows(0, grad * hat)
            add_rows(1, grad)
            scaled = grad * row(0)
            inner = (scaled - jnp.mean(scaled, axis=1, keepdims=True)
                     - hat * jnp.mean(scaled * hat, axis=1, keepdims=True))
            upstream[rows, :] = upstream[rows, :] + inverse * inner
        row_loop(input_rows)
        for kind in range(14):
            value = jnp.sum(gsum[kind], axis=0, keepdims=True)
            if kind == 3 or kind == 7:
                value = value / row(kind)
            small_sum[pl.ds(base + kind, 1), :] = value
        return carry

    lax.fori_loop(0, layers, one_layer, 0)
    small_total.start(0)
    for copy in out_copies:
        copy.wait()
    pool[0] = upstream[...].astype(jnp.bfloat16)
    rows_out[...] = dot_tn(to_place[...], pool[0]).astype(jnp.bfloat16).reshape(rows_out.shape)
    for copy in grad_copies:
        copy.start()
    for number in range(4):
        scatter.pass_on(chunks + number - 1)
        scatter.tick(chunks + number)
        small_total.add(number)
        if number < 3:
            small_total.start(number + 1)
    scatter.pass_on(chunks + 3)
    scatter.tick(chunks + 4)
    for copy in grad_copies:
        copy.wait()


def backward_all(whole, vec, grad_in, resids, middles, result, acts, hiddens, slopes, to_place, other):
    layers = whole.shape[0]
    full = grad_in.shape
    width = full[1]
    chunks = layers * PER_LAYER
    any_spec = pl.BlockSpec(memory_space=pl.ANY)
    vmem = pl.BlockSpec(memory_space=pltpu.VMEM)
    bf16, f32 = jnp.bfloat16, jnp.float32
    rows_shape = (2, HALF_PAD, width)
    return pl.pallas_call(
        functools.partial(bwd_kernel, layers),
        out_shape=(
            jax.ShapeDtypeStruct((layers, 3, SHARD, CHUNK // 2), bf16),
            jax.ShapeDtypeStruct((layers, CHUNK // 2, SHARD), bf16),
            jax.ShapeDtypeStruct((layers, SHARD, 2 * CHUNK), bf16),
            jax.ShapeDtypeStruct((layers, 2 * CHUNK, SHARD), bf16),
            jax.ShapeDtypeStruct(vec.shape, f32),
            jax.ShapeDtypeStruct(rows_shape, bf16),
            jax.ShapeDtypeStruct(rows_shape, bf16),
            jax.ShapeDtypeStruct(whole.shape, bf16),
        ),
        in_specs=[any_spec, vmem] + [any_spec] * 7 + [vmem, vmem],
        out_specs=(vmem,) * 5 + (any_spec,) * 3,
        scratch_shapes=[
            pltpu.VMEM((SLOTS, NX, NZ, NY, SHARD, CHUNK), bf16),
            pltpu.VMEM((NX, NZ, NY, SHARD, CHUNK), bf16),
        ] + landing_shapes() + [
            pltpu.VMEM(full, f32),
            pltpu.VMEM(full, bf16),
            pltpu.VMEM(full, bf16),
            pltpu.VMEM(full, f32),
            pltpu.VMEM(full, f32),
            pltpu.VMEM((4,) + full, bf16),
            pltpu.VMEM((4,) + full, bf16),
            pltpu.VMEM((NX, NZ, NY, NC, SHARD, CHUNK), bf16),
            pltpu.VMEM((NZ, NY, NC, SHARD, CHUNK), bf16),
            pltpu.VMEM(rows_shape, bf16),
            pltpu.VMEM((14, 8, width), f32),
            pltpu.VMEM((6,) + vec.shape, f32),
            pltpu.SemaphoreType.DMA((chunks, len(ROUTES) + 1, 6)),
            pltpu.SemaphoreType.DMA((chunks, len(ROUTES) + 1, 6)),
            pltpu.SemaphoreType.DMA((chunks,)),
            pltpu.SemaphoreType.REGULAR((7,)),
            pltpu.SemaphoreType.DMA((6,)),
            pltpu.SemaphoreType.DMA((6,)),
            pltpu.SemaphoreType.DMA((6,)),
            pltpu.SemaphoreType.DMA((2,)),
            pltpu.SemaphoreType.DMA((6,)),
            pltpu.SemaphoreType.DMA((1,)),
        ],
        compiler_params=pltpu.CompilerParams(
            collective_id=2, has_side_effects=True, vmem_limit_bytes=63 * 1024 * 1024),
        name="backward_all",
    )(whole, vec, grad_in, resids, middles, result, acts, hiddens, slopes, to_place, other)


def spread_small(vectors, qv_bias, up_bias):
    layers = vectors.shape[0]
    here = (jnp.arange(NZ * NY * NC) == lax.axis_index("dp"))
    side = (jnp.arange(NX) == lax.axis_index("mp"))
    vec = jnp.where(here[:, None] & side[0], vectors[:, :, None, :], 0).reshape(layers, 8, -1)
    qv = jnp.where(side[:, None, None, None] & here[:, None], qv_bias[:, :, None, :, None, :], 0).reshape(layers, 2, -1)
    up = jnp.where(side[:, None, None, None] & here[:, None], up_bias[:, None, :, None, :], 0).reshape(layers, 4, -1)
    rows = jnp.concatenate([vec, qv, up, jnp.zeros((layers, 2, vec.shape[2]), vec.dtype)], axis=1)
    return rows.reshape(layers * 16, -1)


def placement(ids):
    same = ids[:, None] == ids[None, :]
    count = jnp.sum(same, axis=1)
    order = jnp.arange(ids.shape[0])
    before = order[None, :] < order[:, None]
    long = count > 100
    kind = (long[:, None] == long[None, :]) & before
    inside = jnp.sum(same & before, axis=1)
    earlier = jnp.sum(kind, axis=1) - inside
    return jnp.where(long, jnp.where(earlier > 0, 208, 0) + inside, 416 + earlier + inside)


def on_device_fast(
    tokens, segments, qkv_weight, out_weight, up_weight, down_weight, vectors, qv_bias, up_bias, cotangent
):
    layers = qkv_weight.shape[0]
    half = tokens.shape[1]
    width = tokens.shape[2]
    place_x = lax.axis_index("mp")
    shard = jnp.concatenate(
        [qkv_weight[:, 0], qkv_weight[:, 1], qkv_weight[:, 2], jnp.swapaxes(out_weight, 1, 2),
         up_weight, jnp.swapaxes(down_weight, 1, 2)], axis=2)
    extra = ((0, 0), (0, HALF_PAD - half), (0, 0))
    ids = lax.dynamic_index_in_dim(segments, place_x, 0, keepdims=False)
    position = placement(ids)
    spread = jnp.concatenate([
        jnp.pad(position[:half], (0, HALF_PAD - half), constant_values=-1),
        jnp.pad(position[half:], (0, HALF_PAD - half), constant_values=-1)])
    to_place = (jnp.arange(PADDED)[:, None] == spread[None, :]).astype(jnp.bfloat16)
    new_ids = jnp.max(jnp.where(jnp.arange(PADDED)[:, None] == position[None, :], ids[None, :], -1), axis=1)
    other = jnp.stack([
        jnp.pad((new_ids[a:a + n][:, None] != new_ids[a:a + n][None, :]).astype(jnp.float32), ((0, 224 - n), (0, 224 - n)))
        for a, n in WINDOWS])
    whole, vec_rows, grad_in, resids, middles, result, acts, hiddens, slopes = forward_all(
        shard, spread_small(vectors, qv_bias, up_bias), jnp.pad(tokens, extra), jnp.pad(cotangent, extra), to_place, other)
    qkv_sum, out_sum, up_sum, down_sum, small, out_rows, grad_rows, _ = backward_all(
        whole, vec_rows, grad_in, resids, middles, result, acts, hiddens, slopes, to_place, other)
    small = small.reshape(layers, 16, width)
    dp = lax.axis_index("dp")
    vec = lax.dynamic_index_in_dim(small[:, :8].reshape(layers, 8, -1, 64), dp, 2, keepdims=False)
    qv = small[:, 8:10].reshape(layers, 2, NX, -1, NZ * NY * NC, 4)
    qv = lax.dynamic_index_in_dim(lax.dynamic_index_in_dim(qv, dp, 4, keepdims=False), place_x, 2, keepdims=False)
    up = small[:, 10:14].reshape(layers, NX, -1, NZ * NY * NC, 4)
    up = lax.dynamic_index_in_dim(lax.dynamic_index_in_dim(up, dp, 3, keepdims=False), place_x, 1, keepdims=False)
    return (
        out_rows[:, :half],
        grad_rows[:, :half].astype(jnp.float32),
        qkv_sum.astype(jnp.float32),
        out_sum.astype(jnp.float32),
        up_sum.astype(jnp.float32),
        down_sum.astype(jnp.float32),
        vec,
        qv,
        up,
    )


def solution(mesh):
    placed = (
        P(None, ("dp", "mp"), None),
        P(None, "dp"),
        P(None, None, "dp", "mp"),
        P(None, "mp", "dp"),
        P(None, "dp", "mp"),
        P(None, "mp", "dp"),
        P(None, None, "dp"),
        P(None, None, "mp", "dp"),
        P(None, "mp", "dp"),
        P(None, ("dp", "mp"), None),
    )
    fast = dict(mesh.shape) == {"dp": NZ * NY * NC, "mp": NX}
    return jax.shard_map(
        on_device_fast if fast else on_device,
        mesh=mesh,
        in_specs=placed,
        out_specs=(
            P(None, ("dp", "mp"), None),
            P(None, ("dp", "mp"), None),
            P(None, None, "dp", "mp"),
            P(None, "mp", "dp"),
            P(None, "dp", "mp"),
            P(None, "mp", "dp"),
            P(None, None, "dp"),
            P(None, None, "mp", "dp"),
            P(None, "mp", "dp"),
        ),
        check_vma=False,
    )
```
